32 devices in a mesh: gx: 8 (over z, x), gy: 4 (over y, core).
Axes of the slice: x: 2, y: 2, z: 4, core: 2. Of those that a mesh axis runs over, the one named last changes fastest.
Arguments:
- potential_warmth: float32 [576, 30, 3000], P(('gx', 'gy')), may hold values from -6 to 6
- saltiness_anomaly: float32 [576, 30, 3000], P(('gx', 'gy')), may hold values from -6 to 6
- topmost_thermal_inflow: float32 [576, 3000], P(('gx', 'gy')), may hold values from -8 to 8
- diffusivity_factor: float32 [29], replicated, may hold values from 0.05 to 5
- place_tile_number: int32 [576], P(('gx', 'gy')), may hold values from -1 to 575, as said below
- place_stack_strata: int32 [576, 3000], P(('gx', 'gy')), may hold values from 0 to 30, as said below
- mesh_stack_strata: int32 [1200, 1440], P('gy', 'gx'), may hold values from 0 to 30, as said below
Outputs:
- temperature_new: float32 [576, 30, 3000], P(('gx', 'gy'))
- salinity_new: float32 [576, 30, 3000], P(('gx', 'gy'))
- surface_height: float32 [1200, 1440], P('gy', 'gx')
- misfit_vector: float32 [1200, 1440], P('gy', 'gx')
The draws below stay inside these ranges and needn't reach their ends.
Inputs may be any that keep to these rules, and one draw needn't show every extreme that they name: `place_tile_number`: block (by, bx) has id by * 24 + bx. Every block holding an ocean column (mesh_stack_strata > 0) sits in exactly one slot, no block twice, and unlisted blocks are all land. The device at gx, gy holds only blocks with by // 6 = gy, and at most 3 blocks with the same bx // 3; some device holds exactly 3 such blocks. `place_stack_strata`: entry i * 60 + j of a slot equals mesh_stack_strata at row by * 50 + i, column bx * 60 + j of the slot's block; empty slots hold zeros. `mesh_stack_strata`: zero on land.
All inputs are finite; a program needn't handle non-finite values.
Results may differ from the reference program's by a relative error of at most 0.0003.
Values sent between devices are 32-bit elements; how exact they have to be, the bound alone decides.
No kernel may reach another device: no remote copies, remote signals or barrier semaphores. Data moves between devices by JAX's collectives and lax.ppermute only.
A program may use at most 256 MiB of HBM per device.

```python
import math
import jax
import jax.numpy as jnp

TILE_SPAN_EASTWARD = 60
TILE_SPAN_NORTH = 50
KX = 3
KY = 6
SEA_DEPTH_STRATA = 30
ITERS = 3
SLOTS = 18
CAP = 3
PLACES_OVERALL = 576
NX = 1440
NY = 1200
N_GX = 8
N_GY = 4


def ocean_layout(key):
    blocks_x = NX // TILE_SPAN_EASTWARD
    blocks_y = NY // TILE_SPAN_NORTH
    key_land, key_cols, key_coast, key_order = jax.random.split(key, 4)
    land_blocks = jax.random.randint(key_land, (blocks_y, blocks_x), 0, 4) == 0
    forced_ocean = (jnp.arange(blocks_x) < CAP)[None, :] & (jnp.arange(blocks_y) == 0)[:, None]
    land_blocks = land_blocks & jnp.logical_not(forced_ocean)
    column_depth = jax.random.randint(key_cols, (NY, NX), 1, SEA_DEPTH_STRATA + 1)
    coastal = jax.random.randint(key_coast, (NY, NX), 0, 8) == 0
    column_depth = jnp.where(coastal, 0, column_depth)
    column_depth = column_depth.at[0, 0].set(SEA_DEPTH_STRATA)
    land_cells = jnp.repeat(jnp.repeat(land_blocks, TILE_SPAN_NORTH, axis=0), TILE_SPAN_EASTWARD, axis=1)
    grid_depth = jnp.where(land_cells, 0, column_depth).astype(jnp.int32)
    scores = jax.random.randint(key_order, (N_GY, N_GX), 0, 2 ** 20) * N_GX + jnp.arange(N_GX)[None, :]
    shuffled = jnp.argsort(scores, axis=1).astype(jnp.int32)
    slot_index = jnp.arange(SLOTS)
    shifts = shuffled[:, slot_index // CAP]
    device_x = jnp.arange(N_GX)
    owners = (device_x[:, None, None] - shifts[None, :, :]) % N_GX
    bands = jnp.arange(N_GY)[None, :, None]
    block_col = owners * KX + slot_index % KX
    block_row = bands * KY + slot_index // KX
    is_land = land_blocks[block_row, block_col]
    identity = jnp.where(is_land, -1, block_row * blocks_x + block_col).astype(jnp.int32)
    cell_index = jnp.arange(TILE_SPAN_EASTWARD * TILE_SPAN_NORTH)
    grid_rows = block_row[..., None] * TILE_SPAN_NORTH + cell_index // TILE_SPAN_EASTWARD
    grid_cols = block_col[..., None] * TILE_SPAN_EASTWARD + cell_index % TILE_SPAN_EASTWARD
    slot_depth = jnp.where(is_land[..., None], 0, grid_depth[grid_rows, grid_cols]).astype(jnp.int32)
    return (grid_depth, identity.reshape(-1), slot_depth.reshape(-1, TILE_SPAN_EASTWARD * TILE_SPAN_NORTH))


def draw_place_tile_number(key, part):
    shared = ocean_layout(key)
    return shared[1]


def draw_place_stack_strata(key, part):
    shared = ocean_layout(key)
    return shared[2]


def draw_mesh_stack_strata(key, part):
    shared = ocean_layout(key)
    return shared[0]


def levels(rng, dims, pieces, smallest, high):
    loudness, own = 1.0, jax.random.fold_in(rng, 6)
    for position, blocks in pieces:
        steps = jnp.exp(jax.random.uniform(jax.random.fold_in(own, position), (blocks,), jnp.float32, smallest / len(pieces), high / len(pieces)))
        loudness = loudness * jnp.repeat(steps, dims[position] // blocks).reshape([-1 if axis == position else 1 for axis in range(len(dims))])
    return loudness


def gaussian(own_key, extent, spread, reach, shards=(), dtype=jnp.bfloat16):
    drawn = spread * jax.random.normal(own_key, extent, jnp.float32)
    if shards:
        drawn = drawn * levels(own_key, extent, shards, -0.22, 0.18)
    return jnp.clip(drawn, -reach, reach).astype(dtype)


def setup_inputs(seed: int = 0) -> dict:
    key_of = jax.random.split(jax.random.key(seed), 8)
    return {
        "potential_warmth": gaussian(key_of[0], (PLACES_OVERALL, SEA_DEPTH_STRATA, TILE_SPAN_EASTWARD * TILE_SPAN_NORTH), 1.0, 6.0, ((0, 32),), jnp.float32),
        "saltiness_anomaly": gaussian(key_of[1], (PLACES_OVERALL, SEA_DEPTH_STRATA, TILE_SPAN_EASTWARD * TILE_SPAN_NORTH), 1.0, 6.0, ((0, 32),), jnp.float32),
        "topmost_thermal_inflow": gaussian(key_of[2], (PLACES_OVERALL, TILE_SPAN_EASTWARD * TILE_SPAN_NORTH), 1.5, 8.0, ((0, 32),), jnp.float32),
        "diffusivity_factor": jnp.clip(jnp.exp(jax.random.uniform(key_of[3], (SEA_DEPTH_STRATA - 1,), jnp.float32, math.log(0.05), math.log(5.0))), 0.05, 5.0),
        "place_tile_number": draw_place_tile_number(jax.random.fold_in(key_of[7], 71), 0),
        "place_stack_strata": draw_place_stack_strata(jax.random.fold_in(key_of[7], 71), 0),
        "mesh_stack_strata": draw_mesh_stack_strata(jax.random.fold_in(key_of[7], 71), 0),
    }


HALINE_CONTRACT = 0.8
THERMAL_EXPANSE = 0.6
DAMPING = 0.05


def thomas_vertical_inverse(potential_warmth, saltiness_anomaly, topmost_thermal_inflow, diffusivity_factor, marine_strata_number):
    wet_strata_number = potential_warmth.shape[1]
    coupling = [jnp.where(stratum_position + 1 < marine_strata_number, diffusivity_factor[stratum_position], 0.0).astype(jnp.float32) for stratum_position in range(wet_strata_number - 1)]
    forced = jnp.where(marine_strata_number > 0, topmost_thermal_inflow, 0.0)
    gains = []
    heat_rows = []
    salt_rows = []
    for stratum_position in range(wet_strata_number):
        pivots = jnp.ones(topmost_thermal_inflow.shape, jnp.float32)
        thermal_forcing_part = potential_warmth[:, stratum_position, :]
        salt_term = saltiness_anomaly[:, stratum_position, :]
        if stratum_position == 0:
            thermal_forcing_part = thermal_forcing_part + forced
        if stratum_position + 1 < wet_strata_number:
            pivots = pivots + coupling[stratum_position]
        if stratum_position > 0:
            pivots = pivots + coupling[stratum_position - 1] - coupling[stratum_position - 1] * gains[stratum_position - 1]
            thermal_forcing_part = thermal_forcing_part + coupling[stratum_position - 1] * heat_rows[stratum_position - 1]
            salt_term = salt_term + coupling[stratum_position - 1] * salt_rows[stratum_position - 1]
        if stratum_position + 1 < wet_strata_number:
            gains.append(coupling[stratum_position] / pivots)
        else:
            gains.append(jnp.zeros_like(pivots))
        heat_rows.append(thermal_forcing_part / pivots)
        salt_rows.append(salt_term / pivots)
    heat_out = [heat_rows[wet_strata_number - 1]]
    salt_out = [salt_rows[wet_strata_number - 1]]
    for stratum_position in range(wet_strata_number - 2, -1, -1):
        heat_out.append(heat_rows[stratum_position] + gains[stratum_position] * heat_out[-1])
        salt_out.append(salt_rows[stratum_position] + gains[stratum_position] * salt_out[-1])
    return jnp.stack(heat_out[::-1], axis=1), jnp.stack(salt_out[::-1], axis=1)


def weight_balanced(revised_warmth, revised_saltiness, marine_strata_number):
    running = jnp.zeros(marine_strata_number.shape, jnp.float32)
    layers_out = []
    for stratum_position in range(revised_warmth.shape[1]):
        mass_per_volume = jnp.where(stratum_position < marine_strata_number, HALINE_CONTRACT * revised_saltiness[:, stratum_position, :] - THERMAL_EXPANSE * revised_warmth[:, stratum_position, :], 0.0)
        running = running + mass_per_volume
        layers_out.append(running)
    return jnp.stack(layers_out, axis=1)


def neighbours(field):
    east_side = jnp.roll(field, -1, axis=-1)
    west_side = jnp.roll(field, 1, axis=-1)
    folded = jnp.flip(field[..., -1:, :], axis=-1)
    north_side = jnp.concatenate([field[..., 1:, :], folded], axis=-2)
    south_side = jnp.concatenate([jnp.zeros_like(field[..., :1, :]), field[..., :-1, :]], axis=-2)
    return (east_side, west_side, north_side, south_side)


def reference(potential_warmth, saltiness_anomaly, topmost_thermal_inflow, diffusivity_factor, place_tile_number, place_stack_strata, mesh_stack_strata):
    revised_warmth, revised_saltiness = thomas_vertical_inverse(potential_warmth, saltiness_anomaly, topmost_thermal_inflow, diffusivity_factor, place_stack_strata)
    normal_stress = weight_balanced(revised_warmth, revised_saltiness, place_stack_strata)
    blocks_x = NX // TILE_SPAN_EASTWARD
    blocks_y = NY // TILE_SPAN_NORTH
    block_total = blocks_x * blocks_y
    targets = jnp.where(place_tile_number >= 0, place_tile_number, block_total).astype(jnp.int32)
    placed = jnp.zeros((block_total + 1, SEA_DEPTH_STRATA, TILE_SPAN_EASTWARD * TILE_SPAN_NORTH), jnp.float32).at[targets].set(normal_stress)[:block_total]
    pressure_grid = placed.reshape(blocks_y, blocks_x, SEA_DEPTH_STRATA, TILE_SPAN_NORTH, TILE_SPAN_EASTWARD).transpose(2, 0, 3, 1, 4).reshape(SEA_DEPTH_STRATA, NY, NX)
    depth = mesh_stack_strata.astype(jnp.float32)
    faces = [jnp.minimum(depth, other_depth) for other_depth in neighbours(depth)]
    rhs = jnp.zeros((NY, NX), jnp.float32)
    for stratum_position in range(SEA_DEPTH_STRATA):
        layer_field = pressure_grid[stratum_position]
        for neighbour, face_levels in zip(neighbours(layer_field), faces):
            rhs = rhs + jnp.where(stratum_position < face_levels, neighbour - layer_field, 0.0)
    rhs = rhs / SEA_DEPTH_STRATA
    weights = [face_levels / SEA_DEPTH_STRATA for face_levels in faces]
    damping = jnp.where(depth > 0, DAMPING, 1.0)
    diagonal = damping + weights[0] + weights[1] + weights[2] + weights[3]

    def operate(field):
        result = damping * field
        for neighbour, weight in zip(neighbours(field), weights):
            result = result + weight * (field - neighbour)
        return result

    elevation = jnp.zeros((NY, NX), jnp.float32)
    misfit_vector = rhs
    precond = misfit_vector / diagonal
    direction = precond
    precond_dot = jnp.sum(misfit_vector * precond)
    for iteration in range(ITERS):
        image_field = operate(direction)
        step_size = precond_dot / jnp.sum(direction * image_field)
        elevation = elevation + step_size * direction
        misfit_vector = misfit_vector - step_size * image_field
        precond = misfit_vector / diagonal
        next_dot = jnp.sum(misfit_vector * precond)
        direction = precond + (next_dot / precond_dot) * direction
        precond_dot = next_dot
    return revised_warmth, revised_saltiness, elevation, misfit_vector
```

```python
import functools
import numpy as np
import jax
import jax.numpy as jnp
from jax import lax
from jax.experimental import pallas as pl
from jax.experimental.pallas import tpu as pltpu
from jax.sharding import PartitionSpec as P

SPAN_E = 60
SPAN_N = 50
KX = 3
KY = 6
LEVELS = 30
HALINE = 0.8
THERMAL = 0.6
RATIO = THERMAL / HALINE
DAMPING = 0.05
COLS = SPAN_E * SPAN_N
TILES = 24
SLOT_ROWS = 24
STEP = 25
PITCH = 33
EDGE = 384
FLAT = TILES * 128
RY = KY * SPAN_N
RX = KX * SPAN_E
GY = 312
GX = 256
F32 = jnp.float32
MIB = 2**20


def widths():
    return [(c, min(128, COLS - 128 * c)) for c in range(TILES)]


def vm():
    return pl.BlockSpec(memory_space=pltpu.VMEM)


def sm():
    return pl.BlockSpec(memory_space=pltpu.SMEM)


def hbm():
    return pl.BlockSpec(memory_space=pltpu.HBM)


def divide(x, d):
    return (x * (2**20 // d + 1)) >> 20


def coefficient(coef, kind, k):
    return coef[8 * (kind * LEVELS + k) : 8 * (kind * LEVELS + k) + 8, :]


def fill_coefficients(mixing, coef):
    ones = jnp.ones((8, 128), F32)
    base = ones
    for k in range(LEVELS):
        last = 8 * (2 * LEVELS + k)
        coef[last : last + 8, :] = ones / base
        if k + 1 < LEVELS:
            here = jnp.full((8, 128), mixing[k], F32)
            q = ones / (base + here)
            g = here * q
            coef[8 * k : 8 * k + 8, :] = g
            coef[8 * (LEVELS + k) : 8 * (LEVELS + k) + 8, :] = q
            base = ones + here - here * g


def spread_slots(rows, slots_by_column):
    for c, w in widths():
        rows[c * STEP : c * STEP + slots_by_column.shape[0], 0:w] = slots_by_column[:, c * 128 : c * 128 + w]


def pieces_of(rows, start, step):
    return [rows[pl.ds(u * 8 * step + start, 8, stride=step), :] for u in range(TILES // 8)]


MID = 25


ROW_SIZE = TILES * PITCH + 8
MID_SIZE = 32 * MID + 8


def copy_in(rows, base, values):
    for c, w in widths():
        rows[base + c * PITCH : base + c * PITCH + LEVELS, 0:w] = values(c, w)


def level_at(j, k, u):
    start = j * MID_SIZE + k * MID + u * 8
    return slice(start, start + 8)


def columns_at(j, k, u):
    return pl.ds(j * ROW_SIZE + u * 8 * PITCH + k, 8, stride=PITCH)


def solve_body(first, group, extra, warm, salt, n_rows, q_rows, coef, *rest):
    warm_out, salt_out, _, warm_rows, salt_rows, warm_mid, salt_mid = rest[extra:]
    step = pl.program_id(0)
    many = range(group)
    each = [(j, u) for j in many for u in range(TILES // 8)]
    n, t, s = {}, {}, {}
    for j in many:
        copy_in(warm_rows, j * ROW_SIZE, lambda c, w: warm[j, :, c * 128 : c * 128 + w])
        copy_in(salt_rows, j * ROW_SIZE, lambda c, w: salt[j, :, c * 128 : c * 128 + w])
        slot = first + step * group + j
        for u, deep in enumerate(pieces_of(n_rows, slot, STEP)):
            n[j, u] = deep
        for u, heat in enumerate(pieces_of(q_rows, slot, STEP)):
            t[j, u] = jnp.where(n[j, u] > 0, heat, 0.0)
    for k in range(LEVELS):
        g = coefficient(coef, 0, k - 1) if k else None
        for j, u in each:
            rt = warm_rows[columns_at(j, k, u), :]
            rs = salt_rows[columns_at(j, k, u), :]
            if k == 0:
                t[j, u] = rt + t[j, u]
                s[j, u] = rs
            else:
                e = jnp.where(n[j, u] > k, g, 0.0)
                t[j, u] = rt + e * t[j, u]
                s[j, u] = rs + e * s[j, u]
            warm_mid[level_at(j, k, u), :] = t[j, u]
            salt_mid[level_at(j, k, u), :] = s[j, u]
    for k in range(LEVELS - 1, -1, -1):
        last = coefficient(coef, 2, k)
        q = coefficient(coef, 1, k) if k + 1 < LEVELS else None
        g = coefficient(coef, 0, k) if k + 1 < LEVELS else None
        for j, u in each:
            a = jnp.where(n[j, u] > k, last, 1.0)
            if k + 1 < LEVELS:
                more = n[j, u] > k + 1
                a = jnp.where(more, q, a)
                e = jnp.where(more, g, 0.0)
                t[j, u] = a * warm_mid[level_at(j, k, u), :] + e * t[j, u]
                s[j, u] = a * salt_mid[level_at(j, k, u), :] + e * s[j, u]
            else:
                t[j, u] = a * t[j, u]
                s[j, u] = a * s[j, u]
            warm_mid[level_at(j, k, u), :] = t[j, u]
            salt_mid[level_at(j, k, u), :] = s[j, u]
    for j in many:
        for c, w in widths():
            for k in range(0, LEVELS, 8):
                h = min(8, LEVELS - k)
                part = pl.ds(j * MID_SIZE + k * MID + c, h, stride=MID)
                warm_out[j, k : k + h, c * 128 : c * 128 + w] = warm_mid[part, :][:, 0:w]
                salt_out[j, k : k + h, c * 128 : c * 128 + w] = salt_mid[part, :][:, 0:w]


def mark_shape():
    return jax.ShapeDtypeStruct((8, 128), F32)


def coefficient_shape():
    return (3 * LEVELS * 8, 128)


def solve_columns(warm, salt, columns, first, count, before, after):
    group = 3 if first % 3 == 0 and count % 3 == 0 else 1
    block = pl.BlockSpec((group, LEVELS, COLS), lambda i: (first // group + i, 0, 0))
    extra = len(before) + len(after)
    return pl.pallas_call(
        functools.partial(solve_body, first, group, extra),
        grid=(count // group,),
        out_shape=(jax.ShapeDtypeStruct(warm.shape, F32), jax.ShapeDtypeStruct(salt.shape, F32), mark_shape()),
        in_specs=[block, block] + [vm()] * 3 + [hbm()] * extra,
        out_specs=(block, block, hbm()),
        scratch_shapes=[
            pltpu.VMEM((group * ROW_SIZE, 128), F32),
            pltpu.VMEM((group * ROW_SIZE, 128), F32),
            pltpu.VMEM((group * MID_SIZE, 128), F32),
            pltpu.VMEM((group * MID_SIZE, 128), F32),
        ],
        input_output_aliases={5: 0, 6: 1} if before else {},
        compiler_params=pltpu.CompilerParams(vmem_limit_bytes=49 * MIB),
        cost_estimate=pl.CostEstimate(flops=count * 2_000_000, bytes_accessed=count * 1_600_000, transcendentals=0),
        name="column_solve",
    )(warm, salt, *columns, *before, *after)


def rim_sources():
    lane = lax.broadcasted_iota(jnp.int32, (8, 128), 1)
    one = jnp.where(lane < 64, lane, lane - 64)
    along_x = jnp.where(one < SPAN_N, one * SPAN_E + jnp.where(lane < 64, 0, SPAN_E - 1), -1)
    along_y = jnp.where(one < SPAN_E, one + jnp.where(lane < 64, 0, COLS - SPAN_E), -1)
    return along_x, along_y


def lanes_of(x, index):
    return jnp.take_along_axis(x, index, axis=1, mode="promise_in_bounds")


def rim_of(tile):
    sources = rim_sources()
    used = (range(TILES), (0, TILES - 2, TILES - 1))
    out = [None, None]
    for c in range(TILES):
        now = tile(c)
        for d in range(2):
            if c in used[d]:
                before = out[d] or [jnp.zeros((8, 128), F32)] * len(now)
                here = (sources[d] >> 7) == c
                out[d] = [jnp.where(here, lanes_of(v, sources[d] & 127), p) for v, p in zip(now, before)]
    return out


def tables_body(span_x, span_y, mixing, ids, depth, inflow, after, *rest):
    n_rows, q_rows, coef, pick, rim_x, rim_y, listed, padded = rest
    slots = depth.shape[0]
    n_rows[...] = jnp.zeros(n_rows.shape, jnp.int32)
    spread_slots(n_rows, depth)
    spread_slots(q_rows, inflow)
    fill_coefficients(mixing, coef)
    padded[...] = jnp.zeros((SLOT_ROWS, FLAT), F32)
    padded[0:slots, 0:COLS] = depth[...].astype(F32)
    rims = rim_of(lambda c: [padded[8 * g : 8 * g + 8, c * 128 : c * 128 + 128] for g in range(SLOT_ROWS // 8)])
    for ref, parts in zip((rim_x, rim_y), rims):
        ref[...] = jnp.concatenate(parts, axis=0)
    blocks_x = KX * span_x
    row = lax.broadcasted_iota(jnp.int32, (SLOT_ROWS, 128), 0)
    held = jnp.zeros((SLOT_ROWS, 128), jnp.int32)
    for s in range(slots):
        held = jnp.where(row == s, jnp.maximum(ids[s], 0), held)
    lane = lax.broadcasted_iota(jnp.int32, (8, 128), 1)
    line = jnp.full((8, 128), -1.0, F32)
    for s in range(slots):
        line = jnp.where(lane == s, ids[s].astype(F32), line)
    listed[...] = line
    up = divide(held, blocks_x)
    across = held - blocks_x * up
    band = up - KY * divide(up, KY)

    def spot(b, m, folds=False):
        o = divide(b, KX)
        c = b - KX * o
        return jnp.where(folds, span_x - 1 - o, o) * 32 + c * 8 + m

    spots = (
        spot(jnp.where(across == 0, blocks_x, across) - 1, band + 1),
        spot(jnp.where(across == blocks_x - 1, -1, across) + 1, band + 1),
        spot(across, band),
        spot(across, band + 2, up == KY * span_y - 1),
    )
    at = lax.broadcasted_iota(jnp.int32, (SLOT_ROWS, 128), 1)
    for d, where in enumerate(spots):
        for t in range(span_x * 32 // 128):
            pick[d * SLOT_ROWS : (d + 1) * SLOT_ROWS, t * 128 : t * 128 + 128] = jnp.where(
                at + t * 128 == where, 1.0, 0.0
            )


def column_tables(span_x, span_y, mixing, ids, depth, inflow, after):
    rows = (TILES * STEP + 8, 128)
    return pl.pallas_call(
        functools.partial(tables_body, span_x, span_y),
        out_shape=(
            jax.ShapeDtypeStruct(rows, jnp.int32),
            jax.ShapeDtypeStruct(rows, F32),
            jax.ShapeDtypeStruct(coefficient_shape(), F32),
        )
        + (jax.ShapeDtypeStruct((4 * SLOT_ROWS, span_x * 32), F32),)
        + (jax.ShapeDtypeStruct((SLOT_ROWS, 128), F32),) * 2
        + (jax.ShapeDtypeStruct((8, 128), F32),),
        in_specs=[sm(), sm(), vm(), vm(), hbm()],
        out_specs=(vm(),) * 7,
        scratch_shapes=[pltpu.VMEM((SLOT_ROWS, FLAT), F32)],
        compiler_params=pltpu.CompilerParams(vmem_limit_bytes=12 * MIB),
        cost_estimate=pl.CostEstimate(flops=5_000_000, bytes_accessed=3_000_000, transcendentals=0),
        name="column_tables",
    )(mixing, ids, depth, inflow, after)


def spread_lines(span_y, top, bottom, out):
    here = lax.axis_index("gy")
    for p in range(span_y):
        out[p] = jnp.where(here == p - 1, top, jnp.where(here == p + 1, bottom, 0.0))


def beside_lines(span_y, lines, folded):
    here = lax.axis_index("gy")
    ups = jnp.where(here == span_y - 1, folded, lines[jnp.minimum(here + 1, span_y - 1)])
    downs = jnp.where(here == 0, 0.0, lines[jnp.maximum(here - 1, 0)])
    return ups, downs


def edges_body(span_x, span_y, depth, lines, held, table, extended, _, rows):
    ups, downs = beside_lines(span_y, lines, 0.0)
    top = lax.axis_index("gy") == span_y - 1
    extended[...] = depth[...]
    extended[RY : RY + 4, :] = ups[0:4]
    extended[GY - 4 : GY, :] = downs[0:4]
    lane = lax.broadcasted_iota(jnp.int32, (8, GX), 1)
    pick = lax.broadcasted_iota(jnp.int32, (8, GX), 0)
    ext16 = extended[...].astype(jnp.bfloat16)

    def columns(wanted):
        hot = jnp.where(lane == wanted, 1.0, 0.0).astype(jnp.bfloat16)
        out = lax.dot_general(hot, ext16, (((1,), (1,)), ((), ())), preferred_element_type=F32)
        return jnp.concatenate([out, jnp.zeros((8, EDGE - GY), F32)], axis=1)

    sides = columns(jnp.where(pick < 3, pick * SPAN_E, jnp.where(pick < 6, (pick - 3) * SPAN_E + SPAN_E - 1, -1)))
    rows[...] = jnp.zeros((16, GX), F32)
    for m in range(KY + 1):
        rows[m + 1 : m + 2, :] = extended[m * SPAN_N : m * SPAN_N + 1, :]
        y = m * SPAN_N - 1 if m else GY - 1
        rows[8 + m : 9 + m, :] = extended[y : y + 1, :]
    turned = turn(jnp.concatenate([extended[RY - 1 - y : RY - y, :] for y in range(4)] * 2, axis=0))
    rows[KY + 1 : KY + 2, :] = jnp.where(top, turned[0:1], rows[KY + 1 : KY + 2, :])
    low = rows[0:8, :]
    high = rows[8:16, :]
    lane1 = lane[:, 0:128]
    for b in range(KX):
        a = pltpu.roll(low, (192 - b * SPAN_E) % GX, 1)
        z = pltpu.roll(high, (128 - b * SPAN_E) % GX, 1)
        both = jnp.where(lane >= 192, a, z)
        table[0, 8 * b : 8 * b + 8, 128:256] = both[:, 128:256]
        table[0, 8 * b : 8 * b + 8, 0:128] = jnp.zeros((8, 128), F32)
        table[0, 8 * b : 8 * b + 8, 256:384] = jnp.zeros((8, 128), F32)
    for m in range(KY):
        z = pltpu.roll(sides, (EDGE - m * SPAN_N) % EDGE, 1)[:, 0:128]
        a = pltpu.roll(sides, (EDGE + 64 - m * SPAN_N) % EDGE, 1)[:, 0:128]
        for b in range(KX):
            table[0, 8 * b + m + 1 : 8 * b + m + 2, 0:128] = jnp.where(
                lane1[0:1] >= 64, a[b : b + 1], z[3 + b : 4 + b]
            )
    table[0, 0:1, 256:384] = held[0:1, :]
    table[0, 8:12, 256:384] = turned[0:4, 0:128]
    table[0, 12:16, 256:384] = turned[0:4, 128:256]
    table[0, 24:32, :] = columns(jnp.where(pick < 4, pick, RX - 8 + pick))
    for d in range(1, span_x):
        table[d] = table[0]


def block_edges(span_x, span_y, depth, lines, held):
    return pl.pallas_call(
        functools.partial(edges_body, span_x, span_y),
        out_shape=(
            jax.ShapeDtypeStruct((span_x, 32, EDGE), F32),
            jax.ShapeDtypeStruct((GY, GX), F32),
            mark_shape(),
        ),
        in_specs=[vm()] * 3,
        out_specs=(vm(),) * 2 + (hbm(),),
        scratch_shapes=[pltpu.VMEM((16, GX), F32)],
        compiler_params=pltpu.CompilerParams(vmem_limit_bytes=12 * MIB),
        name="block_edges",
    )(depth, lines, held)


def ends_body(span_y, depth, region, out, wide):
    wide[...] = jnp.zeros(wide.shape, F32)
    wide[0:RX, 0:RY] = depth[...].astype(F32)
    region[...] = wide[...].T[0:GY, :]

    def lines(first):
        return jnp.concatenate([region[first : first + 4, :], jnp.zeros((4, GX), F32)], axis=0)

    spread_lines(span_y, lines(RY - 4), lines(0), out)


def region_ends(span_y, depth_t):
    return pl.pallas_call(
        functools.partial(ends_body, span_y),
        out_shape=(
            jax.ShapeDtypeStruct((GY, GX), F32),
            jax.ShapeDtypeStruct((span_y, 8, GX), F32),
        ),
        in_specs=[vm()],
        out_specs=(vm(),) * 2,
        scratch_shapes=[pltpu.VMEM((GX, EDGE), F32)],
        compiler_params=pltpu.CompilerParams(vmem_limit_bytes=12 * MIB),
        name="region_ends",
    )(depth_t)


ROWS = 40
HALF = 13


SLOT_STEP = 201


def shifted(x, by):
    rows = x.shape[0]
    lane = lax.broadcasted_iota(jnp.int32, x.shape, 1)
    near = pltpu.roll(x, -by % 128, 1)
    far = pltpu.roll(near, (rows - 1) if by > 0 else 1, 0)
    return jnp.where(lane < 128 - by if by > 0 else lane >= -by, near, far)


def flux_body(
    slots, group, warm, salt, n_rows, q_rows, coef, after, pieces, rim_x, rim_y,
    faces, found, rows, middle, totals,
):
    step = pl.program_id(0)
    lane = lax.broadcasted_iota(jnp.int32, (1, FLAT), 1)
    col = lane - SPAN_E * divide(lane, SPAN_E)

    @pl.when(step == 0)
    def _():
        faces[...] = jnp.zeros(faces.shape, jnp.int32)

    many = range(group)
    each = [(j, u) for j in many for u in range(TILES // 8)]
    place = lax.broadcasted_iota(jnp.int32, (TILES, 128), 0) * 128
    place = place + lax.broadcasted_iota(jnp.int32, (TILES, 128), 1)
    in_row = place - SPAN_E * divide(place, SPAN_E)
    n, x = {}, {}
    for j in many:
        copy_in(
            rows,
            j * ROW_SIZE,
            lambda c, w: salt[j, :, c * 128 : c * 128 + w] - RATIO * warm[j, :, c * 128 : c * 128 + w],
        )
        slot = step * group + j
        for u, deep in enumerate(pieces_of(n_rows, slot, STEP)):
            n[j, u] = deep
        for u, heat in enumerate(pieces_of(q_rows, slot, STEP)):
            x[j, u] = RATIO * heat
        deep = jnp.concatenate([n[j, u] for u in range(TILES // 8)], axis=0)
        for d, (by, inside) in enumerate(
            (
                (1, in_row < SPAN_E - 1),
                (-1, in_row > 0),
                (SPAN_E, place < COLS - SPAN_E),
                (-SPAN_E, place >= SPAN_E),
            )
        ):
            start = (8 * j + d) * MID
            faces[start : start + TILES, :] = jnp.where(inside, jnp.minimum(deep, shifted(deep, by)), 0)
    for k in range(LEVELS):
        g = coefficient(coef, 0, k - 1) if k else None
        for j, u in each:
            right = rows[columns_at(j, k, u), :]
            x[j, u] = right + g * x[j, u] if k else right - x[j, u]
            middle[j, k, u * 8 : u * 8 + 8, :] = x[j, u]
    for k in range(LEVELS - 1, -1, -1):
        last = coefficient(coef, 2, k)
        q = coefficient(coef, 1, k) if k + 1 < LEVELS else None
        g = coefficient(coef, 0, k) if k + 1 < LEVELS else None
        for j, u in each:
            if k + 1 < LEVELS:
                more = n[j, u] > k + 1
                a = jnp.where(more, q, last)
                e = jnp.where(more, g, 0.0)
                x[j, u] = a * middle[j, k, u * 8 : u * 8 + 8, :] + e * x[j, u]
            else:
                x[j, u] = last * x[j, u]
            middle[j, k, u * 8 : u * 8 + 8, :] = x[j, u]
    zero = jnp.zeros((8, 128), F32)
    pressure = {at: zero for at in each}
    total = {at: zero for at in each}
    for k in range(LEVELS):
        for j, u in each:
            pressure[j, u] = pressure[j, u] + middle[j, k, u * 8 : u * 8 + 8, :]
            total[j, u] = total[j, u] + pressure[j, u]
            totals[level_at(j, k, u), :] = total[j, u]

    for j in many:
        slot = step * group + j

        def tile(c):
            now = [totals[pl.ds(j * MID_SIZE + 8 * g * MID + c, 8, stride=MID), :] for g in range(4)]
            level = faces[pl.ds(8 * j * MID + c, 8, stride=MID), :] - 1
            sums = zero
            for g in range(4):
                one_of = jnp.take_along_axis(now[g], level & 7, axis=0, mode="promise_in_bounds")
                sums = jnp.where((level >> 3) == g, one_of, sums)
            found[pl.ds(slot * SLOT_STEP + c * 8, 8), :] = sums
            return now

        for ref, parts in zip((rim_x, rim_y), rim_of(tile)):
            for g in range(4):
                ref[j, 8 * g : 8 * g + 8, :] = parts[g]

    @pl.when(step == slots // group - 1)
    def _():
        def flat(d):
            return jnp.concatenate(
                [found[pl.ds(c * 8 + d, SLOT_ROWS, stride=SLOT_STEP), :] for c in range(TILES)], axis=1
            )

        east, west, north, south = (flat(d) for d in range(4))
        from_east = pltpu.roll(west, FLAT - 1, 1)
        from_west = pltpu.roll(east, 1, 1)
        net = -(east + west + north + south)
        net = net + jnp.where(col < SPAN_E - 1, from_east, 0.0)
        net = net + jnp.where(col > 0, from_west, 0.0)
        net = net + jnp.where(lane < COLS - SPAN_E, pltpu.roll(south, FLAT - SPAN_E, 1), 0.0)
        net = net + jnp.where(lane >= SPAN_E, pltpu.roll(north, SPAN_E, 1), 0.0)
        l = lax.broadcasted_iota(jnp.int32, (1, 128), 1)
        for t in range(26):
            halves = []
            for h in range(2):
                r = 2 * t + h
                if r in (0, SPAN_N + 1):
                    continue
                start = (r - 1) * SPAN_E
                a = start // 128
                row = net[:, a * 128 : a * 128 + 128]
                if start % 128 + SPAN_E > 128:
                    row = jnp.where(l >= start % 128, row, net[:, a * 128 + 128 : a * 128 + 256])
                row = pltpu.roll(row, (64 * h + 1 - start) % 128, 1)
                halves.append(jnp.where((l > 64 * h) & (l <= 64 * h + SPAN_E), row, 0.0))
            pieces[t * STEP : t * STEP + SLOT_ROWS, :] = halves[0] + halves[1] if len(halves) == 2 else halves[0]


def face_sums(warm, salt, columns, after):
    slots = warm.shape[0]
    group = 3 if slots % 3 == 0 else 1
    block = pl.BlockSpec((group, LEVELS, COLS), lambda i: (i, 0, 0))
    rim = pl.BlockSpec((group, 32, 128), lambda i: (i, 0, 0))
    return pl.pallas_call(
        functools.partial(flux_body, slots, group),
        grid=(slots // group,),
        out_shape=(jax.ShapeDtypeStruct((26 * STEP + 6, 128), F32),)
        + (jax.ShapeDtypeStruct((slots, 32, 128), F32),) * 2,
        in_specs=[block, block] + [vm()] * 3 + [hbm()],
        out_specs=(vm(), rim, rim),
        scratch_shapes=[
            pltpu.VMEM((8 * group * MID, 128), jnp.int32),
            pltpu.VMEM((SLOT_ROWS * SLOT_STEP, 128), F32),
            pltpu.VMEM((group * ROW_SIZE, 128), F32),
            pltpu.VMEM((group, LEVELS, TILES, 128), F32),
            pltpu.VMEM((group * MID_SIZE, 128), F32),
        ],
        compiler_params=pltpu.CompilerParams(vmem_limit_bytes=49 * MIB),
        cost_estimate=pl.CostEstimate(flops=40_000_000, bytes_accessed=15_000_000, transcendentals=0),
        name="face_sums",
    )(warm, salt, *columns, after)


def received_rows(span_x, cap, edges):
    blocks_x = KX * span_x
    keys = jnp.concatenate([edges[d * 32 : d * 32 + 1, 256:384] for d in range(span_x)], axis=0).astype(jnp.int32)
    held = jnp.maximum(keys, 0)
    owner = jnp.where(keys >= 0, divide(held - blocks_x * divide(held, blocks_x), KX), -1)
    one_of = [jnp.where(owner == o, 1.0, 0.0) for o in range(span_x)]
    earlier = lax.broadcasted_iota(jnp.int32, (128, 128), 0) < lax.broadcasted_iota(jnp.int32, (128, 128), 1)
    counted = jnp.dot(
        jnp.concatenate(one_of, axis=0).astype(jnp.bfloat16),
        jnp.where(earlier, 1.0, 0.0).astype(jnp.bfloat16),
        preferred_element_type=F32,
    )
    at = lax.broadcasted_iota(jnp.int32, (span_x, 128), 0).astype(F32) * cap + 1.0
    for o in range(span_x):
        at = at + one_of[o] * counted[o * span_x : (o + 1) * span_x]
    here_x = lax.axis_index("gx")
    first = lax.axis_index("gy") * KY

    def beside(x):
        x = jnp.where(x < 0, x + blocks_x, x)
        return jnp.where(x >= blocks_x, x - blocks_x, x)

    base = here_x * KX
    over = (span_x - 1 - here_x) * KX
    wanted = [(first + p // KX) * blocks_x + base + p % KX for p in range(KX * KY)]
    wanted += [(first + p) * blocks_x + beside(base - 1) for p in range(KY)]
    wanted += [(first + p) * blocks_x + beside(base + KX) for p in range(KY)]
    wanted += [(first + KY - 1) * blocks_x + x for x in [over + g for g in range(KX)]]
    wanted += [(first + KY - 1) * blocks_x + beside(x) for x in (over - 1, over + KX)]
    lines = [jnp.sum(jnp.where(keys == w, at, 0.0), axis=0, keepdims=True) for w in wanted]
    lines += [jnp.zeros((1, 128), F32)] * (ROWS - len(lines))
    sums = jnp.sum(jnp.concatenate(lines, axis=0), axis=1, keepdims=True) - 1.0
    return jnp.broadcast_to(sums, (ROWS, 128)).astype(jnp.int32)


def outgoing_body(
    span_x, cap, slots, ids, pick, edges, n_x, n_y, inside, rim_x, rim_y, out, rows, _, pieces, q_x, q_y, source, counts
):
    blocks_x = KX * span_x
    for d in range(span_x):
        counts[d] = 0
    for d in range(span_x * cap):
        source[d] = 0
    for s in range(slots):
        held = jnp.maximum(ids[s], 0)
        owner = divide(held - blocks_x * divide(held, blocks_x), KX)
        rank = counts[owner]

        @pl.when(ids[s] >= 0)
        def _():
            source[owner * cap + jnp.minimum(rank, cap - 1)] = s
            counts[owner] = rank + 1

    rows[...] = received_rows(span_x, cap, edges)
    near = jnp.dot(
        pick[...].astype(jnp.bfloat16), edges[:, 0:GX].astype(jnp.bfloat16), preferred_element_type=F32
    )
    l = lax.broadcasted_iota(jnp.int32, (1, 128), 1)
    w, e, so, no = (near[d * SLOT_ROWS : (d + 1) * SLOT_ROWS] for d in range(4))
    q_x[...] = jnp.zeros(q_x.shape, F32)
    q_y[...] = jnp.zeros(q_y.shape, F32)
    level = lax.broadcasted_iota(jnp.int32, (32, 128), 0).astype(F32) + 1.0
    for n, other, rim, q in (
        (n_x, jnp.where(l < 64, w[:, 0:128], e[:, 0:128]), rim_x, q_x),
        (n_y, jnp.where(l < 64, so[:, 128:256], no[:, 128:256]), rim_y, q_y),
    ):
        face = jnp.minimum(n[...], other)
        for s in range(slots):
            hit = jnp.where(face[s : s + 1] == level, rim[s], 0.0)
            q[s : s + 1, :] = jnp.sum(hit, axis=0, keepdims=True)

    groups = range(SLOT_ROWS // 8)
    lane = lax.broadcasted_iota(jnp.int32, (8, 128), 1)
    in_row = lane & 63
    odd = lane >> 6
    adds = jnp.where((in_row == 0) | (in_row == SPAN_E + 1), 1.0, 0.0)
    adds = jnp.where((in_row == 1) | (in_row == SPAN_E), -1.0, adds)
    zero = jnp.zeros((8, 128), F32)
    strips = [[[zero for _ in groups] for _ in range(2)] for _ in range(2)]
    for t in range(26):
        p, at = t // HALF, 4 * (t % HALF)
        i = 2 * t - 1 + odd
        index = jnp.clip(i, 0, SPAN_N - 1) + jnp.where(in_row >= 32, 64, 0)
        sign = jnp.where((i >= 0) & (i < SPAN_N), adds, 0.0)
        band = (in_row >= at) & (in_row < at + 4)
        for g in groups:
            rows8 = slice(8 * g, 8 * g + 8)
            v = inside[t * STEP + 8 * g : t * STEP + 8 * g + 8, :] + sign * lanes_of(q_x[rows8, :], index)
            core = (in_row >= 1) & (in_row <= SPAN_E)
            if t == 0:
                v = v + jnp.where(core & (odd == 0), pltpu.roll(q_y[rows8, :], 1, 1), 0.0)
                v = v - jnp.where(core & (odd == 1), pltpu.roll(q_y[rows8, :], 65, 1), 0.0)
            if t == 25:
                v = v - jnp.where(core & (odd == 0), pltpu.roll(q_y[rows8, :], 65, 1), 0.0)
                v = v + jnp.where(core & (odd == 1), pltpu.roll(q_y[rows8, :], 1, 1), 0.0)
            pieces[t * STEP + 8 * g : t * STEP + 8 * g + 8, :] = v
            strips[0][p][g] = jnp.where(band, pltpu.roll(v, at, 1), strips[0][p][g])
            strips[1][p][g] = jnp.where(band, pltpu.roll(v, (at - SPAN_E + 2) % 128, 1), strips[1][p][g])
    for side in range(2):
        for p in range(2):
            for g in groups:
                start = (26 + 2 * side + p) * STEP + 8 * g
                pieces[start : start + 8, :] = strips[side][p][g]
    pieces[30 * STEP : 32 * STEP + 8, :] = jnp.zeros((2 * STEP + 8, 128), F32)

    tile_row = lax.broadcasted_iota(jnp.int32, (8, 128), 0)
    corner = (in_row >= 52) & (in_row < 60)
    for d in range(span_x):
        for c in range(cap):
            other = span_x - 1 - d
            own = source[d * cap + c]
            left = source[(d - 1) % span_x * cap + c]
            right = source[(d + 1) % span_x * cap + c]
            fold = source[other * cap + c]
            fold_west = source[(other - 1) % span_x * cap + c]
            fold_east = source[(other + 1) % span_x * cap + c]

            def last(slot):
                return pieces[pl.ds(24 * STEP + slot, 8, stride=STEP), :]

            tail = jnp.where(tile_row < 2, last(own), jnp.where(tile_row < 4, last(right), last(left)))
            tail = jnp.where(tile_row >= 6, pltpu.roll(last(fold), 6, 0), tail)
            tail = jnp.where((tile_row == 3) & corner, pltpu.roll(last(fold_east), 8, 1), tail)
            tail = jnp.where((tile_row == 5) & corner, pltpu.roll(last(fold_west), 8, 1), tail)
            out[d * cap + c, 0:24, :] = pieces[pl.ds(own, 24, stride=STEP), :]
            out[d * cap + c, 24:32, :] = tail


def outgoing_blocks(span_x, cap, ids, pick, edges, rims, sums):
    slots = ids.shape[0]
    return pl.pallas_call(
        functools.partial(outgoing_body, span_x, cap, slots),
        out_shape=(
            jax.ShapeDtypeStruct((span_x * cap, 32, 128), F32),
            jax.ShapeDtypeStruct((ROWS, 128), jnp.int32),
            mark_shape(),
        ),
        in_specs=[sm()] + [vm()] * 7,
        out_specs=(vm(), vm(), hbm()),
        scratch_shapes=[pltpu.VMEM((32 * STEP + 8, 128), F32)]
        + [pltpu.VMEM((SLOT_ROWS, 128), F32)] * 2
        + [pltpu.SMEM((span_x * cap,), jnp.int32), pltpu.SMEM((span_x,), jnp.int32)],
        compiler_params=pltpu.CompilerParams(vmem_limit_bytes=12 * MIB),
        name="outgoing_blocks",
    )(ids, pick, edges, *rims, *sums)


def turn(x):
    lane = lax.broadcasted_iota(jnp.int32, (8, 128), 1)
    halves = [
        jnp.take_along_axis(x[:, h * 128 : h * 128 + 128], 127 - lane, axis=1, mode="promise_in_bounds")
        for h in (1, 0)
    ]
    return pltpu.roll(jnp.concatenate(halves, axis=1), (RX - GX) % GX, 1)


def region_body(span_y, rows, got, after, region, out, folded, tiles, sides):
    tiles[...] = jnp.zeros(tiles.shape, F32)
    sides[...] = jnp.zeros(sides.shape, F32)
    for p in range(KX * KY):
        r = rows[p, 0]
        block = got[pl.ds(pl.multiple_of(jnp.maximum(r, 0) * 32, 32), 32), :]
        block = jnp.where(r >= 0, block, 0.0)
        tiles[pl.ds((p % KX) * 8 + p // KX, 32, stride=STEP), :] = block
    for p in range(2 * KY):
        r = rows[KX * KY + p, 0]
        block = got[pl.ds(pl.multiple_of(jnp.maximum(r, 0) * 32 + 24, 8), 8), :]
        block = jnp.where(r >= 0, block, 0.0)
        sides[pl.ds((p // KY) * 8 + p % KY, 8, stride=17), :] = block
    at_fold = KX * KY + 2 * KY
    for g in range(KX + 2):
        r = rows[at_fold + g, 0]
        block = got[pl.ds(pl.multiple_of(jnp.maximum(r, 0) * 32 + 24, 8), 8), :]
        block = jnp.where(r >= 0, block, 0.0)
        if g < KX:
            for t in range(2):
                tiles[(24 + t) * STEP + g * 8 + 6 : (24 + t) * STEP + g * 8 + 7, :] = block[6 + t : 7 + t]
        elif g == KX:
            sides[5 * 17 + 6 : 5 * 17 + 7, :] = pltpu.roll(block, 120, 1)[5:6]
        else:
            sides[3 * 17 + 14 : 3 * 17 + 15, :] = pltpu.roll(block, 120, 1)[3:4]
    lane = lax.broadcasted_iota(jnp.int32, (8, 128), 1)
    sub = lax.broadcasted_iota(jnp.int32, (8, 128), 0)

    def assembled(r):
        t, base = r // 2, (r % 2) * 64
        v = [tiles[t * STEP + 8 * g : t * STEP + 8 * g + 8, :] for g in range(KX)]
        a = pltpu.roll(v[0], (-1 - base) % 128, 1)
        b = pltpu.roll(v[1], (59 - base) % 128, 1)
        c = pltpu.roll(v[2], (119 - base) % 128, 1)
        to = base + 4 * (t % HALF)
        p = t // HALF
        w = sides[(4 + p) * 17 : (4 + p) * 17 + 8, :]
        e = sides[(2 + p) * 17 + 8 : (2 + p) * 17 + 16, :]
        w = pltpu.roll(w, (125 - to) % 128, 1)
        e = pltpu.roll(e, (51 - to) % 128, 1)
        left = jnp.where(lane <= 60, a, 0.0)
        left = left + jnp.where((lane >= 59) & (lane <= 120), b, 0.0)
        left = left + jnp.where(lane >= 119, c, 0.0)
        left = left + jnp.where(lane == 0, w, 0.0)
        right = jnp.where(lane <= 52, c, 0.0)
        right = right + jnp.where(lane == 127, a, 0.0)
        right = right + jnp.where(lane >= 125, w, 0.0)
        right = right + jnp.where((lane >= 51) & (lane <= 54), e, 0.0)
        return left, right

    region[...] = jnp.zeros(region.shape, F32)
    below = assembled(0)
    above = assembled(SPAN_N + 1)
    over = [above]
    for r in range(1, SPAN_N + 1):
        parts = assembled(r)
        if r > SPAN_N - 3:
            over.insert(1, parts)
        for h in range(2):
            v = parts[h]
            if r == 1:
                v = v + jnp.where((sub >= 1) & (sub < KY), pltpu.roll(above[h], 1, 0), 0.0)
            if r == SPAN_N:
                v = v + jnp.where(sub < KY - 1, pltpu.roll(below[h], 7, 0), 0.0)
            region[pl.ds(h * GY + r - 1, KY, stride=SPAN_N), :] = v[0:KY]
    for h in range(2):
        region[h * GY + RY : h * GY + RY + 1, :] = above[h][KY - 1 : KY]
        region[h * GY + GY - 1 : h * GY + GY, :] = below[h][0:1]

    def lines(ys):
        cut = [
            jnp.concatenate([region[y : y + 1, :], region[GY + y : GY + y + 1, :]], axis=1) for y in ys
        ]
        return jnp.concatenate(cut + [jnp.zeros((8 - len(ys), GX), F32)], axis=0)

    spread_lines(span_y, lines([RY - 3, RY - 2, RY - 1, RY]), lines([GY - 1, 0, 1, 2]), out)
    over = [jnp.concatenate([part[6:7] for part in parts], axis=1) for parts in over]
    folded[...] = turn(jnp.concatenate(over + [jnp.zeros((4, GX), F32)], axis=0))


def region_sums(span_y, rows, got, after):
    return pl.pallas_call(
        functools.partial(region_body, span_y),
        out_shape=(
            jax.ShapeDtypeStruct((2 * GY, 128), F32),
            jax.ShapeDtypeStruct((span_y, 8, GX), F32),
            jax.ShapeDtypeStruct((8, GX), F32),
        ),
        in_specs=[sm(), vm(), hbm()],
        out_specs=(vm(),) * 3,
        scratch_shapes=[pltpu.VMEM((32 * STEP + 8, 128), F32), pltpu.VMEM((8 * 17, 128), F32)],
        compiler_params=pltpu.CompilerParams(vmem_limit_bytes=12 * MIB),
        name="region_sums",
    )(rows, got.reshape(-1, 128), after)


def basis_body(span_x, span_y, region, lines, folded, extended, edges, basis, diag_out, dots, mark):
    ext = extended[...]
    here = lax.axis_index("gx")
    lane8 = lax.broadcasted_iota(jnp.int32, (8, GX), 1)
    row8 = lax.broadcasted_iota(jnp.int32, (8, GX), 0)
    put_west = jnp.where((row8 >= 4) & (lane8 == GX - 8 + row8), 1.0, 0.0).astype(jnp.bfloat16)
    put_east = jnp.where((row8 < 4) & (lane8 == RX + row8), 1.0, 0.0).astype(jnp.bfloat16)
    for other, put in ((here + span_x - 1, put_west), (here + 1, put_east)):
        cols = edges[pl.ds(pl.multiple_of(other % span_x * 32 + 24, 8), 8), :]
        ext = ext + lax.dot_general(
            cols[:, 0:GY].astype(jnp.bfloat16), put, (((0,), (0,)), ((), ())), preferred_element_type=F32
        )

    fold = []
    for step in (0, -1, 1):
        other = span_x - 1 - here + step + span_x
        part = edges[pl.ds(pl.multiple_of(lax.rem(other, span_x) * 32 + 8, 8), 8), 256:384]
        fold.append(jnp.concatenate([part[0:4], part[4:8]], axis=1))
    lane4 = lax.broadcasted_iota(jnp.int32, (4, GX), 1)
    beyond = jnp.where(lane4 < RX, fold[0], 0.0)
    beyond = jnp.where((lane4 >= RX) & (lane4 < RX + 4), pltpu.roll(fold[1], RX, 1), beyond)
    beyond = jnp.where(lane4 >= GX - 4, pltpu.roll(fold[2], GX - RX, 1), beyond)
    beyond = jnp.where(lax.axis_index("gy") == span_y - 1, beyond, 0.0)
    ext = ext + jnp.concatenate([jnp.zeros((RY, GX), F32), beyond, jnp.zeros((GY - RY - 4, GX), F32)], axis=0)

    def south_of(x):
        return pltpu.roll(x, 1, 0)

    def north_of(x):
        return pltpu.roll(x, GY - 1, 0)

    def west_of(x):
        return pltpu.roll(x, 1, 1)

    def east_of(x):
        return pltpu.roll(x, GX - 1, 1)

    to_east = jnp.minimum(ext, east_of(ext)) / LEVELS
    to_north = jnp.minimum(ext, north_of(ext)) / LEVELS
    to_west = west_of(to_east)
    to_south = south_of(to_north)
    diagonal = jnp.where(ext > 0, DAMPING, 1.0) + to_east + to_west + to_north + to_south
    inverse = 1.0 / diagonal
    ups, downs = beside_lines(span_y, lines, folded[...])
    partial = jnp.concatenate([region[0:GY, :], region[GY : 2 * GY, :]], axis=1)
    gap = lambda rows: jnp.zeros((rows, GX), F32)
    extra = jnp.concatenate(
        [downs[3:4], gap(RY - 2), ups[0:4], gap(GY - RY - 6), downs[0:3]], axis=0
    )
    zero = (partial + extra) * (HALINE / LEVELS) * inverse

    def smooth(x):
        return inverse * (
            to_east * east_of(x) + to_west * west_of(x) + to_north * north_of(x) + to_south * south_of(x)
        )

    vectors = [zero, smooth(zero)]
    vectors.append(2.0 * smooth(vectors[1]) - vectors[0])
    vectors.append(2.0 * smooth(vectors[2]) - vectors[1])
    lane = lax.broadcasted_iota(jnp.int32, (GY, GX), 1)
    row = lax.broadcasted_iota(jnp.int32, (GY, GX), 0)
    inside = (lane < RX) & (row < RY)
    diag_out[...] = diagonal
    clean = [jnp.where(inside, v, 0.0) for v in vectors]
    position = lax.broadcasted_iota(jnp.int32, (8, 128), 1)
    packed = jnp.zeros((8, 128), F32)
    number = 0
    for i in range(4):
        basis[i] = clean[i]
        scaled = clean[i] * diagonal
        for j in range(i, 4):
            prod = scaled * clean[j]
            part = jnp.sum(prod.reshape(GY // 8, 8, GX), axis=0)
            part = part[:, 0:128] + part[:, 128:256]
            packed = packed + jnp.where(position == number, jnp.sum(part, axis=1, keepdims=True), 0.0)
            number += 1
    for d in range(dots.shape[0]):
        dots[d] = packed


def krylov_basis(span_x, span_y, region, lines, folded, extended, edges):
    return pl.pallas_call(
        functools.partial(basis_body, span_x, span_y),
        out_shape=(
            jax.ShapeDtypeStruct((4, GY, GX), F32),
            jax.ShapeDtypeStruct((GY, GX), F32),
            jax.ShapeDtypeStruct((span_x * span_y, 8, 128), F32),
            mark_shape(),
        ),
        in_specs=[vm()] * 5,
        out_specs=(vm(),) * 3 + (hbm(),),
        compiler_params=pltpu.CompilerParams(vmem_limit_bytes=12 * MIB),
        name="krylov_basis",
    )(region, lines, folded, extended, edges)


def combine_body(dots, basis, diagonal, after, height, misfit):
    sums = jnp.sum(dots[...], axis=0, keepdims=True)
    lane = lax.broadcasted_iota(jnp.int32, (1, 128), 1)
    g = {}
    number = 0
    for i in range(4):
        for j in range(i, 4):
            v = jnp.sum(jnp.where(lane == number, sums, 0.0), axis=1, keepdims=True)
            g[i, j] = g[j, i] = v
            number += 1

    def inner(a, b):
        out = jnp.zeros((1, 1), F32)
        for i in range(4):
            for j in range(4):
                if a[i] is not None and b[j] is not None:
                    out = out + a[i] * b[j] * g[i, j]
        return out

    def add(a, b):
        return a if b is None else b if a is None else a + b

    def image(a):
        out = list(a)
        for k in range(3):
            if a[k] is None:
                continue
            if k == 0:
                out[1] = add(out[1], -a[0])
            else:
                out[k + 1] = add(out[k + 1], -0.5 * a[k])
                out[k - 1] = add(out[k - 1], -0.5 * a[k])
        return out

    one = jnp.ones((1, 1), F32)
    res = [one, None, None, None]
    way = list(res)
    high = [None] * 4
    gamma = inner(res, res)
    for iteration in range(3):
        moved = image(way)
        size = gamma / inner(way, moved)
        high = [h if w is None else add(h, size * w) for h, w in zip(high, way)]
        res = [r if m is None else add(r, -size * m) for r, m in zip(res, moved)]
        if iteration < 2:
            after = inner(res, res)
            ratio = after / gamma
            way = [r if w is None else add(r, ratio * w) for r, w in zip(res, way)]
            gamma = after
    out = jnp.zeros((GY, GX), F32)
    left = jnp.zeros((GY, GX), F32)
    for k in range(4):
        v = basis[k]
        if high[k] is not None:
            out = out + high[k] * v
        left = left + res[k] * v
    gap = jnp.zeros((384 - GY, GX), F32)
    height[...] = jnp.concatenate([out, gap], axis=0).T[0:RX, 0:RY]
    misfit[...] = jnp.concatenate([left * diagonal[...], gap], axis=0).T[0:RX, 0:RY]


def combine(dots, basis, diagonal, after):
    return pl.pallas_call(
        combine_body,
        out_shape=(jax.ShapeDtypeStruct((RX, RY), F32),) * 2,
        in_specs=[vm()] * 3 + [hbm()],
        out_specs=(vm(),) * 2,
        compiler_params=pltpu.CompilerParams(vmem_limit_bytes=12 * MIB),
        name="combine",
    )(dots, basis, diagonal, after)


def across(lines):
    return lax.all_to_all(lines, "gy", split_axis=0, concat_axis=0, tiled=True)


def on_device(warm, salt, inflow, mixing, tiles, slot_depth, depth):
    span_x = lax.axis_size("gx")
    span_y = lax.axis_size("gy")
    slots = tiles.shape[0]
    cap = (KX * KY + span_x - 1) // span_x
    both = ("gx", "gy")
    bounds = [slots * i // 18 for i in (0, 12, 18)]

    def solve(part, before, after):
        first, end = bounds[part], bounds[part + 1]
        return solve_columns(warm, salt, columns, first, end - first, before, (after,))

    region_depth, lines = region_ends(span_y, depth.T)
    n_rows, q_rows, coef, pick, n_x, n_y, held = column_tables(
        span_x, span_y, mixing, tiles, slot_depth, inflow, region_depth
    )
    columns = (n_rows, q_rows, coef)
    table, extended, mark = block_edges(span_x, span_y, region_depth, across(lines), held)
    edges = lax.all_to_all(table, "gx", split_axis=0, concat_axis=0, tiled=True)
    sums = face_sums(warm, salt, columns, mark)
    flat_edges = edges.reshape(-1, EDGE)
    blocks, rows, mark = outgoing_blocks(span_x, cap, tiles, pick, flat_edges, (n_x, n_y), sums)
    got = lax.all_to_all(blocks, "gx", split_axis=0, concat_axis=0, tiled=True)
    *solved, done = solve(0, (), mark)

    region, lines, folded = region_sums(span_y, rows, got, done)
    basis, diagonal, dots, mark = krylov_basis(
        span_x, span_y, region, across(lines), folded, extended, flat_edges
    )
    sums = lax.all_to_all(dots, both, split_axis=0, concat_axis=0, tiled=True)
    *solved, done = solve(1, solved, mark)
    height, misfit = combine(sums.reshape(-1, 128), basis, diagonal, done)
    return (solved[0], solved[1], height.T, misfit.T)


def solution(mesh):
    in_specs = (
        P(("gx", "gy"), None, None),
        P(("gx", "gy"), None, None),
        P(("gx", "gy"), None),
        P(),
        P(("gx", "gy")),
        P(("gx", "gy"), None),
        P("gy", "gx"),
    )
    out_specs = (
        P(("gx", "gy"), None, None),
        P(("gx", "gy"), None, None),
        P("gy", "gx"),
        P("gy", "gx"),
    )
    return jax.shard_map(on_device, mesh=mesh, in_specs=in_specs, out_specs=out_specs, check_vma=False)
```

```python
import functools
import numpy as np
import jax
import jax.numpy as jnp
from jax import lax
from jax.experimental import pallas as pl
from jax.experimental.pallas import tpu as pltpu
from jax.sharding import PartitionSpec as P

SPAN_E = 60
SPAN_N = 50
KX = 3
KY = 6
LEVELS = 30
HALINE = 0.8
THERMAL = 0.6
RATIO = THERMAL / HALINE
DAMPING = 0.05
COLS = SPAN_E * SPAN_N
TILES = 24
SLOT_ROWS = 24
STEP = 25
PITCH = 33
EDGE = 384
FLAT = TILES * 128
RY = KY * SPAN_N
RX = KX * SPAN_E
GY = 312
GX = 256
F32 = jnp.float32
MIB = 2**20


def widths():
    return [(c, min(128, COLS - 128 * c)) for c in range(TILES)]


def vm():
    return pl.BlockSpec(memory_space=pltpu.VMEM)


def sm():
    return pl.BlockSpec(memory_space=pltpu.SMEM)


def hbm():
    return pl.BlockSpec(memory_space=pltpu.HBM)


def divide(x, d):
    return (x * (2**20 // d + 1)) >> 20


def coefficient(coef, kind, k):
    return coef[8 * (kind * LEVELS + k) : 8 * (kind * LEVELS + k) + 8, :]


def fill_coefficients(mixing, coef):
    ones = jnp.ones((8, 128), F32)
    base = ones
    for k in range(LEVELS):
        last = 8 * (2 * LEVELS + k)
        coef[last : last + 8, :] = ones / base
        if k + 1 < LEVELS:
            here = jnp.full((8, 128), mixing[k], F32)
            q = ones / (base + here)
            g = here * q
            coef[8 * k : 8 * k + 8, :] = g
            coef[8 * (LEVELS + k) : 8 * (LEVELS + k) + 8, :] = q
            base = ones + here - here * g


def spread_slots(rows, slots_by_column):
    for c, w in widths():
        rows[c * STEP : c * STEP + slots_by_column.shape[0], 0:w] = slots_by_column[:, c * 128 : c * 128 + w]


def pieces_of(rows, start, step):
    return [rows[pl.ds(u * 8 * step + start, 8, stride=step), :] for u in range(TILES // 8)]


MID = 25


ROW_SIZE = TILES * PITCH + 8
MID_SIZE = 32 * MID + 8


def copy_in(rows, base, values):
    for c, w in widths():
        rows[base + c * PITCH : base + c * PITCH + LEVELS, 0:w] = values(c, w)


def level_at(j, k, u):
    start = j * MID_SIZE + k * MID + u * 8
    return slice(start, start + 8)


def columns_at(j, k, u):
    return pl.ds(j * ROW_SIZE + u * 8 * PITCH + k, 8, stride=PITCH)


AHEAD = 4
BEHIND = 3


def solve_body(first, count, extra, warm, salt, n_rows, q_rows, coef, *rest):
    warm_out, salt_out, _, warm_in, salt_in, warm_done, salt_done, *rest = rest[extra:]
    warm_rows, salt_rows, warm_mid, salt_mid, came, left = rest

    def fetch(i):
        b = lax.rem(i, AHEAD)
        return [
            pltpu.make_async_copy(source.at[first + i], to.at[b], came.at[b, d])
            for d, (source, to) in enumerate(((warm, warm_in), (salt, salt_in)))
        ]

    def put(i):
        b = lax.rem(i, BEHIND)
        return [
            pltpu.make_async_copy(source.at[b], to.at[first + i], left.at[b, d])
            for d, (source, to) in enumerate(((warm_done, warm_out), (salt_done, salt_out)))
        ]

    for i in range(min(AHEAD, count)):
        for copy in fetch(i):
            copy.start()
    each = [(0, u) for u in range(TILES // 8)]

    def one(i, carry):
        b = lax.rem(i, AHEAD)
        n, t, s = {}, {}, {}
        for copy in fetch(i):
            copy.wait()
        copy_in(warm_rows, 0, lambda c, w: warm_in[b, :, c * 128 : c * 128 + w])
        copy_in(salt_rows, 0, lambda c, w: salt_in[b, :, c * 128 : c * 128 + w])

        @pl.when(i + AHEAD < count)
        def _():
            for copy in fetch(i + AHEAD):
                copy.start()

        for u, deep in enumerate(pieces_of(n_rows, first + i, STEP)):
            n[0, u] = deep
        for u, heat in enumerate(pieces_of(q_rows, first + i, STEP)):
            t[0, u] = jnp.where(n[0, u] > 0, heat, 0.0)
        for k in range(LEVELS):
            g = coefficient(coef, 0, k - 1) if k else None
            for j, u in each:
                rt = warm_rows[columns_at(j, k, u), :]
                rs = salt_rows[columns_at(j, k, u), :]
                if k == 0:
                    t[j, u] = rt + t[j, u]
                    s[j, u] = rs
                else:
                    e = jnp.where(n[j, u] > k, g, 0.0)
                    t[j, u] = rt + e * t[j, u]
                    s[j, u] = rs + e * s[j, u]
                warm_mid[level_at(j, k, u), :] = t[j, u]
                salt_mid[level_at(j, k, u), :] = s[j, u]
        for k in range(LEVELS - 1, -1, -1):
            last = coefficient(coef, 2, k)
            q = coefficient(coef, 1, k) if k + 1 < LEVELS else None
            g = coefficient(coef, 0, k) if k + 1 < LEVELS else None
            for j, u in each:
                a = jnp.where(n[j, u] > k, last, 1.0)
                if k + 1 < LEVELS:
                    more = n[j, u] > k + 1
                    a = jnp.where(more, q, a)
                    e = jnp.where(more, g, 0.0)
                    t[j, u] = a * warm_mid[level_at(j, k, u), :] + e * t[j, u]
                    s[j, u] = a * salt_mid[level_at(j, k, u), :] + e * s[j, u]
                else:
                    t[j, u] = a * t[j, u]
                    s[j, u] = a * s[j, u]
                warm_mid[level_at(j, k, u), :] = t[j, u]
                salt_mid[level_at(j, k, u), :] = s[j, u]

        @pl.when(i >= BEHIND)
        def _():
            for copy in put(i - BEHIND):
                copy.wait()

        o = lax.rem(i, BEHIND)
        for c, w in widths():
            for k in range(0, LEVELS, 8):
                h = min(8, LEVELS - k)
                part = pl.ds(k * MID + c, h, stride=MID)
                warm_done[o, k : k + h, c * 128 : c * 128 + w] = warm_mid[part, :][:, 0:w]
                salt_done[o, k : k + h, c * 128 : c * 128 + w] = salt_mid[part, :][:, 0:w]
        for copy in put(i):
            copy.start()
        return carry

    lax.fori_loop(0, count, one, 0)
    for i in range(max(0, count - BEHIND), count):
        for copy in put(i):
            copy.wait()


def mark_shape():
    return jax.ShapeDtypeStruct((8, 128), F32)


def coefficient_shape():
    return (3 * LEVELS * 8, 128)


def solve_columns(warm, salt, columns, first, count, before, after):
    extra = len(before) + len(after)
    blocks = lambda size: pltpu.VMEM((size, LEVELS, COLS), F32)
    return pl.pallas_call(
        functools.partial(solve_body, first, count, extra),
        out_shape=(jax.ShapeDtypeStruct(warm.shape, F32), jax.ShapeDtypeStruct(salt.shape, F32), mark_shape()),
        in_specs=[hbm(), hbm()] + [vm()] * 3 + [hbm()] * extra,
        out_specs=(hbm(), hbm(), hbm()),
        scratch_shapes=[blocks(AHEAD)] * 2
        + [blocks(BEHIND)] * 2
        + [pltpu.VMEM((ROW_SIZE, 128), F32)] * 2
        + [pltpu.VMEM((MID_SIZE, 128), F32)] * 2
        + [pltpu.SemaphoreType.DMA((AHEAD, 2)), pltpu.SemaphoreType.DMA((BEHIND, 2))],
        input_output_aliases={5: 0, 6: 1} if before else {},
        compiler_params=pltpu.CompilerParams(vmem_limit_bytes=49 * MIB),
        cost_estimate=pl.CostEstimate(flops=count * 2_000_000, bytes_accessed=count * 1_600_000, transcendentals=0),
        name="column_solve",
    )(warm, salt, *columns, *before, *after)


def rim_sources():
    lane = lax.broadcasted_iota(jnp.int32, (8, 128), 1)
    one = jnp.where(lane < 64, lane, lane - 64)
    along_x = jnp.where(one < SPAN_N, one * SPAN_E + jnp.where(lane < 64, 0, SPAN_E - 1), -1)
    along_y = jnp.where(one < SPAN_E, one + jnp.where(lane < 64, 0, COLS - SPAN_E), -1)
    return along_x, along_y


def lanes_of(x, index):
    return jnp.take_along_axis(x, index, axis=1, mode="promise_in_bounds")


def rim_of(tile):
    sources = rim_sources()
    used = (range(TILES), (0, TILES - 2, TILES - 1))
    out = [None, None]
    for c in range(TILES):
        now = tile(c)
        for d in range(2):
            if c in used[d]:
                before = out[d] or [jnp.zeros((8, 128), F32)] * len(now)
                here = (sources[d] >> 7) == c
                out[d] = [jnp.where(here, lanes_of(v, sources[d] & 127), p) for v, p in zip(now, before)]
    return out


def tables_body(span_x, span_y, mixing, ids, depth, inflow, after, *rest):
    n_rows, q_rows, coef, pick, rim_x, rim_y, listed, padded = rest
    slots = depth.shape[0]
    n_rows[...] = jnp.zeros(n_rows.shape, jnp.int32)
    spread_slots(n_rows, depth)
    spread_slots(q_rows, inflow)
    fill_coefficients(mixing, coef)
    padded[...] = jnp.zeros((SLOT_ROWS, FLAT), F32)
    padded[0:slots, 0:COLS] = depth[...].astype(F32)
    rims = rim_of(lambda c: [padded[8 * g : 8 * g + 8, c * 128 : c * 128 + 128] for g in range(SLOT_ROWS // 8)])
    for ref, parts in zip((rim_x, rim_y), rims):
        ref[...] = jnp.concatenate(parts, axis=0)
    blocks_x = KX * span_x
    row = lax.broadcasted_iota(jnp.int32, (SLOT_ROWS, 128), 0)
    held = jnp.zeros((SLOT_ROWS, 128), jnp.int32)
    for s in range(slots):
        held = jnp.where(row == s, jnp.maximum(ids[s], 0), held)
    lane = lax.broadcasted_iota(jnp.int32, (8, 128), 1)
    line = jnp.full((8, 128), -1.0, F32)
    for s in range(slots):
        line = jnp.where(lane == s, ids[s].astype(F32), line)
    listed[...] = line
    up = divide(held, blocks_x)
    across = held - blocks_x * up
    band = up - KY * divide(up, KY)

    def spot(b, m, folds=False):
        o = divide(b, KX)
        c = b - KX * o
        return jnp.where(folds, span_x - 1 - o, o) * 32 + c * 8 + m

    spots = (
        spot(jnp.where(across == 0, blocks_x, across) - 1, band + 1),
        spot(jnp.where(across == blocks_x - 1, -1, across) + 1, band + 1),
        spot(across, band),
        spot(across, band + 2, up == KY * span_y - 1),
    )
    at = lax.broadcasted_iota(jnp.int32, (SLOT_ROWS, 128), 1)
    for d, where in enumerate(spots):
        for t in range(span_x * 32 // 128):
            pick[d * SLOT_ROWS : (d + 1) * SLOT_ROWS, t * 128 : t * 128 + 128] = jnp.where(
                at + t * 128 == where, 1.0, 0.0
            )


def column_tables(span_x, span_y, mixing, ids, depth, inflow, after):
    rows = (TILES * STEP + 8, 128)
    return pl.pallas_call(
        functools.partial(tables_body, span_x, span_y),
        out_shape=(
            jax.ShapeDtypeStruct(rows, jnp.int32),
            jax.ShapeDtypeStruct(rows, F32),
            jax.ShapeDtypeStruct(coefficient_shape(), F32),
        )
        + (jax.ShapeDtypeStruct((4 * SLOT_ROWS, span_x * 32), F32),)
        + (jax.ShapeDtypeStruct((SLOT_ROWS, 128), F32),) * 2
        + (jax.ShapeDtypeStruct((8, 128), F32),),
        in_specs=[sm(), sm(), vm(), vm(), hbm()],
        out_specs=(vm(),) * 7,
        scratch_shapes=[pltpu.VMEM((SLOT_ROWS, FLAT), F32)],
        compiler_params=pltpu.CompilerParams(vmem_limit_bytes=12 * MIB),
        cost_estimate=pl.CostEstimate(flops=5_000_000, bytes_accessed=3_000_000, transcendentals=0),
        name="column_tables",
    )(mixing, ids, depth, inflow, after)


def spread_lines(span_y, top, bottom, out):
    here = lax.axis_index("gy")
    for p in range(span_y):
        out[p] = jnp.where(here == p - 1, top, jnp.where(here == p + 1, bottom, 0.0))


def beside_lines(span_y, lines, folded):
    here = lax.axis_index("gy")
    ups = jnp.where(here == span_y - 1, folded, lines[jnp.minimum(here + 1, span_y - 1)])
    downs = jnp.where(here == 0, 0.0, lines[jnp.maximum(here - 1, 0)])
    return ups, downs


def edges_body(span_x, span_y, depth, lines, held, table, extended, _, rows):
    ups, downs = beside_lines(span_y, lines, 0.0)
    top = lax.axis_index("gy") == span_y - 1
    extended[...] = depth[...]
    extended[RY : RY + 4, :] = ups[0:4]
    extended[GY - 4 : GY, :] = downs[0:4]
    lane = lax.broadcasted_iota(jnp.int32, (8, GX), 1)
    pick = lax.broadcasted_iota(jnp.int32, (8, GX), 0)
    ext16 = extended[...].astype(jnp.bfloat16)

    def columns(wanted):
        hot = jnp.where(lane == wanted, 1.0, 0.0).astype(jnp.bfloat16)
        out = lax.dot_general(hot, ext16, (((1,), (1,)), ((), ())), preferred_element_type=F32)
        return jnp.concatenate([out, jnp.zeros((8, EDGE - GY), F32)], axis=1)

    sides = columns(jnp.where(pick < 3, pick * SPAN_E, jnp.where(pick < 6, (pick - 3) * SPAN_E + SPAN_E - 1, -1)))
    rows[...] = jnp.zeros((16, GX), F32)
    for m in range(KY + 1):
        rows[m + 1 : m + 2, :] = extended[m * SPAN_N : m * SPAN_N + 1, :]
        y = m * SPAN_N - 1 if m else GY - 1
        rows[8 + m : 9 + m, :] = extended[y : y + 1, :]
    turned = turn(jnp.concatenate([extended[RY - 1 - y : RY - y, :] for y in range(4)] * 2, axis=0))
    rows[KY + 1 : KY + 2, :] = jnp.where(top, turned[0:1], rows[KY + 1 : KY + 2, :])
    low = rows[0:8, :]
    high = rows[8:16, :]
    lane1 = lane[:, 0:128]
    for b in range(KX):
        a = pltpu.roll(low, (192 - b * SPAN_E) % GX, 1)
        z = pltpu.roll(high, (128 - b * SPAN_E) % GX, 1)
        both = jnp.where(lane >= 192, a, z)
        table[0, 8 * b : 8 * b + 8, 128:256] = both[:, 128:256]
        table[0, 8 * b : 8 * b + 8, 0:128] = jnp.zeros((8, 128), F32)
        table[0, 8 * b : 8 * b + 8, 256:384] = jnp.zeros((8, 128), F32)
    for m in range(KY):
        z = pltpu.roll(sides, (EDGE - m * SPAN_N) % EDGE, 1)[:, 0:128]
        a = pltpu.roll(sides, (EDGE + 64 - m * SPAN_N) % EDGE, 1)[:, 0:128]
        for b in range(KX):
            table[0, 8 * b + m + 1 : 8 * b + m + 2, 0:128] = jnp.where(
                lane1[0:1] >= 64, a[b : b + 1], z[3 + b : 4 + b]
            )
    table[0, 0:1, 256:384] = held[0:1, :]
    table[0, 8:12, 256:384] = turned[0:4, 0:128]
    table[0, 12:16, 256:384] = turned[0:4, 128:256]
    table[0, 24:32, :] = columns(jnp.where(pick < 4, pick, RX - 8 + pick))
    for d in range(1, span_x):
        table[d] = table[0]


def block_edges(span_x, span_y, depth, lines, held):
    return pl.pallas_call(
        functools.partial(edges_body, span_x, span_y),
        out_shape=(
            jax.ShapeDtypeStruct((span_x, 32, EDGE), F32),
            jax.ShapeDtypeStruct((GY, GX), F32),
            mark_shape(),
        ),
        in_specs=[vm()] * 3,
        out_specs=(vm(),) * 2 + (hbm(),),
        scratch_shapes=[pltpu.VMEM((16, GX), F32)],
        compiler_params=pltpu.CompilerParams(vmem_limit_bytes=12 * MIB),
        name="block_edges",
    )(depth, lines, held)


def ends_body(span_y, depth, region, out, wide):
    wide[...] = jnp.zeros(wide.shape, F32)
    wide[0:RX, 0:RY] = depth[...].astype(F32)
    region[...] = wide[...].T[0:GY, :]

    def lines(first):
        return jnp.concatenate([region[first : first + 4, :], jnp.zeros((4, GX), F32)], axis=0)

    spread_lines(span_y, lines(RY - 4), lines(0), out)


def region_ends(span_y, depth_t):
    return pl.pallas_call(
        functools.partial(ends_body, span_y),
        out_shape=(
            jax.ShapeDtypeStruct((GY, GX), F32),
            jax.ShapeDtypeStruct((span_y, 8, GX), F32),
        ),
        in_specs=[vm()],
        out_specs=(vm(),) * 2,
        scratch_shapes=[pltpu.VMEM((GX, EDGE), F32)],
        compiler_params=pltpu.CompilerParams(vmem_limit_bytes=12 * MIB),
        name="region_ends",
    )(depth_t)


ROWS = 40
HALF = 13


SLOT_STEP = 201


def shifted(x, by):
    rows = x.shape[0]
    lane = lax.broadcasted_iota(jnp.int32, x.shape, 1)
    near = pltpu.roll(x, -by % 128, 1)
    far = pltpu.roll(near, (rows - 1) if by > 0 else 1, 0)
    return jnp.where(lane < 128 - by if by > 0 else lane >= -by, near, far)


def flux_body(
    slots, group, warm, salt, n_rows, q_rows, coef, after, pieces, rim_x, rim_y,
    faces, found, rows, middle, totals, warm_in, salt_in, came,
):
    lane = lax.broadcasted_iota(jnp.int32, (1, FLAT), 1)
    col = lane - SPAN_E * divide(lane, SPAN_E)

    def fetch(step):
        b = lax.rem(step, 2) * group
        return [
            pltpu.make_async_copy(source.at[step * group + j], to.at[b + j], came.at[b + j, d])
            for j in range(group)
            for d, (source, to) in enumerate(((warm, warm_in), (salt, salt_in)))
        ]

    for step in range(min(2, slots // group)):
        for copy in fetch(step):
            copy.start()
    faces[...] = jnp.zeros(faces.shape, jnp.int32)

    def one(step, carry):
        b = lax.rem(step, 2) * group
        many = range(group)
        each = [(j, u) for j in many for u in range(TILES // 8)]
        place = lax.broadcasted_iota(jnp.int32, (TILES, 128), 0) * 128
        place = place + lax.broadcasted_iota(jnp.int32, (TILES, 128), 1)
        in_row = place - SPAN_E * divide(place, SPAN_E)
        n, x = {}, {}
        for copy in fetch(step):
            copy.wait()
        for j in many:
            copy_in(
                rows,
                j * ROW_SIZE,
                lambda c, w: salt_in[b + j, :, c * 128 : c * 128 + w] - RATIO * warm_in[b + j, :, c * 128 : c * 128 + w],
            )
            slot = step * group + j
            for u, deep in enumerate(pieces_of(n_rows, slot, STEP)):
                n[j, u] = deep
            for u, heat in enumerate(pieces_of(q_rows, slot, STEP)):
                x[j, u] = RATIO * heat
            deep = jnp.concatenate([n[j, u] for u in range(TILES // 8)], axis=0)
            for d, (by, inside) in enumerate(
                (
                    (1, in_row < SPAN_E - 1),
                    (-1, in_row > 0),
                    (SPAN_E, place < COLS - SPAN_E),
                    (-SPAN_E, place >= SPAN_E),
                )
            ):
                start = (8 * j + d) * MID
                faces[start : start + TILES, :] = jnp.where(inside, jnp.minimum(deep, shifted(deep, by)), 0)

        @pl.when(step + 2 < slots // group)
        def _():
            for copy in fetch(step + 2):
                copy.start()

        for k in range(LEVELS):
            g = coefficient(coef, 0, k - 1) if k else None
            for j, u in each:
                right = rows[columns_at(j, k, u), :]
                x[j, u] = right + g * x[j, u] if k else right - x[j, u]
                middle[j, k, u * 8 : u * 8 + 8, :] = x[j, u]
        for k in range(LEVELS - 1, -1, -1):
            last = coefficient(coef, 2, k)
            q = coefficient(coef, 1, k) if k + 1 < LEVELS else None
            g = coefficient(coef, 0, k) if k + 1 < LEVELS else None
            for j, u in each:
                if k + 1 < LEVELS:
                    more = n[j, u] > k + 1
                    a = jnp.where(more, q, last)
                    e = jnp.where(more, g, 0.0)
                    x[j, u] = a * middle[j, k, u * 8 : u * 8 + 8, :] + e * x[j, u]
                else:
                    x[j, u] = last * x[j, u]
                middle[j, k, u * 8 : u * 8 + 8, :] = x[j, u]
        zero = jnp.zeros((8, 128), F32)
        pressure = {at: zero for at in each}
        total = {at: zero for at in each}
        for k in range(LEVELS):
            for j, u in each:
                pressure[j, u] = pressure[j, u] + middle[j, k, u * 8 : u * 8 + 8, :]
                total[j, u] = total[j, u] + pressure[j, u]
                totals[level_at(j, k, u), :] = total[j, u]

        for j in many:
            slot = step * group + j

            def tile(c):
                now = [totals[pl.ds(j * MID_SIZE + 8 * g * MID + c, 8, stride=MID), :] for g in range(4)]
                level = faces[pl.ds(8 * j * MID + c, 8, stride=MID), :] - 1
                sums = zero
                for g in range(4):
                    one_of = jnp.take_along_axis(now[g], level & 7, axis=0, mode="promise_in_bounds")
                    sums = jnp.where((level >> 3) == g, one_of, sums)
                found[pl.ds(slot * SLOT_STEP + c * 8, 8), :] = sums
                return now

            for ref, parts in zip((rim_x, rim_y), rim_of(tile)):
                for g in range(4):
                    ref[slot, 8 * g : 8 * g + 8, :] = parts[g]
        return carry

    lax.fori_loop(0, slots // group, one, 0)

    def flat(d):
        return jnp.concatenate(
            [found[pl.ds(c * 8 + d, SLOT_ROWS, stride=SLOT_STEP), :] for c in range(TILES)], axis=1
        )

    east, west, north, south = (flat(d) for d in range(4))
    from_east = pltpu.roll(west, FLAT - 1, 1)
    from_west = pltpu.roll(east, 1, 1)
    net = -(east + west + north + south)
    net = net + jnp.where(col < SPAN_E - 1, from_east, 0.0)
    net = net + jnp.where(col > 0, from_west, 0.0)
    net = net + jnp.where(lane < COLS - SPAN_E, pltpu.roll(south, FLAT - SPAN_E, 1), 0.0)
    net = net + jnp.where(lane >= SPAN_E, pltpu.roll(north, SPAN_E, 1), 0.0)
    l = lax.broadcasted_iota(jnp.int32, (1, 128), 1)
    for t in range(26):
        halves = []
        for h in range(2):
            r = 2 * t + h
            if r in (0, SPAN_N + 1):
                continue
            start = (r - 1) * SPAN_E
            a = start // 128
            row = net[:, a * 128 : a * 128 + 128]
            if start % 128 + SPAN_E > 128:
                row = jnp.where(l >= start % 128, row, net[:, a * 128 + 128 : a * 128 + 256])
            row = pltpu.roll(row, (64 * h + 1 - start) % 128, 1)
            halves.append(jnp.where((l > 64 * h) & (l <= 64 * h + SPAN_E), row, 0.0))
        pieces[t * STEP : t * STEP + SLOT_ROWS, :] = halves[0] + halves[1] if len(halves) == 2 else halves[0]


def face_sums(warm, salt, columns, after):
    slots = warm.shape[0]
    group = 3 if slots % 3 == 0 else 1
    return pl.pallas_call(
        functools.partial(flux_body, slots, group),
        out_shape=(jax.ShapeDtypeStruct((26 * STEP + 6, 128), F32),)
        + (jax.ShapeDtypeStruct((slots, 32, 128), F32),) * 2,
        in_specs=[hbm(), hbm()] + [vm()] * 3 + [hbm()],
        out_specs=(vm(),) * 3,
        scratch_shapes=[
            pltpu.VMEM((8 * group * MID, 128), jnp.int32),
            pltpu.VMEM((SLOT_ROWS * SLOT_STEP, 128), F32),
            pltpu.VMEM((group * ROW_SIZE, 128), F32),
            pltpu.VMEM((group, LEVELS, TILES, 128), F32),
            pltpu.VMEM((group * MID_SIZE, 128), F32),
            pltpu.VMEM((2 * group, LEVELS, COLS), F32),
            pltpu.VMEM((2 * group, LEVELS, COLS), F32),
            pltpu.SemaphoreType.DMA((2 * group, 2)),
        ],
        compiler_params=pltpu.CompilerParams(vmem_limit_bytes=49 * MIB),
        cost_estimate=pl.CostEstimate(flops=40_000_000, bytes_accessed=15_000_000, transcendentals=0),
        name="face_sums",
    )(warm, salt, *columns, after)


def received_rows(span_x, cap, edges):
    blocks_x = KX * span_x
    keys = jnp.concatenate([edges[d * 32 : d * 32 + 1, 256:384] for d in range(span_x)], axis=0).astype(jnp.int32)
    held = jnp.maximum(keys, 0)
    owner = jnp.where(keys >= 0, divide(held - blocks_x * divide(held, blocks_x), KX), -1)
    one_of = [jnp.where(owner == o, 1.0, 0.0) for o in range(span_x)]
    earlier = lax.broadcasted_iota(jnp.int32, (128, 128), 0) < lax.broadcasted_iota(jnp.int32, (128, 128), 1)
    counted = jnp.dot(
        jnp.concatenate(one_of, axis=0).astype(jnp.bfloat16),
        jnp.where(earlier, 1.0, 0.0).astype(jnp.bfloat16),
        preferred_element_type=F32,
    )
    at = lax.broadcasted_iota(jnp.int32, (span_x, 128), 0).astype(F32) * cap + 1.0
    for o in range(span_x):
        at = at + one_of[o] * counted[o * span_x : (o + 1) * span_x]
    here_x = lax.axis_index("gx")
    first = lax.axis_index("gy") * KY

    def beside(x):
        x = jnp.where(x < 0, x + blocks_x, x)
        return jnp.where(x >= blocks_x, x - blocks_x, x)

    base = here_x * KX
    over = (span_x - 1 - here_x) * KX
    wanted = [(first + p // KX) * blocks_x + base + p % KX for p in range(KX * KY)]
    wanted += [(first + p) * blocks_x + beside(base - 1) for p in range(KY)]
    wanted += [(first + p) * blocks_x + beside(base + KX) for p in range(KY)]
    wanted += [(first + KY - 1) * blocks_x + x for x in [over + g for g in range(KX)]]
    wanted += [(first + KY - 1) * blocks_x + beside(x) for x in (over - 1, over + KX)]
    lines = [jnp.sum(jnp.where(keys == w, at, 0.0), axis=0, keepdims=True) for w in wanted]
    lines += [jnp.zeros((1, 128), F32)] * (ROWS - len(lines))
    sums = jnp.sum(jnp.concatenate(lines, axis=0), axis=1, keepdims=True) - 1.0
    return jnp.broadcast_to(sums, (ROWS, 128)).astype(jnp.int32)


def outgoing_body(
    span_x, cap, slots, ids, pick, edges, n_x, n_y, inside, rim_x, rim_y, out, rows, _, pieces, q_x, q_y, source, counts
):
    blocks_x = KX * span_x
    for d in range(span_x):
        counts[d] = 0
    for d in range(span_x * cap):
        source[d] = 0
    for s in range(slots):
        held = jnp.maximum(ids[s], 0)
        owner = divide(held - blocks_x * divide(held, blocks_x), KX)
        rank = counts[owner]

        @pl.when(ids[s] >= 0)
        def _():
            source[owner * cap + jnp.minimum(rank, cap - 1)] = s
            counts[owner] = rank + 1

    rows[...] = received_rows(span_x, cap, edges)
    near = jnp.dot(
        pick[...].astype(jnp.bfloat16), edges[:, 0:GX].astype(jnp.bfloat16), preferred_element_type=F32
    )
    l = lax.broadcasted_iota(jnp.int32, (1, 128), 1)
    w, e, so, no = (near[d * SLOT_ROWS : (d + 1) * SLOT_ROWS] for d in range(4))
    q_x[...] = jnp.zeros(q_x.shape, F32)
    q_y[...] = jnp.zeros(q_y.shape, F32)
    level = lax.broadcasted_iota(jnp.int32, (32, 128), 0).astype(F32) + 1.0
    for n, other, rim, q in (
        (n_x, jnp.where(l < 64, w[:, 0:128], e[:, 0:128]), rim_x, q_x),
        (n_y, jnp.where(l < 64, so[:, 128:256], no[:, 128:256]), rim_y, q_y),
    ):
        face = jnp.minimum(n[...], other)
        for s in range(slots):
            hit = jnp.where(face[s : s + 1] == level, rim[s], 0.0)
            q[s : s + 1, :] = jnp.sum(hit, axis=0, keepdims=True)

    groups = range(SLOT_ROWS // 8)
    lane = lax.broadcasted_iota(jnp.int32, (8, 128), 1)
    in_row = lane & 63
    odd = lane >> 6
    adds = jnp.where((in_row == 0) | (in_row == SPAN_E + 1), 1.0, 0.0)
    adds = jnp.where((in_row == 1) | (in_row == SPAN_E), -1.0, adds)
    zero = jnp.zeros((8, 128), F32)
    strips = [[[zero for _ in groups] for _ in range(2)] for _ in range(2)]
    for t in range(26):
        p, at = t // HALF, 4 * (t % HALF)
        i = 2 * t - 1 + odd
        index = jnp.clip(i, 0, SPAN_N - 1) + jnp.where(in_row >= 32, 64, 0)
        sign = jnp.where((i >= 0) & (i < SPAN_N), adds, 0.0)
        band = (in_row >= at) & (in_row < at + 4)
        for g in groups:
            rows8 = slice(8 * g, 8 * g + 8)
            v = inside[t * STEP + 8 * g : t * STEP + 8 * g + 8, :] + sign * lanes_of(q_x[rows8, :], index)
            core = (in_row >= 1) & (in_row <= SPAN_E)
            if t == 0:
                v = v + jnp.where(core & (odd == 0), pltpu.roll(q_y[rows8, :], 1, 1), 0.0)
                v = v - jnp.where(core & (odd == 1), pltpu.roll(q_y[rows8, :], 65, 1), 0.0)
            if t == 25:
                v = v - jnp.where(core & (odd == 0), pltpu.roll(q_y[rows8, :], 65, 1), 0.0)
                v = v + jnp.where(core & (odd == 1), pltpu.roll(q_y[rows8, :], 1, 1), 0.0)
            pieces[t * STEP + 8 * g : t * STEP + 8 * g + 8, :] = v
            strips[0][p][g] = jnp.where(band, pltpu.roll(v, at, 1), strips[0][p][g])
            strips[1][p][g] = jnp.where(band, pltpu.roll(v, (at - SPAN_E + 2) % 128, 1), strips[1][p][g])
    for side in range(2):
        for p in range(2):
            for g in groups:
                start = (26 + 2 * side + p) * STEP + 8 * g
                pieces[start : start + 8, :] = strips[side][p][g]
    pieces[30 * STEP : 32 * STEP + 8, :] = jnp.zeros((2 * STEP + 8, 128), F32)

    tile_row = lax.broadcasted_iota(jnp.int32, (8, 128), 0)
    corner = (in_row >= 52) & (in_row < 60)
    for d in range(span_x):
        for c in range(cap):
            other = span_x - 1 - d
            own = source[d * cap + c]
            left = source[(d - 1) % span_x * cap + c]
            right = source[(d + 1) % span_x * cap + c]
            fold = source[other * cap + c]
            fold_west = source[(other - 1) % span_x * cap + c]
            fold_east = source[(other + 1) % span_x * cap + c]

            def last(slot):
                return pieces[pl.ds(24 * STEP + slot, 8, stride=STEP), :]

            tail = jnp.where(tile_row < 2, last(own), jnp.where(tile_row < 4, last(right), last(left)))
            tail = jnp.where(tile_row >= 6, pltpu.roll(last(fold), 6, 0), tail)
            tail = jnp.where((tile_row == 3) & corner, pltpu.roll(last(fold_east), 8, 1), tail)
            tail = jnp.where((tile_row == 5) & corner, pltpu.roll(last(fold_west), 8, 1), tail)
            out[d * cap + c, 0:24, :] = pieces[pl.ds(own, 24, stride=STEP), :]
            out[d * cap + c, 24:32, :] = tail


def outgoing_blocks(span_x, cap, ids, pick, edges, rims, sums):
    slots = ids.shape[0]
    return pl.pallas_call(
        functools.partial(outgoing_body, span_x, cap, slots),
        out_shape=(
            jax.ShapeDtypeStruct((span_x * cap, 32, 128), F32),
            jax.ShapeDtypeStruct((ROWS, 128), jnp.int32),
            mark_shape(),
        ),
        in_specs=[sm()] + [vm()] * 7,
        out_specs=(vm(), vm(), hbm()),
        scratch_shapes=[pltpu.VMEM((32 * STEP + 8, 128), F32)]
        + [pltpu.VMEM((SLOT_ROWS, 128), F32)] * 2
        + [pltpu.SMEM((span_x * cap,), jnp.int32), pltpu.SMEM((span_x,), jnp.int32)],
        compiler_params=pltpu.CompilerParams(vmem_limit_bytes=12 * MIB),
        name="outgoing_blocks",
    )(ids, pick, edges, *rims, *sums)


def turn(x):
    lane = lax.broadcasted_iota(jnp.int32, (8, 128), 1)
    halves = [
        jnp.take_along_axis(x[:, h * 128 : h * 128 + 128], 127 - lane, axis=1, mode="promise_in_bounds")
        for h in (1, 0)
    ]
    return pltpu.roll(jnp.concatenate(halves, axis=1), (RX - GX) % GX, 1)


def region_body(span_y, rows, got, after, region, out, folded, tiles, sides):
    tiles[...] = jnp.zeros(tiles.shape, F32)
    sides[...] = jnp.zeros(sides.shape, F32)
    for p in range(KX * KY):
        r = rows[p, 0]
        block = got[pl.ds(pl.multiple_of(jnp.maximum(r, 0) * 32, 32), 32), :]
        block = jnp.where(r >= 0, block, 0.0)
        tiles[pl.ds((p % KX) * 8 + p // KX, 32, stride=STEP), :] = block
    for p in range(2 * KY):
        r = rows[KX * KY + p, 0]
        block = got[pl.ds(pl.multiple_of(jnp.maximum(r, 0) * 32 + 24, 8), 8), :]
        block = jnp.where(r >= 0, block, 0.0)
        sides[pl.ds((p // KY) * 8 + p % KY, 8, stride=17), :] = block
    at_fold = KX * KY + 2 * KY
    for g in range(KX + 2):
        r = rows[at_fold + g, 0]
        block = got[pl.ds(pl.multiple_of(jnp.maximum(r, 0) * 32 + 24, 8), 8), :]
        block = jnp.where(r >= 0, block, 0.0)
        if g < KX:
            for t in range(2):
                tiles[(24 + t) * STEP + g * 8 + 6 : (24 + t) * STEP + g * 8 + 7, :] = block[6 + t : 7 + t]
        elif g == KX:
            sides[5 * 17 + 6 : 5 * 17 + 7, :] = pltpu.roll(block, 120, 1)[5:6]
        else:
            sides[3 * 17 + 14 : 3 * 17 + 15, :] = pltpu.roll(block, 120, 1)[3:4]
    lane = lax.broadcasted_iota(jnp.int32, (8, 128), 1)
    sub = lax.broadcasted_iota(jnp.int32, (8, 128), 0)

    def assembled(r):
        t, base = r // 2, (r % 2) * 64
        v = [tiles[t * STEP + 8 * g : t * STEP + 8 * g + 8, :] for g in range(KX)]
        a = pltpu.roll(v[0], (-1 - base) % 128, 1)
        b = pltpu.roll(v[1], (59 - base) % 128, 1)
        c = pltpu.roll(v[2], (119 - base) % 128, 1)
        to = base + 4 * (t % HALF)
        p = t // HALF
        w = sides[(4 + p) * 17 : (4 + p) * 17 + 8, :]
        e = sides[(2 + p) * 17 + 8 : (2 + p) * 17 + 16, :]
        w = pltpu.roll(w, (125 - to) % 128, 1)
        e = pltpu.roll(e, (51 - to) % 128, 1)
        left = jnp.where(lane <= 60, a, 0.0)
        left = left + jnp.where((lane >= 59) & (lane <= 120), b, 0.0)
        left = left + jnp.where(lane >= 119, c, 0.0)
        left = left + jnp.where(lane == 0, w, 0.0)
        right = jnp.where(lane <= 52, c, 0.0)
        right = right + jnp.where(lane == 127, a, 0.0)
        right = right + jnp.where(lane >= 125, w, 0.0)
        right = right + jnp.where((lane >= 51) & (lane <= 54), e, 0.0)
        return left, right

    region[...] = jnp.zeros(region.shape, F32)
    below = assembled(0)
    above = assembled(SPAN_N + 1)
    over = [above]
    for r in range(1, SPAN_N + 1):
        parts = assembled(r)
        if r > SPAN_N - 3:
            over.insert(1, parts)
        for h in range(2):
            v = parts[h]
            if r == 1:
                v = v + jnp.where((sub >= 1) & (sub < KY), pltpu.roll(above[h], 1, 0), 0.0)
            if r == SPAN_N:
                v = v + jnp.where(sub < KY - 1, pltpu.roll(below[h], 7, 0), 0.0)
            region[pl.ds(h * GY + r - 1, KY, stride=SPAN_N), :] = v[0:KY]
    for h in range(2):
        region[h * GY + RY : h * GY + RY + 1, :] = above[h][KY - 1 : KY]
        region[h * GY + GY - 1 : h * GY + GY, :] = below[h][0:1]

    def lines(ys):
        cut = [
            jnp.concatenate([region[y : y + 1, :], region[GY + y : GY + y + 1, :]], axis=1) for y in ys
        ]
        return jnp.concatenate(cut + [jnp.zeros((8 - len(ys), GX), F32)], axis=0)

    spread_lines(span_y, lines([RY - 3, RY - 2, RY - 1, RY]), lines([GY - 1, 0, 1, 2]), out)
    over = [jnp.concatenate([part[6:7] for part in parts], axis=1) for parts in over]
    folded[...] = turn(jnp.concatenate(over + [jnp.zeros((4, GX), F32)], axis=0))


def region_sums(span_y, rows, got, after):
    return pl.pallas_call(
        functools.partial(region_body, span_y),
        out_shape=(
            jax.ShapeDtypeStruct((2 * GY, 128), F32),
            jax.ShapeDtypeStruct((span_y, 8, GX), F32),
            jax.ShapeDtypeStruct((8, GX), F32),
        ),
        in_specs=[sm(), vm(), hbm()],
        out_specs=(vm(),) * 3,
        scratch_shapes=[pltpu.VMEM((32 * STEP + 8, 128), F32), pltpu.VMEM((8 * 17, 128), F32)],
        compiler_params=pltpu.CompilerParams(vmem_limit_bytes=12 * MIB),
        name="region_sums",
    )(rows, got.reshape(-1, 128), after)


def basis_body(span_x, span_y, region, lines, folded, extended, edges, basis, diag_out, dots, mark):
    ext = extended[...]
    here = lax.axis_index("gx")
    lane8 = lax.broadcasted_iota(jnp.int32, (8, GX), 1)
    row8 = lax.broadcasted_iota(jnp.int32, (8, GX), 0)
    put_west = jnp.where((row8 >= 4) & (lane8 == GX - 8 + row8), 1.0, 0.0).astype(jnp.bfloat16)
    put_east = jnp.where((row8 < 4) & (lane8 == RX + row8), 1.0, 0.0).astype(jnp.bfloat16)
    for other, put in ((here + span_x - 1, put_west), (here + 1, put_east)):
        cols = edges[pl.ds(pl.multiple_of(other % span_x * 32 + 24, 8), 8), :]
        ext = ext + lax.dot_general(
            cols[:, 0:GY].astype(jnp.bfloat16), put, (((0,), (0,)), ((), ())), preferred_element_type=F32
        )

    fold = []
    for step in (0, -1, 1):
        other = span_x - 1 - here + step + span_x
        part = edges[pl.ds(pl.multiple_of(lax.rem(other, span_x) * 32 + 8, 8), 8), 256:384]
        fold.append(jnp.concatenate([part[0:4], part[4:8]], axis=1))
    lane4 = lax.broadcasted_iota(jnp.int32, (4, GX), 1)
    beyond = jnp.where(lane4 < RX, fold[0], 0.0)
    beyond = jnp.where((lane4 >= RX) & (lane4 < RX + 4), pltpu.roll(fold[1], RX, 1), beyond)
    beyond = jnp.where(lane4 >= GX - 4, pltpu.roll(fold[2], GX - RX, 1), beyond)
    beyond = jnp.where(lax.axis_index("gy") == span_y - 1, beyond, 0.0)
    ext = ext + jnp.concatenate([jnp.zeros((RY, GX), F32), beyond, jnp.zeros((GY - RY - 4, GX), F32)], axis=0)

    def south_of(x):
        return pltpu.roll(x, 1, 0)

    def north_of(x):
        return pltpu.roll(x, GY - 1, 0)

    def west_of(x):
        return pltpu.roll(x, 1, 1)

    def east_of(x):
        return pltpu.roll(x, GX - 1, 1)

    to_east = jnp.minimum(ext, east_of(ext)) / LEVELS
    to_north = jnp.minimum(ext, north_of(ext)) / LEVELS
    to_west = west_of(to_east)
    to_south = south_of(to_north)
    diagonal = jnp.where(ext > 0, DAMPING, 1.0) + to_east + to_west + to_north + to_south
    inverse = 1.0 / diagonal
    ups, downs = beside_lines(span_y, lines, folded[...])
    partial = jnp.concatenate([region[0:GY, :], region[GY : 2 * GY, :]], axis=1)
    gap = lambda rows: jnp.zeros((rows, GX), F32)
    extra = jnp.concatenate(
        [downs[3:4], gap(RY - 2), ups[0:4], gap(GY - RY - 6), downs[0:3]], axis=0
    )
    zero = (partial + extra) * (HALINE / LEVELS) * inverse

    def smooth(x):
        return inverse * (
            to_east * east_of(x) + to_west * west_of(x) + to_north * north_of(x) + to_south * south_of(x)
        )

    vectors = [zero, smooth(zero)]
    vectors.append(2.0 * smooth(vectors[1]) - vectors[0])
    vectors.append(2.0 * smooth(vectors[2]) - vectors[1])
    lane = lax.broadcasted_iota(jnp.int32, (GY, GX), 1)
    row = lax.broadcasted_iota(jnp.int32, (GY, GX), 0)
    inside = (lane < RX) & (row < RY)
    diag_out[...] = diagonal
    clean = [jnp.where(inside, v, 0.0) for v in vectors]
    position = lax.broadcasted_iota(jnp.int32, (8, 128), 1)
    packed = jnp.zeros((8, 128), F32)
    number = 0
    for i in range(4):
        basis[i] = clean[i]
        scaled = clean[i] * diagonal
        for j in range(i, 4):
            prod = scaled * clean[j]
            part = jnp.sum(prod.reshape(GY // 8, 8, GX), axis=0)
            part = part[:, 0:128] + part[:, 128:256]
            packed = packed + jnp.where(position == number, jnp.sum(part, axis=1, keepdims=True), 0.0)
            number += 1
    for d in range(dots.shape[0]):
        dots[d] = packed


def krylov_basis(span_x, span_y, region, lines, folded, extended, edges):
    return pl.pallas_call(
        functools.partial(basis_body, span_x, span_y),
        out_shape=(
            jax.ShapeDtypeStruct((4, GY, GX), F32),
            jax.ShapeDtypeStruct((GY, GX), F32),
            jax.ShapeDtypeStruct((span_x * span_y, 8, 128), F32),
            mark_shape(),
        ),
        in_specs=[vm()] * 5,
        out_specs=(vm(),) * 3 + (hbm(),),
        compiler_params=pltpu.CompilerParams(vmem_limit_bytes=12 * MIB),
        name="krylov_basis",
    )(region, lines, folded, extended, edges)


def combine_body(dots, basis, diagonal, after, height, misfit):
    sums = jnp.sum(dots[...], axis=0, keepdims=True)
    lane = lax.broadcasted_iota(jnp.int32, (1, 128), 1)
    g = {}
    number = 0
    for i in range(4):
        for j in range(i, 4):
            v = jnp.sum(jnp.where(lane == number, sums, 0.0), axis=1, keepdims=True)
            g[i, j] = g[j, i] = v
            number += 1

    def inner(a, b):
        out = jnp.zeros((1, 1), F32)
        for i in range(4):
            for j in range(4):
                if a[i] is not None and b[j] is not None:
                    out = out + a[i] * b[j] * g[i, j]
        return out

    def add(a, b):
        return a if b is None else b if a is None else a + b

    def image(a):
        out = list(a)
        for k in range(3):
            if a[k] is None:
                continue
            if k == 0:
                out[1] = add(out[1], -a[0])
            else:
                out[k + 1] = add(out[k + 1], -0.5 * a[k])
                out[k - 1] = add(out[k - 1], -0.5 * a[k])
        return out

    one = jnp.ones((1, 1), F32)
    res = [one, None, None, None]
    way = list(res)
    high = [None] * 4
    gamma = inner(res, res)
    for iteration in range(3):
        moved = image(way)
        size = gamma / inner(way, moved)
        high = [h if w is None else add(h, size * w) for h, w in zip(high, way)]
        res = [r if m is None else add(r, -size * m) for r, m in zip(res, moved)]
        if iteration < 2:
            after = inner(res, res)
            ratio = after / gamma
            way = [r if w is None else add(r, ratio * w) for r, w in zip(res, way)]
            gamma = after
    out = jnp.zeros((GY, GX), F32)
    left = jnp.zeros((GY, GX), F32)
    for k in range(4):
        v = basis[k]
        if high[k] is not None:
            out = out + high[k] * v
        left = left + res[k] * v
    gap = jnp.zeros((384 - GY, GX), F32)
    height[...] = jnp.concatenate([out, gap], axis=0).T[0:RX, 0:RY]
    misfit[...] = jnp.concatenate([left * diagonal[...], gap], axis=0).T[0:RX, 0:RY]


def combine(dots, basis, diagonal, after):
    return pl.pallas_call(
        combine_body,
        out_shape=(jax.ShapeDtypeStruct((RX, RY), F32),) * 2,
        in_specs=[vm()] * 3 + [hbm()],
        out_specs=(vm(),) * 2,
        compiler_params=pltpu.CompilerParams(vmem_limit_bytes=12 * MIB),
        name="combine",
    )(dots, basis, diagonal, after)


def across(lines):
    return lax.all_to_all(lines, "gy", split_axis=0, concat_axis=0, tiled=True)


def on_device(warm, salt, inflow, mixing, tiles, slot_depth, depth):
    span_x = lax.axis_size("gx")
    span_y = lax.axis_size("gy")
    slots = tiles.shape[0]
    cap = (KX * KY + span_x - 1) // span_x
    both = ("gx", "gy")
    bounds = [slots * i // 18 for i in (0, 12, 18)]

    def solve(part, before, after):
        first, end = bounds[part], bounds[part + 1]
        return solve_columns(warm, salt, columns, first, end - first, before, (after,))

    region_depth, lines = region_ends(span_y, depth.T)
    n_rows, q_rows, coef, pick, n_x, n_y, held = column_tables(
        span_x, span_y, mixing, tiles, slot_depth, inflow, region_depth
    )
    columns = (n_rows, q_rows, coef)
    table, extended, mark = block_edges(span_x, span_y, region_depth, across(lines), held)
    edges = lax.all_to_all(table, "gx", split_axis=0, concat_axis=0, tiled=True)
    sums = face_sums(warm, salt, columns, mark)
    flat_edges = edges.reshape(-1, EDGE)
    blocks, rows, mark = outgoing_blocks(span_x, cap, tiles, pick, flat_edges, (n_x, n_y), sums)
    got = lax.all_to_all(blocks, "gx", split_axis=0, concat_axis=0, tiled=True)
    *solved, done = solve(0, (), mark)

    region, lines, folded = region_sums(span_y, rows, got, done)
    basis, diagonal, dots, mark = krylov_basis(
        span_x, span_y, region, across(lines), folded, extended, flat_edges
    )
    sums = lax.all_to_all(dots, both, split_axis=0, concat_axis=0, tiled=True)
    *solved, done = solve(1, solved, mark)
    height, misfit = combine(sums.reshape(-1, 128), basis, diagonal, done)
    return (solved[0], solved[1], height.T, misfit.T)


def solution(mesh):
    in_specs = (
        P(("gx", "gy"), None, None),
        P(("gx", "gy"), None, None),
        P(("gx", "gy"), None),
        P(),
        P(("gx", "gy")),
        P(("gx", "gy"), None),
        P("gy", "gx"),
    )
    out_specs = (
        P(("gx", "gy"), None, None),
        P(("gx", "gy"), None, None),
        P("gy", "gx"),
        P("gy", "gx"),
    )
    return jax.shard_map(on_device, mesh=mesh, in_specs=in_specs, out_specs=out_specs, check_vma=False)
```

```python
import functools
import numpy as np
import jax
import jax.numpy as jnp
from jax import lax
from jax.experimental import pallas as pl
from jax.experimental.pallas import tpu as pltpu
from jax.sharding import PartitionSpec as P

SPAN_E = 60
SPAN_N = 50
KX = 3
KY = 6
LEVELS = 30
HALINE = 0.8
THERMAL = 0.6
RATIO = THERMAL / HALINE
DAMPING = 0.05
COLS = SPAN_E * SPAN_N
TILES = 24
SLOT_ROWS = 24
STEP = 25
PITCH = 33
EDGE = 384
FLAT = TILES * 128
RY = KY * SPAN_N
RX = KX * SPAN_E
GY = 312
GX = 256
F32 = jnp.float32
MIB = 2**20


def widths():
    return [(c, min(128, COLS - 128 * c)) for c in range(TILES)]


def vm():
    return pl.BlockSpec(memory_space=pltpu.VMEM)


def sm():
    return pl.BlockSpec(memory_space=pltpu.SMEM)


def hbm():
    return pl.BlockSpec(memory_space=pltpu.HBM)


def divide(x, d):
    return (x * (2**20 // d + 1)) >> 20


def coefficient(coef, kind, k):
    return coef[8 * (kind * LEVELS + k) : 8 * (kind * LEVELS + k) + 8, :]


def fill_coefficients(mixing, coef):
    ones = jnp.ones((8, 128), F32)
    base = ones
    for k in range(LEVELS):
        last = 8 * (2 * LEVELS + k)
        coef[last : last + 8, :] = ones / base
        if k + 1 < LEVELS:
            here = jnp.full((8, 128), mixing[k], F32)
            q = ones / (base + here)
            g = here * q
            coef[8 * k : 8 * k + 8, :] = g
            coef[8 * (LEVELS + k) : 8 * (LEVELS + k) + 8, :] = q
            base = ones + here - here * g


def spread_slots(rows, slots_by_column):
    for c, w in widths():
        rows[c * STEP : c * STEP + slots_by_column.shape[0], 0:w] = slots_by_column[:, c * 128 : c * 128 + w]


def pieces_of(rows, start, step):
    return [rows[pl.ds(u * 8 * step + start, 8, stride=step), :] for u in range(TILES // 8)]


MID = 25


ROW_SIZE = TILES * PITCH + 8
MID_SIZE = 32 * MID + 8


def copy_in(rows, base, values):
    for c, w in widths():
        rows[base + c * PITCH : base + c * PITCH + LEVELS, 0:w] = values(c, w)


def level_at(j, k, u):
    start = j * MID_SIZE + k * MID + u * 8
    return slice(start, start + 8)


def columns_at(j, k, u):
    return pl.ds(j * ROW_SIZE + u * 8 * PITCH + k, 8, stride=PITCH)


AHEAD = 4
BEHIND = 3


def solve_body(first, count, extra, warm, salt, n_rows, q_rows, coef, *rest):
    warm_out, salt_out, _, warm_in, salt_in, warm_done, salt_done, *rest = rest[extra:]
    warm_rows, salt_rows, warm_mid, salt_mid, came, left = rest

    def fetch(i):
        b = lax.rem(i, AHEAD)
        return [
            pltpu.make_async_copy(source.at[first + i], to.at[b], came.at[b, d])
            for d, (source, to) in enumerate(((warm, warm_in), (salt, salt_in)))
        ]

    def put(i):
        b = lax.rem(i, BEHIND)
        return [
            pltpu.make_async_copy(source.at[b], to.at[first + i], left.at[b, d])
            for d, (source, to) in enumerate(((warm_done, warm_out), (salt_done, salt_out)))
        ]

    for i in range(min(AHEAD, count)):
        for copy in fetch(i):
            copy.start()
    each = [(0, u) for u in range(TILES // 8)]

    def one(i, carry):
        b = lax.rem(i, AHEAD)
        n, t, s = {}, {}, {}
        for copy in fetch(i):
            copy.wait()
        copy_in(warm_rows, 0, lambda c, w: warm_in[b, :, c * 128 : c * 128 + w])
        copy_in(salt_rows, 0, lambda c, w: salt_in[b, :, c * 128 : c * 128 + w])

        @pl.when(i + AHEAD < count)
        def _():
            for copy in fetch(i + AHEAD):
                copy.start()

        for u, deep in enumerate(pieces_of(n_rows, first + i, STEP)):
            n[0, u] = deep
        for u, heat in enumerate(pieces_of(q_rows, first + i, STEP)):
            t[0, u] = jnp.where(n[0, u] > 0, heat, 0.0)
        for k in range(LEVELS):
            g = coefficient(coef, 0, k - 1) if k else None
            for j, u in each:
                rt = warm_rows[columns_at(j, k, u), :]
                rs = salt_rows[columns_at(j, k, u), :]
                if k == 0:
                    t[j, u] = rt + t[j, u]
                    s[j, u] = rs
                else:
                    e = jnp.where(n[j, u] > k, g, 0.0)
                    t[j, u] = rt + e * t[j, u]
                    s[j, u] = rs + e * s[j, u]
                warm_mid[level_at(j, k, u), :] = t[j, u]
                salt_mid[level_at(j, k, u), :] = s[j, u]
        for k in range(LEVELS - 1, -1, -1):
            last = coefficient(coef, 2, k)
            q = coefficient(coef, 1, k) if k + 1 < LEVELS else None
            g = coefficient(coef, 0, k) if k + 1 < LEVELS else None
            for j, u in each:
                a = jnp.where(n[j, u] > k, last, 1.0)
                if k + 1 < LEVELS:
                    more = n[j, u] > k + 1
                    a = jnp.where(more, q, a)
                    e = jnp.where(more, g, 0.0)
                    t[j, u] = a * warm_mid[level_at(j, k, u), :] + e * t[j, u]
                    s[j, u] = a * salt_mid[level_at(j, k, u), :] + e * s[j, u]
                else:
                    t[j, u] = a * t[j, u]
                    s[j, u] = a * s[j, u]
                warm_mid[level_at(j, k, u), :] = t[j, u]
                salt_mid[level_at(j, k, u), :] = s[j, u]

        @pl.when(i >= BEHIND)
        def _():
            for copy in put(i - BEHIND):
                copy.wait()

        o = lax.rem(i, BEHIND)
        for c, w in widths():
            for k in range(0, LEVELS, 8):
                h = min(8, LEVELS - k)
                part = pl.ds(k * MID + c, h, stride=MID)
                warm_done[o, k : k + h, c * 128 : c * 128 + w] = warm_mid[part, :][:, 0:w]
                salt_done[o, k : k + h, c * 128 : c * 128 + w] = salt_mid[part, :][:, 0:w]
        for copy in put(i):
            copy.start()
        return carry

    lax.fori_loop(0, count, one, 0)
    for i in range(max(0, count - BEHIND), count):
        for copy in put(i):
            copy.wait()


def mark_shape():
    return jax.ShapeDtypeStruct((8, 128), F32)


def coefficient_shape():
    return (3 * LEVELS * 8, 128)


def solve_columns(warm, salt, columns, first, count, before, after):
    extra = len(before) + len(after)
    blocks = lambda size: pltpu.VMEM((size, LEVELS, COLS), F32)
    return pl.pallas_call(
        functools.partial(solve_body, first, count, extra),
        out_shape=(jax.ShapeDtypeStruct(warm.shape, F32), jax.ShapeDtypeStruct(salt.shape, F32), mark_shape()),
        in_specs=[hbm(), hbm()] + [vm()] * 3 + [hbm()] * extra,
        out_specs=(hbm(), hbm(), hbm()),
        scratch_shapes=[blocks(AHEAD)] * 2
        + [blocks(BEHIND)] * 2
        + [pltpu.VMEM((ROW_SIZE, 128), F32)] * 2
        + [pltpu.VMEM((MID_SIZE, 128), F32)] * 2
        + [pltpu.SemaphoreType.DMA((AHEAD, 2)), pltpu.SemaphoreType.DMA((BEHIND, 2))],
        input_output_aliases={5: 0, 6: 1} if before else {},
        compiler_params=pltpu.CompilerParams(vmem_limit_bytes=49 * MIB),
        cost_estimate=pl.CostEstimate(flops=count * 2_000_000, bytes_accessed=count * 1_600_000, transcendentals=0),
        name="column_solve",
    )(warm, salt, *columns, *before, *after)


def lanes_of(x, index):
    return jnp.take_along_axis(x, index, axis=1, mode="promise_in_bounds")


def rim_of(tile):
    lane = lax.broadcasted_iota(jnp.int32, (8, 128), 1)
    one = lane & 63
    index = (one * SPAN_E + jnp.where(lane < 64, 0, SPAN_E - 1)) & 127
    low = high = along = None
    for c in range(TILES):
        now = tile(c)
        place = lane + 128 * c
        col = place - SPAN_E * divide(place, SPAN_E)
        rim = (col == 0) | (col == SPAN_E - 1)
        if c <= 14:
            low = now if c == 0 else [jnp.where(rim, v, p) for v, p in zip(now, low)]
        else:
            high = now if c == 15 else [jnp.where(rim, v, p) for v, p in zip(now, high)]
        if c == 0:
            first = now
        if c == TILES - 2:
            along = now
        if c == TILES - 1:
            along = [jnp.where(lane >= 124, p, v) for v, p in zip(now, along)]
    x = [jnp.where(one < 32, lanes_of(p, index), lanes_of(v, index)) for p, v in zip(low, high)]
    y = [jnp.where(lane < 64, p, pltpu.roll(v, 68, 1)) for p, v in zip(first, along)]
    return x, y


def tables_body(span_x, span_y, mixing, ids, depth, inflow, after, *rest):
    n_rows, q_rows, coef, pick, rim_x, rim_y, listed, padded = rest
    slots = depth.shape[0]
    n_rows[...] = jnp.zeros(n_rows.shape, jnp.int32)
    spread_slots(n_rows, depth)
    spread_slots(q_rows, inflow)
    fill_coefficients(mixing, coef)
    padded[...] = jnp.zeros((SLOT_ROWS, FLAT), F32)
    padded[0:slots, 0:COLS] = depth[...].astype(F32)
    rims = rim_of(lambda c: [padded[8 * g : 8 * g + 8, c * 128 : c * 128 + 128] for g in range(SLOT_ROWS // 8)])
    one = lax.broadcasted_iota(jnp.int32, (1, 128), 1) & 63
    for ref, parts, used in zip((rim_x, rim_y), rims, (SPAN_N, SPAN_E)):
        ref[...] = jnp.where(one < used, jnp.concatenate(parts, axis=0), 0.0)
    blocks_x = KX * span_x
    row = lax.broadcasted_iota(jnp.int32, (SLOT_ROWS, 128), 0)
    held = jnp.zeros((SLOT_ROWS, 128), jnp.int32)
    for s in range(slots):
        held = jnp.where(row == s, jnp.maximum(ids[s], 0), held)
    lane = lax.broadcasted_iota(jnp.int32, (8, 128), 1)
    line = jnp.full((8, 128), -1.0, F32)
    for s in range(slots):
        line = jnp.where(lane == s, ids[s].astype(F32), line)
    listed[...] = line
    up = divide(held, blocks_x)
    across = held - blocks_x * up
    band = up - KY * divide(up, KY)

    def spot(b, m, folds=False):
        o = divide(b, KX)
        c = b - KX * o
        return jnp.where(folds, span_x - 1 - o, o) * 32 + c * 8 + m

    spots = (
        spot(jnp.where(across == 0, blocks_x, across) - 1, band + 1),
        spot(jnp.where(across == blocks_x - 1, -1, across) + 1, band + 1),
        spot(across, band),
        spot(across, band + 2, up == KY * span_y - 1),
    )
    at = lax.broadcasted_iota(jnp.int32, (SLOT_ROWS, 128), 1)
    for d, where in enumerate(spots):
        for t in range(span_x * 32 // 128):
            pick[d * SLOT_ROWS : (d + 1) * SLOT_ROWS, t * 128 : t * 128 + 128] = jnp.where(
                at + t * 128 == where, 1.0, 0.0
            )


def column_tables(span_x, span_y, mixing, ids, depth, inflow, after):
    rows = (TILES * STEP + 8, 128)
    return pl.pallas_call(
        functools.partial(tables_body, span_x, span_y),
        out_shape=(
            jax.ShapeDtypeStruct(rows, jnp.int32),
            jax.ShapeDtypeStruct(rows, F32),
            jax.ShapeDtypeStruct(coefficient_shape(), F32),
        )
        + (jax.ShapeDtypeStruct((4 * SLOT_ROWS, span_x * 32), F32),)
        + (jax.ShapeDtypeStruct((SLOT_ROWS, 128), F32),) * 2
        + (jax.ShapeDtypeStruct((8, 128), F32),),
        in_specs=[sm(), sm(), vm(), vm(), hbm()],
        out_specs=(vm(),) * 7,
        scratch_shapes=[pltpu.VMEM((SLOT_ROWS, FLAT), F32)],
        compiler_params=pltpu.CompilerParams(vmem_limit_bytes=12 * MIB),
        cost_estimate=pl.CostEstimate(flops=5_000_000, bytes_accessed=3_000_000, transcendentals=0),
        name="column_tables",
    )(mixing, ids, depth, inflow, after)


def spread_lines(span_y, top, bottom, out):
    here = lax.axis_index("gy")
    for p in range(span_y):
        out[p] = jnp.where(here == p - 1, top, jnp.where(here == p + 1, bottom, 0.0))


def beside_lines(span_y, lines, folded):
    here = lax.axis_index("gy")
    ups = jnp.where(here == span_y - 1, folded, lines[jnp.minimum(here + 1, span_y - 1)])
    downs = jnp.where(here == 0, 0.0, lines[jnp.maximum(here - 1, 0)])
    return ups, downs


def edges_body(span_x, span_y, depth, lines, held, table, extended, _, rows):
    ups, downs = beside_lines(span_y, lines, 0.0)
    top = lax.axis_index("gy") == span_y - 1
    extended[...] = depth[...]
    extended[RY : RY + 4, :] = ups[0:4]
    extended[GY - 4 : GY, :] = downs[0:4]
    lane = lax.broadcasted_iota(jnp.int32, (8, GX), 1)
    pick = lax.broadcasted_iota(jnp.int32, (8, GX), 0)
    ext16 = extended[...].astype(jnp.bfloat16)

    def columns(wanted):
        hot = jnp.where(lane == wanted, 1.0, 0.0).astype(jnp.bfloat16)
        out = lax.dot_general(hot, ext16, (((1,), (1,)), ((), ())), preferred_element_type=F32)
        return jnp.concatenate([out, jnp.zeros((8, EDGE - GY), F32)], axis=1)

    sides = columns(jnp.where(pick < 3, pick * SPAN_E, jnp.where(pick < 6, (pick - 3) * SPAN_E + SPAN_E - 1, -1)))
    rows[...] = jnp.zeros((16, GX), F32)
    for m in range(KY + 1):
        rows[m + 1 : m + 2, :] = extended[m * SPAN_N : m * SPAN_N + 1, :]
        y = m * SPAN_N - 1 if m else GY - 1
        rows[8 + m : 9 + m, :] = extended[y : y + 1, :]
    turned = turn(jnp.concatenate([extended[RY - 1 - y : RY - y, :] for y in range(4)] * 2, axis=0))
    rows[KY + 1 : KY + 2, :] = jnp.where(top, turned[0:1], rows[KY + 1 : KY + 2, :])
    low = rows[0:8, :]
    high = rows[8:16, :]
    lane1 = lane[:, 0:128]
    for b in range(KX):
        a = pltpu.roll(low, (192 - b * SPAN_E) % GX, 1)
        z = pltpu.roll(high, (128 - b * SPAN_E) % GX, 1)
        both = jnp.where(lane >= 192, a, z)
        table[0, 8 * b : 8 * b + 8, 128:256] = both[:, 128:256]
        table[0, 8 * b : 8 * b + 8, 0:128] = jnp.zeros((8, 128), F32)
        table[0, 8 * b : 8 * b + 8, 256:384] = jnp.zeros((8, 128), F32)
    for m in range(KY):
        z = pltpu.roll(sides, (EDGE - m * SPAN_N) % EDGE, 1)[:, 0:128]
        a = pltpu.roll(sides, (EDGE + 64 - m * SPAN_N) % EDGE, 1)[:, 0:128]
        for b in range(KX):
            table[0, 8 * b + m + 1 : 8 * b + m + 2, 0:128] = jnp.where(
                lane1[0:1] >= 64, a[b : b + 1], z[3 + b : 4 + b]
            )
    table[0, 0:1, 256:384] = held[0:1, :]
    table[0, 8:12, 256:384] = turned[0:4, 0:128]
    table[0, 12:16, 256:384] = turned[0:4, 128:256]
    table[0, 24:32, :] = columns(jnp.where(pick < 4, pick, RX - 8 + pick))
    for d in range(1, span_x):
        table[d] = table[0]


def block_edges(span_x, span_y, depth, lines, held):
    return pl.pallas_call(
        functools.partial(edges_body, span_x, span_y),
        out_shape=(
            jax.ShapeDtypeStruct((span_x, 32, EDGE), F32),
            jax.ShapeDtypeStruct((GY, GX), F32),
            mark_shape(),
        ),
        in_specs=[vm()] * 3,
        out_specs=(vm(),) * 2 + (hbm(),),
        scratch_shapes=[pltpu.VMEM((16, GX), F32)],
        compiler_params=pltpu.CompilerParams(vmem_limit_bytes=12 * MIB),
        name="block_edges",
    )(depth, lines, held)


def ends_body(span_y, depth, region, out, wide):
    wide[...] = jnp.zeros(wide.shape, F32)
    wide[0:RX, 0:RY] = depth[...].astype(F32)
    region[...] = wide[...].T[0:GY, :]

    def lines(first):
        return jnp.concatenate([region[first : first + 4, :], jnp.zeros((4, GX), F32)], axis=0)

    spread_lines(span_y, lines(RY - 4), lines(0), out)


def region_ends(span_y, depth_t):
    return pl.pallas_call(
        functools.partial(ends_body, span_y),
        out_shape=(
            jax.ShapeDtypeStruct((GY, GX), F32),
            jax.ShapeDtypeStruct((span_y, 8, GX), F32),
        ),
        in_specs=[vm()],
        out_specs=(vm(),) * 2,
        scratch_shapes=[pltpu.VMEM((GX, EDGE), F32)],
        compiler_params=pltpu.CompilerParams(vmem_limit_bytes=12 * MIB),
        name="region_ends",
    )(depth_t)


ROWS = 40
HALF = 13


SLOT_STEP = 201


def shifted(x, by):
    rows = x.shape[0]
    lane = lax.broadcasted_iota(jnp.int32, x.shape, 1)
    near = pltpu.roll(x, -by % 128, 1)
    far = pltpu.roll(near, (rows - 1) if by > 0 else 1, 0)
    return jnp.where(lane < 128 - by if by > 0 else lane >= -by, near, far)


def flux_body(
    slots, group, warm, salt, n_rows, q_rows, coef, after, pieces, rim_x, rim_y,
    faces, found, rows, middle, totals, warm_in, salt_in, came,
):
    lane = lax.broadcasted_iota(jnp.int32, (1, FLAT), 1)
    col = lane - SPAN_E * divide(lane, SPAN_E)

    def fetch(step):
        b = lax.rem(step, 2) * group
        return [
            pltpu.make_async_copy(source.at[step * group + j], to.at[b + j], came.at[b + j, d])
            for j in range(group)
            for d, (source, to) in enumerate(((warm, warm_in), (salt, salt_in)))
        ]

    for step in range(min(2, slots // group)):
        for copy in fetch(step):
            copy.start()
    faces[...] = jnp.zeros(faces.shape, jnp.int32)

    def one(step, carry):
        b = lax.rem(step, 2) * group
        many = range(group)
        each = [(j, u) for j in many for u in range(TILES // 8)]
        place = lax.broadcasted_iota(jnp.int32, (TILES, 128), 0) * 128
        place = place + lax.broadcasted_iota(jnp.int32, (TILES, 128), 1)
        in_row = place - SPAN_E * divide(place, SPAN_E)
        n, x = {}, {}
        for copy in fetch(step):
            copy.wait()
        for j in many:
            copy_in(
                rows,
                j * ROW_SIZE,
                lambda c, w: salt_in[b + j, :, c * 128 : c * 128 + w] - RATIO * warm_in[b + j, :, c * 128 : c * 128 + w],
            )
            slot = step * group + j
            for u, deep in enumerate(pieces_of(n_rows, slot, STEP)):
                n[j, u] = deep
            for u, heat in enumerate(pieces_of(q_rows, slot, STEP)):
                x[j, u] = RATIO * heat
            deep = jnp.concatenate([n[j, u] for u in range(TILES // 8)], axis=0)
            for d, (by, inside) in enumerate(
                (
                    (1, in_row < SPAN_E - 1),
                    (-1, in_row > 0),
                    (SPAN_E, place < COLS - SPAN_E),
                    (-SPAN_E, place >= SPAN_E),
                )
            ):
                start = (8 * j + d) * MID
                faces[start : start + TILES, :] = jnp.where(inside, jnp.minimum(deep, shifted(deep, by)), 0)

        @pl.when(step + 2 < slots // group)
        def _():
            for copy in fetch(step + 2):
                copy.start()

        for k in range(LEVELS):
            g = coefficient(coef, 0, k - 1) if k else None
            for j, u in each:
                right = rows[columns_at(j, k, u), :]
                x[j, u] = right + g * x[j, u] if k else right - x[j, u]
                middle[j, k, u * 8 : u * 8 + 8, :] = x[j, u]
        for k in range(LEVELS - 1, -1, -1):
            last = coefficient(coef, 2, k)
            q = coefficient(coef, 1, k) if k + 1 < LEVELS else None
            g = coefficient(coef, 0, k) if k + 1 < LEVELS else None
            for j, u in each:
                if k + 1 < LEVELS:
                    more = n[j, u] > k + 1
                    a = jnp.where(more, q, last)
                    e = jnp.where(more, g, 0.0)
                    x[j, u] = a * middle[j, k, u * 8 : u * 8 + 8, :] + e * x[j, u]
                else:
                    x[j, u] = last * x[j, u]
                middle[j, k, u * 8 : u * 8 + 8, :] = x[j, u]
        zero = jnp.zeros((8, 128), F32)
        pressure = {at: zero for at in each}
        total = {at: zero for at in each}
        for k in range(LEVELS):
            for j, u in each:
                pressure[j, u] = pressure[j, u] + middle[j, k, u * 8 : u * 8 + 8, :]
                total[j, u] = total[j, u] + pressure[j, u]
                totals[level_at(j, k, u), :] = total[j, u]

        for j in many:
            slot = step * group + j

            def tile(c):
                now = [totals[pl.ds(j * MID_SIZE + 8 * g * MID + c, 8, stride=MID), :] for g in range(4)]
                level = faces[pl.ds(8 * j * MID + c, 8, stride=MID), :] - 1
                sums = zero
                for g in range(4):
                    one_of = jnp.take_along_axis(now[g], level & 7, axis=0, mode="promise_in_bounds")
                    sums = jnp.where((level >> 3) == g, one_of, sums)
                found[pl.ds(slot * SLOT_STEP + c * 8, 8), :] = sums
                return now

            for ref, parts in zip((rim_x, rim_y), rim_of(tile)):
                for g in range(4):
                    ref[slot, 8 * g : 8 * g + 8, :] = parts[g]
        return carry

    lax.fori_loop(0, slots // group, one, 0)

    def flat(d):
        return jnp.concatenate(
            [found[pl.ds(c * 8 + d, SLOT_ROWS, stride=SLOT_STEP), :] for c in range(TILES)], axis=1
        )

    east, west, north, south = (flat(d) for d in range(4))
    from_east = pltpu.roll(west, FLAT - 1, 1)
    from_west = pltpu.roll(east, 1, 1)
    net = -(east + west + north + south)
    net = net + jnp.where(col < SPAN_E - 1, from_east, 0.0)
    net = net + jnp.where(col > 0, from_west, 0.0)
    net = net + jnp.where(lane < COLS - SPAN_E, pltpu.roll(south, FLAT - SPAN_E, 1), 0.0)
    net = net + jnp.where(lane >= SPAN_E, pltpu.roll(north, SPAN_E, 1), 0.0)
    l = lax.broadcasted_iota(jnp.int32, (1, 128), 1)
    for t in range(26):
        halves = []
        for h in range(2):
            r = 2 * t + h
            if r in (0, SPAN_N + 1):
                continue
            start = (r - 1) * SPAN_E
            a = start // 128
            row = net[:, a * 128 : a * 128 + 128]
            if start % 128 + SPAN_E > 128:
                row = jnp.where(l >= start % 128, row, net[:, a * 128 + 128 : a * 128 + 256])
            row = pltpu.roll(row, (64 * h + 1 - start) % 128, 1)
            halves.append(jnp.where((l > 64 * h) & (l <= 64 * h + SPAN_E), row, 0.0))
        pieces[t * STEP : t * STEP + SLOT_ROWS, :] = halves[0] + halves[1] if len(halves) == 2 else halves[0]


def face_sums(warm, salt, columns, after):
    slots = warm.shape[0]
    group = 3 if slots % 3 == 0 else 1
    return pl.pallas_call(
        functools.partial(flux_body, slots, group),
        out_shape=(jax.ShapeDtypeStruct((26 * STEP + 6, 128), F32),)
        + (jax.ShapeDtypeStruct((slots, 32, 128), F32),) * 2,
        in_specs=[hbm(), hbm()] + [vm()] * 3 + [hbm()],
        out_specs=(vm(),) * 3,
        scratch_shapes=[
            pltpu.VMEM((8 * group * MID, 128), jnp.int32),
            pltpu.VMEM((SLOT_ROWS * SLOT_STEP, 128), F32),
            pltpu.VMEM((group * ROW_SIZE, 128), F32),
            pltpu.VMEM((group, LEVELS, TILES, 128), F32),
            pltpu.VMEM((group * MID_SIZE, 128), F32),
            pltpu.VMEM((2 * group, LEVELS, COLS), F32),
            pltpu.VMEM((2 * group, LEVELS, COLS), F32),
            pltpu.SemaphoreType.DMA((2 * group, 2)),
        ],
        compiler_params=pltpu.CompilerParams(vmem_limit_bytes=49 * MIB),
        cost_estimate=pl.CostEstimate(flops=40_000_000, bytes_accessed=15_000_000, transcendentals=0),
        name="face_sums",
    )(warm, salt, *columns, after)


def rows_body(span_x, cap, edges, after, rows):
    blocks_x = KX * span_x
    keys = jnp.concatenate([edges[d * 32 : d * 32 + 1, 256:384] for d in range(span_x)], axis=0).astype(jnp.int32)
    held = jnp.maximum(keys, 0)
    owner = jnp.where(keys >= 0, divide(held - blocks_x * divide(held, blocks_x), KX), -1)
    one_of = [jnp.where(owner == o, 1.0, 0.0) for o in range(span_x)]
    earlier = lax.broadcasted_iota(jnp.int32, (128, 128), 0) < lax.broadcasted_iota(jnp.int32, (128, 128), 1)
    counted = jnp.dot(
        jnp.concatenate(one_of, axis=0).astype(jnp.bfloat16),
        jnp.where(earlier, 1.0, 0.0).astype(jnp.bfloat16),
        preferred_element_type=F32,
    )
    at = lax.broadcasted_iota(jnp.int32, (span_x, 128), 0).astype(F32) * cap + 1.0
    for o in range(span_x):
        at = at + one_of[o] * counted[o * span_x : (o + 1) * span_x]
    here_x = lax.axis_index("gx")
    first = lax.axis_index("gy") * KY

    def beside(x):
        x = jnp.where(x < 0, x + blocks_x, x)
        return jnp.where(x >= blocks_x, x - blocks_x, x)

    base = here_x * KX
    over = (span_x - 1 - here_x) * KX
    wanted = [(first + p // KX) * blocks_x + base + p % KX for p in range(KX * KY)]
    wanted += [(first + p) * blocks_x + beside(base - 1) for p in range(KY)]
    wanted += [(first + p) * blocks_x + beside(base + KX) for p in range(KY)]
    wanted += [(first + KY - 1) * blocks_x + x for x in [over + g for g in range(KX)]]
    wanted += [(first + KY - 1) * blocks_x + beside(x) for x in (over - 1, over + KX)]
    lines = [jnp.sum(jnp.where(keys == w, at, 0.0), axis=0, keepdims=True) for w in wanted]
    lines += [jnp.zeros((1, 128), F32)] * (ROWS - len(lines))
    sums = jnp.sum(jnp.concatenate(lines, axis=0), axis=1, keepdims=True) - 1.0
    rows[...] = jnp.broadcast_to(sums, (ROWS, 128)).astype(jnp.int32)


def received_rows(span_x, cap, edges, after):
    return pl.pallas_call(
        functools.partial(rows_body, span_x, cap),
        out_shape=jax.ShapeDtypeStruct((ROWS, 128), jnp.int32),
        in_specs=[vm(), hbm()],
        out_specs=vm(),
        compiler_params=pltpu.CompilerParams(vmem_limit_bytes=12 * MIB),
        name="received_rows",
    )(edges, after)


def outgoing_body(
    span_x, cap, slots, ids, pick, edges, n_x, n_y, inside, rim_x, rim_y, out, _, pieces, q_x, q_y, source, counts
):
    blocks_x = KX * span_x
    for d in range(span_x):
        counts[d] = 0
    for d in range(span_x * cap):
        source[d] = 0
    for s in range(slots):
        held = jnp.maximum(ids[s], 0)
        owner = divide(held - blocks_x * divide(held, blocks_x), KX)
        rank = counts[owner]

        @pl.when(ids[s] >= 0)
        def _():
            source[owner * cap + jnp.minimum(rank, cap - 1)] = s
            counts[owner] = rank + 1

    near = jnp.dot(
        pick[...].astype(jnp.bfloat16), edges[:, 0:GX].astype(jnp.bfloat16), preferred_element_type=F32
    )
    l = lax.broadcasted_iota(jnp.int32, (1, 128), 1)
    w, e, so, no = (near[d * SLOT_ROWS : (d + 1) * SLOT_ROWS] for d in range(4))
    q_x[...] = jnp.zeros(q_x.shape, F32)
    q_y[...] = jnp.zeros(q_y.shape, F32)
    level = lax.broadcasted_iota(jnp.int32, (32, 128), 0).astype(F32) + 1.0
    for n, other, rim, q in (
        (n_x, jnp.where(l < 64, w[:, 0:128], e[:, 0:128]), rim_x, q_x),
        (n_y, jnp.where(l < 64, so[:, 128:256], no[:, 128:256]), rim_y, q_y),
    ):
        face = jnp.minimum(n[...], other)
        for s in range(slots):
            hit = jnp.where(face[s : s + 1] == level, rim[s], 0.0)
            q[s : s + 1, :] = jnp.sum(hit, axis=0, keepdims=True)

    groups = range(SLOT_ROWS // 8)
    lane = lax.broadcasted_iota(jnp.int32, (8, 128), 1)
    in_row = lane & 63
    odd = lane >> 6
    adds = jnp.where((in_row == 0) | (in_row == SPAN_E + 1), 1.0, 0.0)
    adds = jnp.where((in_row == 1) | (in_row == SPAN_E), -1.0, adds)
    zero = jnp.zeros((8, 128), F32)
    strips = [[[zero for _ in groups] for _ in range(2)] for _ in range(2)]
    for t in range(26):
        p, at = t // HALF, 4 * (t % HALF)
        i = 2 * t - 1 + odd
        index = jnp.clip(i, 0, SPAN_N - 1) + jnp.where(in_row >= 32, 64, 0)
        sign = jnp.where((i >= 0) & (i < SPAN_N), adds, 0.0)
        band = (in_row >= at) & (in_row < at + 4)
        for g in groups:
            rows8 = slice(8 * g, 8 * g + 8)
            v = inside[t * STEP + 8 * g : t * STEP + 8 * g + 8, :] + sign * lanes_of(q_x[rows8, :], index)
            core = (in_row >= 1) & (in_row <= SPAN_E)
            if t == 0:
                v = v + jnp.where(core & (odd == 0), pltpu.roll(q_y[rows8, :], 1, 1), 0.0)
                v = v - jnp.where(core & (odd == 1), pltpu.roll(q_y[rows8, :], 65, 1), 0.0)
            if t == 25:
                v = v - jnp.where(core & (odd == 0), pltpu.roll(q_y[rows8, :], 65, 1), 0.0)
                v = v + jnp.where(core & (odd == 1), pltpu.roll(q_y[rows8, :], 1, 1), 0.0)
            pieces[t * STEP + 8 * g : t * STEP + 8 * g + 8, :] = v
            strips[0][p][g] = jnp.where(band, pltpu.roll(v, at, 1), strips[0][p][g])
            strips[1][p][g] = jnp.where(band, pltpu.roll(v, (at - SPAN_E + 2) % 128, 1), strips[1][p][g])
    for side in range(2):
        for p in range(2):
            for g in groups:
                start = (26 + 2 * side + p) * STEP + 8 * g
                pieces[start : start + 8, :] = strips[side][p][g]
    pieces[30 * STEP : 32 * STEP + 8, :] = jnp.zeros((2 * STEP + 8, 128), F32)

    tile_row = lax.broadcasted_iota(jnp.int32, (8, 128), 0)
    corner = (in_row >= 52) & (in_row < 60)
    for d in range(span_x):
        for c in range(cap):
            other = span_x - 1 - d
            own = source[d * cap + c]
            left = source[(d - 1) % span_x * cap + c]
            right = source[(d + 1) % span_x * cap + c]
            fold = source[other * cap + c]
            fold_west = source[(other - 1) % span_x * cap + c]
            fold_east = source[(other + 1) % span_x * cap + c]

            def last(slot):
                return pieces[pl.ds(24 * STEP + slot, 8, stride=STEP), :]

            tail = jnp.where(tile_row < 2, last(own), jnp.where(tile_row < 4, last(right), last(left)))
            tail = jnp.where(tile_row >= 6, pltpu.roll(last(fold), 6, 0), tail)
            tail = jnp.where((tile_row == 3) & corner, pltpu.roll(last(fold_east), 8, 1), tail)
            tail = jnp.where((tile_row == 5) & corner, pltpu.roll(last(fold_west), 8, 1), tail)
            out[d * cap + c, 0:24, :] = pieces[pl.ds(own, 24, stride=STEP), :]
            out[d * cap + c, 24:32, :] = tail


def outgoing_blocks(span_x, cap, ids, pick, edges, rims, sums):
    slots = ids.shape[0]
    return pl.pallas_call(
        functools.partial(outgoing_body, span_x, cap, slots),
        out_shape=(jax.ShapeDtypeStruct((span_x * cap, 32, 128), F32), mark_shape()),
        in_specs=[sm()] + [vm()] * 7,
        out_specs=(vm(), hbm()),
        scratch_shapes=[pltpu.VMEM((32 * STEP + 8, 128), F32)]
        + [pltpu.VMEM((SLOT_ROWS, 128), F32)] * 2
        + [pltpu.SMEM((span_x * cap,), jnp.int32), pltpu.SMEM((span_x,), jnp.int32)],
        compiler_params=pltpu.CompilerParams(vmem_limit_bytes=12 * MIB),
        name="outgoing_blocks",
    )(ids, pick, edges, *rims, *sums)


def turn(x):
    lane = lax.broadcasted_iota(jnp.int32, (8, 128), 1)
    halves = [
        jnp.take_along_axis(x[:, h * 128 : h * 128 + 128], 127 - lane, axis=1, mode="promise_in_bounds")
        for h in (1, 0)
    ]
    return pltpu.roll(jnp.concatenate(halves, axis=1), (RX - GX) % GX, 1)


def region_body(span_y, rows, got, after, region, out, folded, tiles, sides):
    tiles[...] = jnp.zeros(tiles.shape, F32)
    sides[...] = jnp.zeros(sides.shape, F32)
    for p in range(KX * KY):
        r = rows[p, 0]
        block = got[pl.ds(pl.multiple_of(jnp.maximum(r, 0) * 32, 32), 32), :]
        block = jnp.where(r >= 0, block, 0.0)
        tiles[pl.ds((p % KX) * 8 + p // KX, 32, stride=STEP), :] = block
    for p in range(2 * KY):
        r = rows[KX * KY + p, 0]
        block = got[pl.ds(pl.multiple_of(jnp.maximum(r, 0) * 32 + 24, 8), 8), :]
        block = jnp.where(r >= 0, block, 0.0)
        sides[pl.ds((p // KY) * 8 + p % KY, 8, stride=17), :] = block
    at_fold = KX * KY + 2 * KY
    for g in range(KX + 2):
        r = rows[at_fold + g, 0]
        block = got[pl.ds(pl.multiple_of(jnp.maximum(r, 0) * 32 + 24, 8), 8), :]
        block = jnp.where(r >= 0, block, 0.0)
        if g < KX:
            for t in range(2):
                tiles[(24 + t) * STEP + g * 8 + 6 : (24 + t) * STEP + g * 8 + 7, :] = block[6 + t : 7 + t]
        elif g == KX:
            sides[5 * 17 + 6 : 5 * 17 + 7, :] = pltpu.roll(block, 120, 1)[5:6]
        else:
            sides[3 * 17 + 14 : 3 * 17 + 15, :] = pltpu.roll(block, 120, 1)[3:4]
    lane = lax.broadcasted_iota(jnp.int32, (8, 128), 1)
    sub = lax.broadcasted_iota(jnp.int32, (8, 128), 0)

    def assembled(r):
        t, base = r // 2, (r % 2) * 64
        v = [tiles[t * STEP + 8 * g : t * STEP + 8 * g + 8, :] for g in range(KX)]
        a = pltpu.roll(v[0], (-1 - base) % 128, 1)
        b = pltpu.roll(v[1], (59 - base) % 128, 1)
        c = pltpu.roll(v[2], (119 - base) % 128, 1)
        to = base + 4 * (t % HALF)
        p = t // HALF
        w = sides[(4 + p) * 17 : (4 + p) * 17 + 8, :]
        e = sides[(2 + p) * 17 + 8 : (2 + p) * 17 + 16, :]
        w = pltpu.roll(w, (125 - to) % 128, 1)
        e = pltpu.roll(e, (51 - to) % 128, 1)
        left = jnp.where(lane <= 60, a, 0.0)
        left = left + jnp.where((lane >= 59) & (lane <= 120), b, 0.0)
        left = left + jnp.where(lane >= 119, c, 0.0)
        left = left + jnp.where(lane == 0, w, 0.0)
        right = jnp.where(lane <= 52, c, 0.0)
        right = right + jnp.where(lane == 127, a, 0.0)
        right = right + jnp.where(lane >= 125, w, 0.0)
        right = right + jnp.where((lane >= 51) & (lane <= 54), e, 0.0)
        return left, right

    region[...] = jnp.zeros(region.shape, F32)
    below = assembled(0)
    above = assembled(SPAN_N + 1)
    over = [above]
    for r in range(1, SPAN_N + 1):
        parts = assembled(r)
        if r > SPAN_N - 3:
            over.insert(1, parts)
        for h in range(2):
            v = parts[h]
            if r == 1:
                v = v + jnp.where((sub >= 1) & (sub < KY), pltpu.roll(above[h], 1, 0), 0.0)
            if r == SPAN_N:
                v = v + jnp.where(sub < KY - 1, pltpu.roll(below[h], 7, 0), 0.0)
            region[pl.ds(h * GY + r - 1, KY, stride=SPAN_N), :] = v[0:KY]
    for h in range(2):
        region[h * GY + RY : h * GY + RY + 1, :] = above[h][KY - 1 : KY]
        region[h * GY + GY - 1 : h * GY + GY, :] = below[h][0:1]

    def lines(ys):
        cut = [
            jnp.concatenate([region[y : y + 1, :], region[GY + y : GY + y + 1, :]], axis=1) for y in ys
        ]
        return jnp.concatenate(cut + [jnp.zeros((8 - len(ys), GX), F32)], axis=0)

    spread_lines(span_y, lines([RY - 3, RY - 2, RY - 1, RY]), lines([GY - 1, 0, 1, 2]), out)
    over = [jnp.concatenate([part[6:7] for part in parts], axis=1) for parts in over]
    folded[...] = turn(jnp.concatenate(over + [jnp.zeros((4, GX), F32)], axis=0))


def region_sums(span_y, rows, got, after):
    return pl.pallas_call(
        functools.partial(region_body, span_y),
        out_shape=(
            jax.ShapeDtypeStruct((2 * GY, 128), F32),
            jax.ShapeDtypeStruct((span_y, 8, GX), F32),
            jax.ShapeDtypeStruct((8, GX), F32),
        ),
        in_specs=[sm(), vm(), hbm()],
        out_specs=(vm(),) * 3,
        scratch_shapes=[pltpu.VMEM((32 * STEP + 8, 128), F32), pltpu.VMEM((8 * 17, 128), F32)],
        compiler_params=pltpu.CompilerParams(vmem_limit_bytes=12 * MIB),
        name="region_sums",
    )(rows, got.reshape(-1, 128), after)


def south_of(x):
    return pltpu.roll(x, 1, 0)


def north_of(x):
    return pltpu.roll(x, GY - 1, 0)


def west_of(x):
    return pltpu.roll(x, 1, 1)


def east_of(x):
    return pltpu.roll(x, GX - 1, 1)


def weights_body(span_x, span_y, extended, edges, after, *out):
    ext = extended[...]
    here = lax.axis_index("gx")
    lane8 = lax.broadcasted_iota(jnp.int32, (8, GX), 1)
    row8 = lax.broadcasted_iota(jnp.int32, (8, GX), 0)
    put_west = jnp.where((row8 >= 4) & (lane8 == GX - 8 + row8), 1.0, 0.0).astype(jnp.bfloat16)
    put_east = jnp.where((row8 < 4) & (lane8 == RX + row8), 1.0, 0.0).astype(jnp.bfloat16)
    for other, put in ((here + span_x - 1, put_west), (here + 1, put_east)):
        cols = edges[pl.ds(pl.multiple_of(other % span_x * 32 + 24, 8), 8), :]
        ext = ext + lax.dot_general(
            cols[:, 0:GY].astype(jnp.bfloat16), put, (((0,), (0,)), ((), ())), preferred_element_type=F32
        )

    fold = []
    for step in (0, -1, 1):
        other = span_x - 1 - here + step + span_x
        part = edges[pl.ds(pl.multiple_of(lax.rem(other, span_x) * 32 + 8, 8), 8), 256:384]
        fold.append(jnp.concatenate([part[0:4], part[4:8]], axis=1))
    lane4 = lax.broadcasted_iota(jnp.int32, (4, GX), 1)
    beyond = jnp.where(lane4 < RX, fold[0], 0.0)
    beyond = jnp.where((lane4 >= RX) & (lane4 < RX + 4), pltpu.roll(fold[1], RX, 1), beyond)
    beyond = jnp.where(lane4 >= GX - 4, pltpu.roll(fold[2], GX - RX, 1), beyond)
    beyond = jnp.where(lax.axis_index("gy") == span_y - 1, beyond, 0.0)
    ext = ext + jnp.concatenate([jnp.zeros((RY, GX), F32), beyond, jnp.zeros((GY - RY - 4, GX), F32)], axis=0)

    to_east = jnp.minimum(ext, east_of(ext)) / LEVELS
    to_north = jnp.minimum(ext, north_of(ext)) / LEVELS
    to_west = west_of(to_east)
    to_south = south_of(to_north)
    diagonal = jnp.where(ext > 0, DAMPING, 1.0) + to_east + to_west + to_north + to_south
    inverse = 1.0 / diagonal
    for ref, value in zip(out, (to_east, to_west, to_north, to_south, diagonal, inverse)):
        ref[...] = value


def face_weights(span_x, span_y, extended, edges, after):
    return pl.pallas_call(
        functools.partial(weights_body, span_x, span_y),
        out_shape=(jax.ShapeDtypeStruct((GY, GX), F32),) * 6,
        in_specs=[vm()] * 2 + [hbm()],
        out_specs=(vm(),) * 6,
        compiler_params=pltpu.CompilerParams(vmem_limit_bytes=12 * MIB),
        name="face_weights",
    )(extended, edges, after)


def basis_body(span_y, region, lines, folded, east, west, north, south, diag_in, inv_in, basis, dots, mark):
    to_east, to_west, to_north, to_south = east[...], west[...], north[...], south[...]
    diagonal, inverse = diag_in[...], inv_in[...]
    ups, downs = beside_lines(span_y, lines, folded[...])
    partial = jnp.concatenate([region[0:GY, :], region[GY : 2 * GY, :]], axis=1)
    gap = lambda rows: jnp.zeros((rows, GX), F32)
    extra = jnp.concatenate(
        [downs[3:4], gap(RY - 2), ups[0:4], gap(GY - RY - 6), downs[0:3]], axis=0
    )
    zero = (partial + extra) * (HALINE / LEVELS) * inverse

    def smooth(x):
        return inverse * (
            to_east * east_of(x) + to_west * west_of(x) + to_north * north_of(x) + to_south * south_of(x)
        )

    vectors = [zero, smooth(zero)]
    vectors.append(2.0 * smooth(vectors[1]) - vectors[0])
    vectors.append(2.0 * smooth(vectors[2]) - vectors[1])
    lane = lax.broadcasted_iota(jnp.int32, (GY, GX), 1)
    row = lax.broadcasted_iota(jnp.int32, (GY, GX), 0)
    inside = (lane < RX) & (row < RY)
    clean = [jnp.where(inside, v, 0.0) for v in vectors]
    position = lax.broadcasted_iota(jnp.int32, (8, 128), 1)
    packed = jnp.zeros((8, 128), F32)
    number = 0
    for i in range(4):
        basis[i] = clean[i]
        scaled = clean[i] * diagonal
        for j in range(i, 4):
            prod = scaled * clean[j]
            part = jnp.sum(prod.reshape(GY // 8, 8, GX), axis=0)
            part = part[:, 0:128] + part[:, 128:256]
            packed = packed + jnp.where(position == number, jnp.sum(part, axis=1, keepdims=True), 0.0)
            number += 1
    for d in range(dots.shape[0]):
        dots[d] = packed


def krylov_basis(span_x, span_y, region, lines, folded, weights):
    return pl.pallas_call(
        functools.partial(basis_body, span_y),
        out_shape=(
            jax.ShapeDtypeStruct((4, GY, GX), F32),
            jax.ShapeDtypeStruct((span_x * span_y, 8, 128), F32),
            mark_shape(),
        ),
        in_specs=[vm()] * 9,
        out_specs=(vm(),) * 2 + (hbm(),),
        compiler_params=pltpu.CompilerParams(vmem_limit_bytes=12 * MIB),
        name="krylov_basis",
    )(region, lines, folded, *weights)


def combine_body(dots, basis, diagonal, after, height, misfit):
    sums = jnp.sum(dots[...], axis=0, keepdims=True)
    lane = lax.broadcasted_iota(jnp.int32, (1, 128), 1)
    g = {}
    number = 0
    for i in range(4):
        for j in range(i, 4):
            v = jnp.sum(jnp.where(lane == number, sums, 0.0), axis=1, keepdims=True)
            g[i, j] = g[j, i] = v
            number += 1

    def inner(a, b):
        out = jnp.zeros((1, 1), F32)
        for i in range(4):
            for j in range(4):
                if a[i] is not None and b[j] is not None:
                    out = out + a[i] * b[j] * g[i, j]
        return out

    def add(a, b):
        return a if b is None else b if a is None else a + b

    def image(a):
        out = list(a)
        for k in range(3):
            if a[k] is None:
                continue
            if k == 0:
                out[1] = add(out[1], -a[0])
            else:
                out[k + 1] = add(out[k + 1], -0.5 * a[k])
                out[k - 1] = add(out[k - 1], -0.5 * a[k])
        return out

    one = jnp.ones((1, 1), F32)
    res = [one, None, None, None]
    way = list(res)
    high = [None] * 4
    gamma = inner(res, res)
    for iteration in range(3):
        moved = image(way)
        size = gamma / inner(way, moved)
        high = [h if w is None else add(h, size * w) for h, w in zip(high, way)]
        res = [r if m is None else add(r, -size * m) for r, m in zip(res, moved)]
        if iteration < 2:
            after = inner(res, res)
            ratio = after / gamma
            way = [r if w is None else add(r, ratio * w) for r, w in zip(res, way)]
            gamma = after
    out = jnp.zeros((GY, GX), F32)
    left = jnp.zeros((GY, GX), F32)
    for k in range(4):
        v = basis[k]
        if high[k] is not None:
            out = out + high[k] * v
        left = left + res[k] * v
    gap = jnp.zeros((384 - GY, GX), F32)
    height[...] = jnp.concatenate([out, gap], axis=0).T[0:RX, 0:RY]
    misfit[...] = jnp.concatenate([left * diagonal[...], gap], axis=0).T[0:RX, 0:RY]


def combine(dots, basis, diagonal, after):
    return pl.pallas_call(
        combine_body,
        out_shape=(jax.ShapeDtypeStruct((RX, RY), F32),) * 2,
        in_specs=[vm()] * 3 + [hbm()],
        out_specs=(vm(),) * 2,
        compiler_params=pltpu.CompilerParams(vmem_limit_bytes=12 * MIB),
        name="combine",
    )(dots, basis, diagonal, after)


def across(lines):
    return lax.all_to_all(lines, "gy", split_axis=0, concat_axis=0, tiled=True)


def on_device(warm, salt, inflow, mixing, tiles, slot_depth, depth):
    span_x = lax.axis_size("gx")
    span_y = lax.axis_size("gy")
    slots = tiles.shape[0]
    cap = (KX * KY + span_x - 1) // span_x
    both = ("gx", "gy")
    bounds = [slots * i // 18 for i in (0, 13, 18)]

    def solve(part, before, after):
        first, end = bounds[part], bounds[part + 1]
        return solve_columns(warm, salt, columns, first, end - first, before, (after,))

    region_depth, lines = region_ends(span_y, depth.T)
    n_rows, q_rows, coef, pick, n_x, n_y, held = column_tables(
        span_x, span_y, mixing, tiles, slot_depth, inflow, region_depth
    )
    columns = (n_rows, q_rows, coef)
    table, extended, mark = block_edges(span_x, span_y, region_depth, across(lines), held)
    edges = lax.all_to_all(table, "gx", split_axis=0, concat_axis=0, tiled=True)
    sums = face_sums(warm, salt, columns, mark)
    flat_edges = edges.reshape(-1, EDGE)
    blocks, mark = outgoing_blocks(span_x, cap, tiles, pick, flat_edges, (n_x, n_y), sums)
    rows = received_rows(span_x, cap, flat_edges, mark)
    got = lax.all_to_all(blocks, "gx", split_axis=0, concat_axis=0, tiled=True)
    *solved, done = solve(0, (), mark)

    region, lines, folded = region_sums(span_y, rows, got, done)
    weights = face_weights(span_x, span_y, extended, flat_edges, region)
    basis, dots, mark = krylov_basis(span_x, span_y, region, across(lines), folded, weights)
    sums = lax.all_to_all(dots, both, split_axis=0, concat_axis=0, tiled=True)
    *solved, done = solve(1, solved, mark)
    height, misfit = combine(sums.reshape(-1, 128), basis, weights[4], done)
    return (solved[0], solved[1], height.T, misfit.T)


def solution(mesh):
    in_specs = (
        P(("gx", "gy"), None, None),
        P(("gx", "gy"), None, None),
        P(("gx", "gy"), None),
        P(),
        P(("gx", "gy")),
        P(("gx", "gy"), None),
        P("gy", "gx"),
    )
    out_specs = (
        P(("gx", "gy"), None, None),
        P(("gx", "gy"), None, None),
        P("gy", "gx"),
        P("gy", "gx"),
    )
    return jax.shard_map(on_device, mesh=mesh, in_specs=in_specs, out_specs=out_specs, check_vma=False)
```

```python
import functools
import numpy as np
import jax
import jax.numpy as jnp
from jax import lax
from jax.experimental import pallas as pl
from jax.experimental.pallas import tpu as pltpu
from jax.sharding import PartitionSpec as P

SPAN_E = 60
SPAN_N = 50
KX = 3
KY = 6
LEVELS = 30
HALINE = 0.8
THERMAL = 0.6
RATIO = THERMAL / HALINE
DAMPING = 0.05
COLS = SPAN_E * SPAN_N
TILES = 24
SLOT_ROWS = 24
STEP = 25
PITCH = 33
EDGE = 384
FLAT = TILES * 128
RY = KY * SPAN_N
RX = KX * SPAN_E
GY = 312
GX = 256
F32 = jnp.float32
MIB = 2**20


def widths():
    return [(c, min(128, COLS - 128 * c)) for c in range(TILES)]


def vm():
    return pl.BlockSpec(memory_space=pltpu.VMEM)


def sm():
    return pl.BlockSpec(memory_space=pltpu.SMEM)


def hbm():
    return pl.BlockSpec(memory_space=pltpu.HBM)


def divide(x, d):
    return (x * (2**20 // d + 1)) >> 20


def coefficient(coef, kind, k):
    return coef[8 * (kind * LEVELS + k) : 8 * (kind * LEVELS + k) + 8, :]


def fill_coefficients(mixing, coef):
    ones = jnp.ones((8, 128), F32)
    base = ones
    for k in range(LEVELS):
        last = 8 * (2 * LEVELS + k)
        coef[last : last + 8, :] = ones / base
        if k + 1 < LEVELS:
            here = jnp.full((8, 128), mixing[k], F32)
            q = ones / (base + here)
            g = here * q
            coef[8 * k : 8 * k + 8, :] = g
            coef[8 * (LEVELS + k) : 8 * (LEVELS + k) + 8, :] = q
            base = ones + here - here * g


def spread_slots(rows, slots_by_column):
    for c, w in widths():
        rows[c * STEP : c * STEP + slots_by_column.shape[0], 0:w] = slots_by_column[:, c * 128 : c * 128 + w]


def pieces_of(rows, start, step):
    return [rows[pl.ds(u * 8 * step + start, 8, stride=step), :] for u in range(TILES // 8)]


MID = 25


ROW_SIZE = TILES * PITCH + 8
MID_SIZE = 32 * MID + 8


def copy_in(rows, base, values):
    for c, w in widths():
        rows[base + c * PITCH : base + c * PITCH + LEVELS, 0:w] = values(c, w)


def level_at(j, k, u):
    start = j * MID_SIZE + k * MID + u * 8
    return slice(start, start + 8)


def columns_at(j, k, u):
    return pl.ds(j * ROW_SIZE + u * 8 * PITCH + k, 8, stride=PITCH)


AHEAD = 4
BEHIND = 3


def solve_body(first, count, extra, warm, salt, n_rows, q_rows, coef, *rest):
    warm_out, salt_out, _, warm_in, salt_in, warm_done, salt_done, *rest = rest[extra:]
    warm_rows, salt_rows, warm_mid, salt_mid, came, left = rest

    def fetch(i):
        b = lax.rem(i, AHEAD)
        return [
            pltpu.make_async_copy(source.at[first + i], to.at[b], came.at[b, d])
            for d, (source, to) in enumerate(((warm, warm_in), (salt, salt_in)))
        ]

    def put(i):
        b = lax.rem(i, BEHIND)
        return [
            pltpu.make_async_copy(source.at[b], to.at[first + i], left.at[b, d])
            for d, (source, to) in enumerate(((warm_done, warm_out), (salt_done, salt_out)))
        ]

    for i in range(min(AHEAD, count)):
        for copy in fetch(i):
            copy.start()
    each = [(0, u) for u in range(TILES // 8)]

    def one(i, carry):
        b = lax.rem(i, AHEAD)
        n, t, s = {}, {}, {}
        for copy in fetch(i):
            copy.wait()
        copy_in(warm_rows, 0, lambda c, w: warm_in[b, :, c * 128 : c * 128 + w])
        copy_in(salt_rows, 0, lambda c, w: salt_in[b, :, c * 128 : c * 128 + w])

        @pl.when(i + AHEAD < count)
        def _():
            for copy in fetch(i + AHEAD):
                copy.start()

        for u, deep in enumerate(pieces_of(n_rows, first + i, STEP)):
            n[0, u] = deep
        for u, heat in enumerate(pieces_of(q_rows, first + i, STEP)):
            t[0, u] = jnp.where(n[0, u] > 0, heat, 0.0)
        for k in range(LEVELS):
            g = coefficient(coef, 0, k - 1) if k else None
            for j, u in each:
                rt = warm_rows[columns_at(j, k, u), :]
                rs = salt_rows[columns_at(j, k, u), :]
                if k == 0:
                    t[j, u] = rt + t[j, u]
                    s[j, u] = rs
                else:
                    e = jnp.where(n[j, u] > k, g, 0.0)
                    t[j, u] = rt + e * t[j, u]
                    s[j, u] = rs + e * s[j, u]
                warm_mid[level_at(j, k, u), :] = t[j, u]
                salt_mid[level_at(j, k, u), :] = s[j, u]
        for k in range(LEVELS - 1, -1, -1):
            last = coefficient(coef, 2, k)
            q = coefficient(coef, 1, k) if k + 1 < LEVELS else None
            g = coefficient(coef, 0, k) if k + 1 < LEVELS else None
            for j, u in each:
                a = jnp.where(n[j, u] > k, last, 1.0)
                if k + 1 < LEVELS:
                    more = n[j, u] > k + 1
                    a = jnp.where(more, q, a)
                    e = jnp.where(more, g, 0.0)
                    t[j, u] = a * warm_mid[level_at(j, k, u), :] + e * t[j, u]
                    s[j, u] = a * salt_mid[level_at(j, k, u), :] + e * s[j, u]
                else:
                    t[j, u] = a * t[j, u]
                    s[j, u] = a * s[j, u]
                warm_mid[level_at(j, k, u), :] = t[j, u]
                salt_mid[level_at(j, k, u), :] = s[j, u]

        @pl.when(i >= BEHIND)
        def _():
            for copy in put(i - BEHIND):
                copy.wait()

        o = lax.rem(i, BEHIND)
        for c, w in widths():
            for k in range(0, LEVELS, 8):
                h = min(8, LEVELS - k)
                part = pl.ds(k * MID + c, h, stride=MID)
                warm_done[o, k : k + h, c * 128 : c * 128 + w] = warm_mid[part, :][:, 0:w]
                salt_done[o, k : k + h, c * 128 : c * 128 + w] = salt_mid[part, :][:, 0:w]
        for copy in put(i):
            copy.start()
        return carry

    lax.fori_loop(0, count, one, 0)
    for i in range(max(0, count - BEHIND), count):
        for copy in put(i):
            copy.wait()


def mark_shape():
    return jax.ShapeDtypeStruct((8, 128), F32)


def coefficient_shape():
    return (3 * LEVELS * 8, 128)


def solve_columns(warm, salt, columns, first, count, before, after):
    extra = len(before) + len(after)
    blocks = lambda size: pltpu.VMEM((size, LEVELS, COLS), F32)
    return pl.pallas_call(
        functools.partial(solve_body, first, count, extra),
        out_shape=(jax.ShapeDtypeStruct(warm.shape, F32), jax.ShapeDtypeStruct(salt.shape, F32), mark_shape()),
        in_specs=[hbm(), hbm()] + [vm()] * 3 + [hbm()] * extra,
        out_specs=(hbm(), hbm(), hbm()),
        scratch_shapes=[blocks(AHEAD)] * 2
        + [blocks(BEHIND)] * 2
        + [pltpu.VMEM((ROW_SIZE, 128), F32)] * 2
        + [pltpu.VMEM((MID_SIZE, 128), F32)] * 2
        + [pltpu.SemaphoreType.DMA((AHEAD, 2)), pltpu.SemaphoreType.DMA((BEHIND, 2))],
        input_output_aliases={5: 0, 6: 1} if before else {},
        compiler_params=pltpu.CompilerParams(vmem_limit_bytes=49 * MIB),
        cost_estimate=pl.CostEstimate(flops=count * 2_000_000, bytes_accessed=count * 1_600_000, transcendentals=0),
        name="column_solve",
    )(warm, salt, *columns, *before, *after)


def lanes_of(x, index):
    return jnp.take_along_axis(x, index, axis=1, mode="promise_in_bounds")


def rim_of(tile):
    lane = lax.broadcasted_iota(jnp.int32, (8, 128), 1)
    one = lane & 63
    index = (one * SPAN_E + jnp.where(lane < 64, 0, SPAN_E - 1)) & 127
    low = high = along = None
    for c in range(TILES):
        now = tile(c)
        place = lane + 128 * c
        col = place - SPAN_E * divide(place, SPAN_E)
        rim = (col == 0) | (col == SPAN_E - 1)
        if c <= 14:
            low = now if c == 0 else [jnp.where(rim, v, p) for v, p in zip(now, low)]
        else:
            high = now if c == 15 else [jnp.where(rim, v, p) for v, p in zip(now, high)]
        if c == 0:
            first = now
        if c == TILES - 2:
            along = now
        if c == TILES - 1:
            along = [jnp.where(lane >= 124, p, v) for v, p in zip(now, along)]
    x = [jnp.where(one < 32, lanes_of(p, index), lanes_of(v, index)) for p, v in zip(low, high)]
    y = [jnp.where(lane < 64, p, pltpu.roll(v, 68, 1)) for p, v in zip(first, along)]
    return x, y


def tables_body(span_x, span_y, mixing, ids, depth, inflow, after, *rest):
    n_rows, q_rows, coef, pick, rim_x, rim_y, listed, padded = rest
    slots = depth.shape[0]
    n_rows[...] = jnp.zeros(n_rows.shape, jnp.int32)
    spread_slots(n_rows, depth)
    spread_slots(q_rows, inflow)
    fill_coefficients(mixing, coef)
    padded[...] = jnp.zeros((SLOT_ROWS, FLAT), F32)
    padded[0:slots, 0:COLS] = depth[...].astype(F32)
    rims = rim_of(lambda c: [padded[8 * g : 8 * g + 8, c * 128 : c * 128 + 128] for g in range(SLOT_ROWS // 8)])
    one = lax.broadcasted_iota(jnp.int32, (1, 128), 1) & 63
    for ref, parts, used in zip((rim_x, rim_y), rims, (SPAN_N, SPAN_E)):
        ref[...] = jnp.where(one < used, jnp.concatenate(parts, axis=0), 0.0)
    blocks_x = KX * span_x
    row = lax.broadcasted_iota(jnp.int32, (SLOT_ROWS, 128), 0)
    held = jnp.zeros((SLOT_ROWS, 128), jnp.int32)
    for s in range(slots):
        held = jnp.where(row == s, jnp.maximum(ids[s], 0), held)
    lane = lax.broadcasted_iota(jnp.int32, (8, 128), 1)
    line = jnp.full((8, 128), -1.0, F32)
    for s in range(slots):
        line = jnp.where(lane == s, ids[s].astype(F32), line)
    listed[...] = line
    up = divide(held, blocks_x)
    across = held - blocks_x * up
    band = up - KY * divide(up, KY)

    def spot(b, m, folds=False):
        o = divide(b, KX)
        c = b - KX * o
        return jnp.where(folds, span_x - 1 - o, o) * 32 + c * 8 + m

    spots = (
        spot(jnp.where(across == 0, blocks_x, across) - 1, band + 1),
        spot(jnp.where(across == blocks_x - 1, -1, across) + 1, band + 1),
        spot(across, band),
        spot(across, band + 2, up == KY * span_y - 1),
    )
    at = lax.broadcasted_iota(jnp.int32, (SLOT_ROWS, 128), 1)
    for d, where in enumerate(spots):
        for t in range(span_x * 32 // 128):
            pick[d * SLOT_ROWS : (d + 1) * SLOT_ROWS, t * 128 : t * 128 + 128] = jnp.where(
                at + t * 128 == where, 1.0, 0.0
            )


def column_tables(span_x, span_y, mixing, ids, depth, inflow, after):
    rows = (TILES * STEP + 8, 128)
    return pl.pallas_call(
        functools.partial(tables_body, span_x, span_y),
        out_shape=(
            jax.ShapeDtypeStruct(rows, jnp.int32),
            jax.ShapeDtypeStruct(rows, F32),
            jax.ShapeDtypeStruct(coefficient_shape(), F32),
        )
        + (jax.ShapeDtypeStruct((4 * SLOT_ROWS, span_x * 32), F32),)
        + (jax.ShapeDtypeStruct((SLOT_ROWS, 128), F32),) * 2
        + (jax.ShapeDtypeStruct((8, 128), F32),),
        in_specs=[sm(), sm(), vm(), vm(), hbm()],
        out_specs=(vm(),) * 7,
        scratch_shapes=[pltpu.VMEM((SLOT_ROWS, FLAT), F32)],
        compiler_params=pltpu.CompilerParams(vmem_limit_bytes=12 * MIB),
        cost_estimate=pl.CostEstimate(flops=5_000_000, bytes_accessed=3_000_000, transcendentals=0),
        name="column_tables",
    )(mixing, ids, depth, inflow, after)


def spread_lines(span_y, top, bottom, out):
    here = lax.axis_index("gy")
    for p in range(span_y):
        out[p] = jnp.where(here == p - 1, top, jnp.where(here == p + 1, bottom, 0.0))


def beside_lines(span_y, lines, folded):
    here = lax.axis_index("gy")
    ups = jnp.where(here == span_y - 1, folded, lines[jnp.minimum(here + 1, span_y - 1)])
    downs = jnp.where(here == 0, 0.0, lines[jnp.maximum(here - 1, 0)])
    return ups, downs


def edges_body(span_x, span_y, depth, lines, held, out, extended, _, rows, table, sent):
    ups, downs = beside_lines(span_y, lines, 0.0)
    top = lax.axis_index("gy") == span_y - 1
    extended[...] = depth[...]
    extended[RY : RY + 4, :] = ups[0:4]
    extended[GY - 4 : GY, :] = downs[0:4]
    lane = lax.broadcasted_iota(jnp.int32, (8, GX), 1)
    pick = lax.broadcasted_iota(jnp.int32, (8, GX), 0)
    ext16 = extended[...].astype(jnp.bfloat16)

    def columns(wanted):
        hot = jnp.where(lane == wanted, 1.0, 0.0).astype(jnp.bfloat16)
        out = lax.dot_general(hot, ext16, (((1,), (1,)), ((), ())), preferred_element_type=F32)
        return jnp.concatenate([out, jnp.zeros((8, EDGE - GY), F32)], axis=1)

    sides = columns(jnp.where(pick < 3, pick * SPAN_E, jnp.where(pick < 6, (pick - 3) * SPAN_E + SPAN_E - 1, -1)))
    rows[...] = jnp.zeros((16, GX), F32)
    for m in range(KY + 1):
        rows[m + 1 : m + 2, :] = extended[m * SPAN_N : m * SPAN_N + 1, :]
        y = m * SPAN_N - 1 if m else GY - 1
        rows[8 + m : 9 + m, :] = extended[y : y + 1, :]
    turned = turn(jnp.concatenate([extended[RY - 1 - y : RY - y, :] for y in range(4)] * 2, axis=0))
    rows[KY + 1 : KY + 2, :] = jnp.where(top, turned[0:1], rows[KY + 1 : KY + 2, :])
    low = rows[0:8, :]
    high = rows[8:16, :]
    lane1 = lane[:, 0:128]
    for b in range(KX):
        a = pltpu.roll(low, (192 - b * SPAN_E) % GX, 1)
        z = pltpu.roll(high, (128 - b * SPAN_E) % GX, 1)
        both = jnp.where(lane >= 192, a, z)
        table[8 * b : 8 * b + 8, 128:256] = both[:, 128:256]
        table[8 * b : 8 * b + 8, 0:128] = jnp.zeros((8, 128), F32)
        table[8 * b : 8 * b + 8, 256:384] = jnp.zeros((8, 128), F32)
    for m in range(KY):
        z = pltpu.roll(sides, (EDGE - m * SPAN_N) % EDGE, 1)[:, 0:128]
        a = pltpu.roll(sides, (EDGE + 64 - m * SPAN_N) % EDGE, 1)[:, 0:128]
        for b in range(KX):
            table[8 * b + m + 1 : 8 * b + m + 2, 0:128] = jnp.where(
                lane1[0:1] >= 64, a[b : b + 1], z[3 + b : 4 + b]
            )
    table[0:1, 256:384] = held[0:1, :]
    table[8:12, 256:384] = turned[0:4, 0:128]
    table[12:16, 256:384] = turned[0:4, 128:256]
    table[24:32, :] = columns(jnp.where(pick < 4, pick, RX - 8 + pick))
    copies = [pltpu.make_async_copy(table, out.at[d], sent.at[d]) for d in range(span_x)]
    for copy in copies:
        copy.start()
    for copy in copies:
        copy.wait()


def block_edges(span_x, span_y, depth, lines, held):
    return pl.pallas_call(
        functools.partial(edges_body, span_x, span_y),
        out_shape=(
            jax.ShapeDtypeStruct((span_x, 32, EDGE), F32),
            jax.ShapeDtypeStruct((GY, GX), F32),
            mark_shape(),
        ),
        in_specs=[vm()] * 3,
        out_specs=(hbm(), vm(), hbm()),
        scratch_shapes=[
            pltpu.VMEM((16, GX), F32),
            pltpu.VMEM((32, EDGE), F32),
            pltpu.SemaphoreType.DMA((span_x,)),
        ],
        compiler_params=pltpu.CompilerParams(vmem_limit_bytes=12 * MIB),
        name="block_edges",
    )(depth, lines, held)


def ends_body(span_y, depth, region, out, wide):
    wide[...] = jnp.zeros(wide.shape, F32)
    wide[0:RX, 0:RY] = depth[...].astype(F32)
    region[...] = wide[...].T[0:GY, :]

    def lines(first):
        return jnp.concatenate([region[first : first + 4, :], jnp.zeros((4, GX), F32)], axis=0)

    spread_lines(span_y, lines(RY - 4), lines(0), out)


def region_ends(span_y, depth_t):
    return pl.pallas_call(
        functools.partial(ends_body, span_y),
        out_shape=(
            jax.ShapeDtypeStruct((GY, GX), F32),
            jax.ShapeDtypeStruct((span_y, 8, GX), F32),
        ),
        in_specs=[vm()],
        out_specs=(vm(),) * 2,
        scratch_shapes=[pltpu.VMEM((GX, EDGE), F32)],
        compiler_params=pltpu.CompilerParams(vmem_limit_bytes=12 * MIB),
        name="region_ends",
    )(depth_t)


ROWS = 40
HALF = 13


SLOT_STEP = 201


def shifted(x, by):
    rows = x.shape[0]
    lane = lax.broadcasted_iota(jnp.int32, x.shape, 1)
    near = pltpu.roll(x, -by % 128, 1)
    far = pltpu.roll(near, (rows - 1) if by > 0 else 1, 0)
    return jnp.where(lane < 128 - by if by > 0 else lane >= -by, near, far)


def flux_body(
    slots, group, warm, salt, n_rows, q_rows, coef, after, pieces, rim_x, rim_y,
    faces, found, rows, middle, totals, warm_in, salt_in, came,
):
    lane = lax.broadcasted_iota(jnp.int32, (1, FLAT), 1)
    col = lane - SPAN_E * divide(lane, SPAN_E)

    def fetch(step):
        b = lax.rem(step, 2) * group
        return [
            pltpu.make_async_copy(source.at[step * group + j], to.at[b + j], came.at[b + j, d])
            for j in range(group)
            for d, (source, to) in enumerate(((warm, warm_in), (salt, salt_in)))
        ]

    for step in range(min(2, slots // group)):
        for copy in fetch(step):
            copy.start()
    faces[...] = jnp.zeros(faces.shape, jnp.int32)

    def one(step, carry):
        b = lax.rem(step, 2) * group
        many = range(group)
        each = [(j, u) for j in many for u in range(TILES // 8)]
        place = lax.broadcasted_iota(jnp.int32, (TILES, 128), 0) * 128
        place = place + lax.broadcasted_iota(jnp.int32, (TILES, 128), 1)
        in_row = place - SPAN_E * divide(place, SPAN_E)
        n, x = {}, {}
        for copy in fetch(step):
            copy.wait()
        for j in many:
            copy_in(
                rows,
                j * ROW_SIZE,
                lambda c, w: salt_in[b + j, :, c * 128 : c * 128 + w] - RATIO * warm_in[b + j, :, c * 128 : c * 128 + w],
            )
            slot = step * group + j
            for u, deep in enumerate(pieces_of(n_rows, slot, STEP)):
                n[j, u] = deep
            for u, heat in enumerate(pieces_of(q_rows, slot, STEP)):
                x[j, u] = RATIO * heat
            deep = jnp.concatenate([n[j, u] for u in range(TILES // 8)], axis=0)
            for d, (by, inside) in enumerate(
                (
                    (1, in_row < SPAN_E - 1),
                    (-1, in_row > 0),
                    (SPAN_E, place < COLS - SPAN_E),
                    (-SPAN_E, place >= SPAN_E),
                )
            ):
                start = (8 * j + d) * MID
                faces[start : start + TILES, :] = jnp.where(inside, jnp.minimum(deep, shifted(deep, by)), 0)

        @pl.when(step + 2 < slots // group)
        def _():
            for copy in fetch(step + 2):
                copy.start()

        for k in range(LEVELS):
            g = coefficient(coef, 0, k - 1) if k else None
            for j, u in each:
                right = rows[columns_at(j, k, u), :]
                x[j, u] = right + g * x[j, u] if k else right - x[j, u]
                middle[j, k, u * 8 : u * 8 + 8, :] = x[j, u]
        for k in range(LEVELS - 1, -1, -1):
            last = coefficient(coef, 2, k)
            q = coefficient(coef, 1, k) if k + 1 < LEVELS else None
            g = coefficient(coef, 0, k) if k + 1 < LEVELS else None
            for j, u in each:
                if k + 1 < LEVELS:
                    more = n[j, u] > k + 1
                    a = jnp.where(more, q, last)
                    e = jnp.where(more, g, 0.0)
                    x[j, u] = a * middle[j, k, u * 8 : u * 8 + 8, :] + e * x[j, u]
                else:
                    x[j, u] = last * x[j, u]
                middle[j, k, u * 8 : u * 8 + 8, :] = x[j, u]
        zero = jnp.zeros((8, 128), F32)
        pressure = {at: zero for at in each}
        total = {at: zero for at in each}
        for k in range(LEVELS):
            for j, u in each:
                pressure[j, u] = pressure[j, u] + middle[j, k, u * 8 : u * 8 + 8, :]
                total[j, u] = total[j, u] + pressure[j, u]
                totals[level_at(j, k, u), :] = total[j, u]

        for j in many:
            slot = step * group + j

            def tile(c):
                now = [totals[pl.ds(j * MID_SIZE + 8 * g * MID + c, 8, stride=MID), :] for g in range(4)]
                level = faces[pl.ds(8 * j * MID + c, 8, stride=MID), :] - 1
                sums = zero
                for g in range(4):
                    one_of = jnp.take_along_axis(now[g], level & 7, axis=0, mode="promise_in_bounds")
                    sums = jnp.where((level >> 3) == g, one_of, sums)
                found[pl.ds(slot * SLOT_STEP + c * 8, 8), :] = sums
                return now

            for ref, parts in zip((rim_x, rim_y), rim_of(tile)):
                for g in range(4):
                    ref[slot, 8 * g : 8 * g + 8, :] = parts[g]
        return carry

    lax.fori_loop(0, slots // group, one, 0)

    def flat(d):
        return jnp.concatenate(
            [found[pl.ds(c * 8 + d, SLOT_ROWS, stride=SLOT_STEP), :] for c in range(TILES)], axis=1
        )

    east, west, north, south = (flat(d) for d in range(4))
    from_east = pltpu.roll(west, FLAT - 1, 1)
    from_west = pltpu.roll(east, 1, 1)
    net = -(east + west + north + south)
    net = net + jnp.where(col < SPAN_E - 1, from_east, 0.0)
    net = net + jnp.where(col > 0, from_west, 0.0)
    net = net + jnp.where(lane < COLS - SPAN_E, pltpu.roll(south, FLAT - SPAN_E, 1), 0.0)
    net = net + jnp.where(lane >= SPAN_E, pltpu.roll(north, SPAN_E, 1), 0.0)
    l = lax.broadcasted_iota(jnp.int32, (1, 128), 1)
    for t in range(26):
        halves = []
        for h in range(2):
            r = 2 * t + h
            if r in (0, SPAN_N + 1):
                continue
            start = (r - 1) * SPAN_E
            a = start // 128
            row = net[:, a * 128 : a * 128 + 128]
            if start % 128 + SPAN_E > 128:
                row = jnp.where(l >= start % 128, row, net[:, a * 128 + 128 : a * 128 + 256])
            row = pltpu.roll(row, (64 * h + 1 - start) % 128, 1)
            halves.append(jnp.where((l > 64 * h) & (l <= 64 * h + SPAN_E), row, 0.0))
        pieces[t * STEP : t * STEP + SLOT_ROWS, :] = halves[0] + halves[1] if len(halves) == 2 else halves[0]


def face_sums(warm, salt, columns, after):
    slots = warm.shape[0]
    group = 3 if slots % 3 == 0 else 1
    return pl.pallas_call(
        functools.partial(flux_body, slots, group),
        out_shape=(jax.ShapeDtypeStruct((26 * STEP + 6, 128), F32),)
        + (jax.ShapeDtypeStruct((slots, 32, 128), F32),) * 2,
        in_specs=[hbm(), hbm()] + [vm()] * 3 + [hbm()],
        out_specs=(vm(),) * 3,
        scratch_shapes=[
            pltpu.VMEM((8 * group * MID, 128), jnp.int32),
            pltpu.VMEM((SLOT_ROWS * SLOT_STEP, 128), F32),
            pltpu.VMEM((group * ROW_SIZE, 128), F32),
            pltpu.VMEM((group, LEVELS, TILES, 128), F32),
            pltpu.VMEM((group * MID_SIZE, 128), F32),
            pltpu.VMEM((2 * group, LEVELS, COLS), F32),
            pltpu.VMEM((2 * group, LEVELS, COLS), F32),
            pltpu.SemaphoreType.DMA((2 * group, 2)),
        ],
        compiler_params=pltpu.CompilerParams(vmem_limit_bytes=49 * MIB),
        cost_estimate=pl.CostEstimate(flops=40_000_000, bytes_accessed=15_000_000, transcendentals=0),
        name="face_sums",
    )(warm, salt, *columns, after)


def received_rows(span_x, cap, edges):
    blocks_x = KX * span_x
    keys = jnp.concatenate([edges[d * 32 : d * 32 + 1, 256:384] for d in range(span_x)], axis=0).astype(jnp.int32)
    held = jnp.maximum(keys, 0)
    owner = jnp.where(keys >= 0, divide(held - blocks_x * divide(held, blocks_x), KX), -1)
    one_of = [jnp.where(owner == o, 1.0, 0.0) for o in range(span_x)]
    earlier = lax.broadcasted_iota(jnp.int32, (128, 128), 0) < lax.broadcasted_iota(jnp.int32, (128, 128), 1)
    counted = jnp.dot(
        jnp.concatenate(one_of, axis=0).astype(jnp.bfloat16),
        jnp.where(earlier, 1.0, 0.0).astype(jnp.bfloat16),
        preferred_element_type=F32,
    )
    at = lax.broadcasted_iota(jnp.int32, (span_x, 128), 0).astype(F32) * cap + 1.0
    for o in range(span_x):
        at = at + one_of[o] * counted[o * span_x : (o + 1) * span_x]
    here_x = lax.axis_index("gx")
    first = lax.axis_index("gy") * KY

    def beside(x):
        x = jnp.where(x < 0, x + blocks_x, x)
        return jnp.where(x >= blocks_x, x - blocks_x, x)

    base = here_x * KX
    over = (span_x - 1 - here_x) * KX
    wanted = [(first + p // KX) * blocks_x + base + p % KX for p in range(KX * KY)]
    wanted += [(first + p) * blocks_x + beside(base - 1) for p in range(KY)]
    wanted += [(first + p) * blocks_x + beside(base + KX) for p in range(KY)]
    wanted += [(first + KY - 1) * blocks_x + x for x in [over + g for g in range(KX)]]
    wanted += [(first + KY - 1) * blocks_x + beside(x) for x in (over - 1, over + KX)]
    lines = [jnp.sum(jnp.where(keys == w, at, 0.0), axis=0, keepdims=True) for w in wanted]
    lines += [jnp.zeros((1, 128), F32)] * (ROWS - len(lines))
    sums = jnp.sum(jnp.concatenate(lines, axis=0), axis=1, keepdims=True) - 1.0
    return jnp.broadcast_to(sums, (ROWS, 128)).astype(jnp.int32)


def outgoing_body(
    span_x, cap, slots, ids, pick, edges, n_x, n_y, inside, rim_x, rim_y, out, rows, _, pieces, q_x, q_y, source, counts, ready, sent
):
    blocks_x = KX * span_x
    for d in range(span_x + 1):
        counts[d] = 0
    for d in range(span_x * cap):
        source[d] = 0
    for s in range(slots):
        held = jnp.maximum(ids[s], 0)
        owner = divide(held - blocks_x * divide(held, blocks_x), KX)
        owner = jnp.where(ids[s] >= 0, owner, span_x)
        rank = counts[owner]
        source[owner * cap + jnp.minimum(rank, cap - 1)] = s
        counts[owner] = rank + 1

    rows[...] = received_rows(span_x, cap, edges)
    near = jnp.dot(
        pick[...].astype(jnp.bfloat16), edges[:, 0:GX].astype(jnp.bfloat16), preferred_element_type=F32
    )
    l = lax.broadcasted_iota(jnp.int32, (1, 128), 1)
    w, e, so, no = (near[d * SLOT_ROWS : (d + 1) * SLOT_ROWS] for d in range(4))
    q_x[...] = jnp.zeros(q_x.shape, F32)
    q_y[...] = jnp.zeros(q_y.shape, F32)
    level = lax.broadcasted_iota(jnp.int32, (32, 128), 0).astype(F32) + 1.0
    for n, other, rim, q in (
        (n_x, jnp.where(l < 64, w[:, 0:128], e[:, 0:128]), rim_x, q_x),
        (n_y, jnp.where(l < 64, so[:, 128:256], no[:, 128:256]), rim_y, q_y),
    ):
        face = jnp.minimum(n[...], other)
        for s in range(slots):
            hit = jnp.where(face[s : s + 1] == level, rim[s], 0.0)
            q[s : s + 1, :] = jnp.sum(hit, axis=0, keepdims=True)

    groups = range(SLOT_ROWS // 8)
    lane = lax.broadcasted_iota(jnp.int32, (8, 128), 1)
    in_row = lane & 63
    odd = lane >> 6
    adds = jnp.where((in_row == 0) | (in_row == SPAN_E + 1), 1.0, 0.0)
    adds = jnp.where((in_row == 1) | (in_row == SPAN_E), -1.0, adds)
    zero = jnp.zeros((8, 128), F32)
    strips = [[[zero for _ in groups] for _ in range(2)] for _ in range(2)]
    for t in range(26):
        p, at = t // HALF, 4 * (t % HALF)
        i = 2 * t - 1 + odd
        index = jnp.clip(i, 0, SPAN_N - 1) + jnp.where(in_row >= 32, 64, 0)
        sign = jnp.where((i >= 0) & (i < SPAN_N), adds, 0.0)
        band = (in_row >= at) & (in_row < at + 4)
        for g in groups:
            rows8 = slice(8 * g, 8 * g + 8)
            v = inside[t * STEP + 8 * g : t * STEP + 8 * g + 8, :] + sign * lanes_of(q_x[rows8, :], index)
            core = (in_row >= 1) & (in_row <= SPAN_E)
            if t == 0:
                v = v + jnp.where(core & (odd == 0), pltpu.roll(q_y[rows8, :], 1, 1), 0.0)
                v = v - jnp.where(core & (odd == 1), pltpu.roll(q_y[rows8, :], 65, 1), 0.0)
            if t == 25:
                v = v - jnp.where(core & (odd == 0), pltpu.roll(q_y[rows8, :], 65, 1), 0.0)
                v = v + jnp.where(core & (odd == 1), pltpu.roll(q_y[rows8, :], 1, 1), 0.0)
            pieces[t * STEP + 8 * g : t * STEP + 8 * g + 8, :] = v
            strips[0][p][g] = jnp.where(band, pltpu.roll(v, at, 1), strips[0][p][g])
            strips[1][p][g] = jnp.where(band, pltpu.roll(v, (at - SPAN_E + 2) % 128, 1), strips[1][p][g])
    for side in range(2):
        for p in range(2):
            for g in groups:
                start = (26 + 2 * side + p) * STEP + 8 * g
                pieces[start : start + 8, :] = strips[side][p][g]
    pieces[30 * STEP : 32 * STEP + 8, :] = jnp.zeros((2 * STEP + 8, 128), F32)

    def put(r):
        return pltpu.make_async_copy(ready.at[r], out.at[r], sent.at[r])

    tile_row = lax.broadcasted_iota(jnp.int32, (8, 128), 0)
    corner = (in_row >= 52) & (in_row < 60)
    for d in range(span_x):
        for c in range(cap):
            other = span_x - 1 - d
            own = source[d * cap + c]
            left = source[(d - 1) % span_x * cap + c]
            right = source[(d + 1) % span_x * cap + c]
            fold = source[other * cap + c]
            fold_west = source[(other - 1) % span_x * cap + c]
            fold_east = source[(other + 1) % span_x * cap + c]

            def last(slot):
                return pieces[pl.ds(24 * STEP + slot, 8, stride=STEP), :]

            tail = jnp.where(tile_row < 2, last(own), jnp.where(tile_row < 4, last(right), last(left)))
            tail = jnp.where(tile_row >= 6, pltpu.roll(last(fold), 6, 0), tail)
            tail = jnp.where((tile_row == 3) & corner, pltpu.roll(last(fold_east), 8, 1), tail)
            tail = jnp.where((tile_row == 5) & corner, pltpu.roll(last(fold_west), 8, 1), tail)
            ready[d * cap + c, 0:24, :] = pieces[pl.ds(own, 24, stride=STEP), :]
            ready[d * cap + c, 24:32, :] = tail
            put(d * cap + c).start()
    for r in range(span_x * cap):
        put(r).wait()


def outgoing_blocks(span_x, cap, ids, pick, edges, rims, sums):
    slots = ids.shape[0]
    return pl.pallas_call(
        functools.partial(outgoing_body, span_x, cap, slots),
        out_shape=(
            jax.ShapeDtypeStruct((span_x * cap, 32, 128), F32),
            jax.ShapeDtypeStruct((ROWS, 128), jnp.int32),
            mark_shape(),
        ),
        in_specs=[sm()] + [vm()] * 7,
        out_specs=(hbm(), vm(), hbm()),
        scratch_shapes=[pltpu.VMEM((32 * STEP + 8, 128), F32)]
        + [pltpu.VMEM((SLOT_ROWS, 128), F32)] * 2
        + [pltpu.SMEM(((span_x + 1) * cap,), jnp.int32), pltpu.SMEM((span_x + 1,), jnp.int32)]
        + [pltpu.VMEM((span_x * cap, 32, 128), F32), pltpu.SemaphoreType.DMA((span_x * cap,))],
        compiler_params=pltpu.CompilerParams(vmem_limit_bytes=12 * MIB),
        name="outgoing_blocks",
    )(ids, pick, edges, *rims, *sums)


def turn(x):
    lane = lax.broadcasted_iota(jnp.int32, (8, 128), 1)
    halves = [
        jnp.take_along_axis(x[:, h * 128 : h * 128 + 128], 127 - lane, axis=1, mode="promise_in_bounds")
        for h in (1, 0)
    ]
    return pltpu.roll(jnp.concatenate(halves, axis=1), (RX - GX) % GX, 1)


def region_body(span_y, rows, got, after, region, out, folded, tiles, sides):
    tiles[...] = jnp.zeros(tiles.shape, F32)
    sides[...] = jnp.zeros(sides.shape, F32)
    for p in range(KX * KY):
        r = rows[p, 0]
        block = got[pl.ds(pl.multiple_of(jnp.maximum(r, 0) * 32, 32), 32), :]
        block = jnp.where(r >= 0, block, 0.0)
        tiles[pl.ds((p % KX) * 8 + p // KX, 32, stride=STEP), :] = block
    for p in range(2 * KY):
        r = rows[KX * KY + p, 0]
        block = got[pl.ds(pl.multiple_of(jnp.maximum(r, 0) * 32 + 24, 8), 8), :]
        block = jnp.where(r >= 0, block, 0.0)
        sides[pl.ds((p // KY) * 8 + p % KY, 8, stride=17), :] = block
    at_fold = KX * KY + 2 * KY
    for g in range(KX + 2):
        r = rows[at_fold + g, 0]
        block = got[pl.ds(pl.multiple_of(jnp.maximum(r, 0) * 32 + 24, 8), 8), :]
        block = jnp.where(r >= 0, block, 0.0)
        if g < KX:
            for t in range(2):
                tiles[(24 + t) * STEP + g * 8 + 6 : (24 + t) * STEP + g * 8 + 7, :] = block[6 + t : 7 + t]
        elif g == KX:
            sides[5 * 17 + 6 : 5 * 17 + 7, :] = pltpu.roll(block, 120, 1)[5:6]
        else:
            sides[3 * 17 + 14 : 3 * 17 + 15, :] = pltpu.roll(block, 120, 1)[3:4]
    lane = lax.broadcasted_iota(jnp.int32, (8, 128), 1)
    sub = lax.broadcasted_iota(jnp.int32, (8, 128), 0)

    def assembled(r):
        t, base = r // 2, (r % 2) * 64
        v = [tiles[t * STEP + 8 * g : t * STEP + 8 * g + 8, :] for g in range(KX)]
        a = pltpu.roll(v[0], (-1 - base) % 128, 1)
        b = pltpu.roll(v[1], (59 - base) % 128, 1)
        c = pltpu.roll(v[2], (119 - base) % 128, 1)
        to = base + 4 * (t % HALF)
        p = t // HALF
        w = sides[(4 + p) * 17 : (4 + p) * 17 + 8, :]
        e = sides[(2 + p) * 17 + 8 : (2 + p) * 17 + 16, :]
        w = pltpu.roll(w, (125 - to) % 128, 1)
        e = pltpu.roll(e, (51 - to) % 128, 1)
        left = jnp.where(lane <= 60, a, 0.0)
        left = left + jnp.where((lane >= 59) & (lane <= 120), b, 0.0)
        left = left + jnp.where(lane >= 119, c, 0.0)
        left = left + jnp.where(lane == 0, w, 0.0)
        right = jnp.where(lane <= 52, c, 0.0)
        right = right + jnp.where(lane == 127, a, 0.0)
        right = right + jnp.where(lane >= 125, w, 0.0)
        right = right + jnp.where((lane >= 51) & (lane <= 54), e, 0.0)
        return left, right

    region[...] = jnp.zeros(region.shape, F32)
    below = assembled(0)
    above = assembled(SPAN_N + 1)
    over = [above]
    for r in range(1, SPAN_N + 1):
        parts = assembled(r)
        if r > SPAN_N - 3:
            over.insert(1, parts)
        for h in range(2):
            v = parts[h]
            if r == 1:
                v = v + jnp.where((sub >= 1) & (sub < KY), pltpu.roll(above[h], 1, 0), 0.0)
            if r == SPAN_N:
                v = v + jnp.where(sub < KY - 1, pltpu.roll(below[h], 7, 0), 0.0)
            region[pl.ds(h * GY + r - 1, KY, stride=SPAN_N), :] = v[0:KY]
    for h in range(2):
        region[h * GY + RY : h * GY + RY + 1, :] = above[h][KY - 1 : KY]
        region[h * GY + GY - 1 : h * GY + GY, :] = below[h][0:1]

    def lines(ys):
        cut = [
            jnp.concatenate([region[y : y + 1, :], region[GY + y : GY + y + 1, :]], axis=1) for y in ys
        ]
        return jnp.concatenate(cut + [jnp.zeros((8 - len(ys), GX), F32)], axis=0)

    spread_lines(span_y, lines([RY - 3, RY - 2, RY - 1, RY]), lines([GY - 1, 0, 1, 2]), out)
    over = [jnp.concatenate([part[6:7] for part in parts], axis=1) for parts in over]
    folded[...] = turn(jnp.concatenate(over + [jnp.zeros((4, GX), F32)], axis=0))


def region_sums(span_y, rows, got, after):
    return pl.pallas_call(
        functools.partial(region_body, span_y),
        out_shape=(
            jax.ShapeDtypeStruct((2 * GY, 128), F32),
            jax.ShapeDtypeStruct((span_y, 8, GX), F32),
            jax.ShapeDtypeStruct((8, GX), F32),
        ),
        in_specs=[sm(), vm(), hbm()],
        out_specs=(vm(),) * 3,
        scratch_shapes=[pltpu.VMEM((32 * STEP + 8, 128), F32), pltpu.VMEM((8 * 17, 128), F32)],
        compiler_params=pltpu.CompilerParams(vmem_limit_bytes=12 * MIB),
        name="region_sums",
    )(rows, got.reshape(-1, 128), after)


def basis_body(span_x, span_y, region, lines, folded, extended, edges, basis, diag_out, dots, mark):
    ext = extended[...]
    here = lax.axis_index("gx")
    lane8 = lax.broadcasted_iota(jnp.int32, (8, GX), 1)
    row8 = lax.broadcasted_iota(jnp.int32, (8, GX), 0)
    put_west = jnp.where((row8 >= 4) & (lane8 == GX - 8 + row8), 1.0, 0.0).astype(jnp.bfloat16)
    put_east = jnp.where((row8 < 4) & (lane8 == RX + row8), 1.0, 0.0).astype(jnp.bfloat16)
    for other, put in ((here + span_x - 1, put_west), (here + 1, put_east)):
        cols = edges[pl.ds(pl.multiple_of(other % span_x * 32 + 24, 8), 8), :]
        ext = ext + lax.dot_general(
            cols[:, 0:GY].astype(jnp.bfloat16), put, (((0,), (0,)), ((), ())), preferred_element_type=F32
        )

    fold = []
    for step in (0, -1, 1):
        other = span_x - 1 - here + step + span_x
        part = edges[pl.ds(pl.multiple_of(lax.rem(other, span_x) * 32 + 8, 8), 8), 256:384]
        fold.append(jnp.concatenate([part[0:4], part[4:8]], axis=1))
    lane4 = lax.broadcasted_iota(jnp.int32, (4, GX), 1)
    beyond = jnp.where(lane4 < RX, fold[0], 0.0)
    beyond = jnp.where((lane4 >= RX) & (lane4 < RX + 4), pltpu.roll(fold[1], RX, 1), beyond)
    beyond = jnp.where(lane4 >= GX - 4, pltpu.roll(fold[2], GX - RX, 1), beyond)
    beyond = jnp.where(lax.axis_index("gy") == span_y - 1, beyond, 0.0)
    ext = ext + jnp.concatenate([jnp.zeros((RY, GX), F32), beyond, jnp.zeros((GY - RY - 4, GX), F32)], axis=0)

    def south_of(x):
        return pltpu.roll(x, 1, 0)

    def north_of(x):
        return pltpu.roll(x, GY - 1, 0)

    def west_of(x):
        return pltpu.roll(x, 1, 1)

    def east_of(x):
        return pltpu.roll(x, GX - 1, 1)

    to_east = jnp.minimum(ext, east_of(ext)) / LEVELS
    to_north = jnp.minimum(ext, north_of(ext)) / LEVELS
    to_west = west_of(to_east)
    to_south = south_of(to_north)
    diagonal = jnp.where(ext > 0, DAMPING, 1.0) + to_east + to_west + to_north + to_south
    inverse = 1.0 / diagonal
    ups, downs = beside_lines(span_y, lines, folded[...])
    partial = jnp.concatenate([region[0:GY, :], region[GY : 2 * GY, :]], axis=1)
    gap = lambda rows: jnp.zeros((rows, GX), F32)
    extra = jnp.concatenate(
        [downs[3:4], gap(RY - 2), ups[0:4], gap(GY - RY - 6), downs[0:3]], axis=0
    )
    zero = (partial + extra) * (HALINE / LEVELS) * inverse

    def smooth(x):
        return inverse * (
            to_east * east_of(x) + to_west * west_of(x) + to_north * north_of(x) + to_south * south_of(x)
        )

    vectors = [zero, smooth(zero)]
    vectors.append(2.0 * smooth(vectors[1]) - vectors[0])
    vectors.append(2.0 * smooth(vectors[2]) - vectors[1])
    lane = lax.broadcasted_iota(jnp.int32, (GY, GX), 1)
    row = lax.broadcasted_iota(jnp.int32, (GY, GX), 0)
    inside = (lane < RX) & (row < RY)
    diag_out[...] = diagonal
    clean = [jnp.where(inside, v, 0.0) for v in vectors]
    position = lax.broadcasted_iota(jnp.int32, (8, 128), 1)
    packed = jnp.zeros((8, 128), F32)
    number = 0
    for i in range(4):
        basis[i] = clean[i]
        scaled = clean[i] * diagonal
        for j in range(i, 4):
            prod = scaled * clean[j]
            part = jnp.sum(prod.reshape(GY // 8, 8, GX), axis=0)
            part = part[:, 0:128] + part[:, 128:256]
            packed = packed + jnp.where(position == number, jnp.sum(part, axis=1, keepdims=True), 0.0)
            number += 1
    for d in range(dots.shape[0]):
        dots[d] = packed


def krylov_basis(span_x, span_y, region, lines, folded, extended, edges):
    return pl.pallas_call(
        functools.partial(basis_body, span_x, span_y),
        out_shape=(
            jax.ShapeDtypeStruct((4, GY, GX), F32),
            jax.ShapeDtypeStruct((GY, GX), F32),
            jax.ShapeDtypeStruct((span_x * span_y, 8, 128), F32),
            mark_shape(),
        ),
        in_specs=[vm()] * 5,
        out_specs=(vm(),) * 3 + (hbm(),),
        compiler_params=pltpu.CompilerParams(vmem_limit_bytes=12 * MIB),
        name="krylov_basis",
    )(region, lines, folded, extended, edges)


def combine_body(dots, basis, diagonal, after, height, misfit):
    sums = jnp.sum(dots[...], axis=0, keepdims=True)
    lane = lax.broadcasted_iota(jnp.int32, (1, 128), 1)
    g = {}
    number = 0
    for i in range(4):
        for j in range(i, 4):
            v = jnp.sum(jnp.where(lane == number, sums, 0.0), axis=1, keepdims=True)
            g[i, j] = g[j, i] = v
            number += 1

    def inner(a, b):
        out = jnp.zeros((1, 1), F32)
        for i in range(4):
            for j in range(4):
                if a[i] is not None and b[j] is not None:
                    out = out + a[i] * b[j] * g[i, j]
        return out

    def add(a, b):
        return a if b is None else b if a is None else a + b

    def image(a):
        out = list(a)
        for k in range(3):
            if a[k] is None:
                continue
            if k == 0:
                out[1] = add(out[1], -a[0])
            else:
                out[k + 1] = add(out[k + 1], -0.5 * a[k])
                out[k - 1] = add(out[k - 1], -0.5 * a[k])
        return out

    one = jnp.ones((1, 1), F32)
    res = [one, None, None, None]
    way = list(res)
    high = [None] * 4
    gamma = inner(res, res)
    for iteration in range(3):
        moved = image(way)
        size = gamma / inner(way, moved)
        high = [h if w is None else add(h, size * w) for h, w in zip(high, way)]
        res = [r if m is None else add(r, -size * m) for r, m in zip(res, moved)]
        if iteration < 2:
            after = inner(res, res)
            ratio = after / gamma
            way = [r if w is None else add(r, ratio * w) for r, w in zip(res, way)]
            gamma = after
    out = jnp.zeros((GY, GX), F32)
    left = jnp.zeros((GY, GX), F32)
    for k in range(4):
        v = basis[k]
        if high[k] is not None:
            out = out + high[k] * v
        left = left + res[k] * v
    gap = jnp.zeros((384 - GY, GX), F32)
    height[...] = jnp.concatenate([out, gap], axis=0).T[0:RX, 0:RY]
    misfit[...] = jnp.concatenate([left * diagonal[...], gap], axis=0).T[0:RX, 0:RY]


def combine(dots, basis, diagonal, after):
    return pl.pallas_call(
        combine_body,
        out_shape=(jax.ShapeDtypeStruct((RX, RY), F32),) * 2,
        in_specs=[vm()] * 3 + [hbm()],
        out_specs=(vm(),) * 2,
        compiler_params=pltpu.CompilerParams(vmem_limit_bytes=12 * MIB),
        name="combine",
    )(dots, basis, diagonal, after)


def across(lines):
    return lax.all_to_all(lines, "gy", split_axis=0, concat_axis=0, tiled=True)


def on_device(warm, salt, inflow, mixing, tiles, slot_depth, depth):
    span_x = lax.axis_size("gx")
    span_y = lax.axis_size("gy")
    slots = tiles.shape[0]
    cap = (KX * KY + span_x - 1) // span_x
    both = ("gx", "gy")
    bounds = [slots * i // 18 for i in (0, 14, 18)]

    def solve(part, before, after):
        first, end = bounds[part], bounds[part + 1]
        return solve_columns(warm, salt, columns, first, end - first, before, (after,))

    region_depth, lines = region_ends(span_y, depth.T)
    n_rows, q_rows, coef, pick, n_x, n_y, held = column_tables(
        span_x, span_y, mixing, tiles, slot_depth, inflow, region_depth
    )
    columns = (n_rows, q_rows, coef)
    table, extended, mark = block_edges(span_x, span_y, region_depth, across(lines), held)
    edges = lax.all_to_all(table, "gx", split_axis=0, concat_axis=0, tiled=True)
    sums = face_sums(warm, salt, columns, mark)
    flat_edges = edges.reshape(-1, EDGE)
    blocks, rows, mark = outgoing_blocks(span_x, cap, tiles, pick, flat_edges, (n_x, n_y), sums)
    got = lax.all_to_all(blocks, "gx", split_axis=0, concat_axis=0, tiled=True)
    *solved, done = solve(0, (), mark)

    region, lines, folded = region_sums(span_y, rows, got, done)
    basis, diagonal, dots, mark = krylov_basis(
        span_x, span_y, region, across(lines), folded, extended, flat_edges
    )
    sums = lax.all_to_all(dots, both, split_axis=0, concat_axis=0, tiled=True)
    *solved, done = solve(1, solved, mark)
    height, misfit = combine(sums.reshape(-1, 128), basis, diagonal, done)
    return (solved[0], solved[1], height.T, misfit.T)


def solution(mesh):
    in_specs = (
        P(("gx", "gy"), None, None),
        P(("gx", "gy"), None, None),
        P(("gx", "gy"), None),
        P(),
        P(("gx", "gy")),
        P(("gx", "gy"), None),
        P("gy", "gx"),
    )
    out_specs = (
        P(("gx", "gy"), None, None),
        P(("gx", "gy"), None, None),
        P("gy", "gx"),
        P("gy", "gx"),
    )
    return jax.shard_map(on_device, mesh=mesh, in_specs=in_specs, out_specs=out_specs, check_vma=False)
```
